128 devices in a mesh: gx: 4 (over z_hi, core), gy: 4 (over x), gz: 8 (over y, z_lo).
Axes of the slice: x: 4, y: 4, z: 4 (z_hi: 2, z_lo: 2; z = z_hi * 2 + z_lo), core: 2. Of those that a mesh axis runs over, the one named last changes fastest.
Arguments:
- offsets: float32 [16, 16, 16, 3, 16], P('gx', 'gy', 'gz'), as said below
- species: int32 [16, 16, 16, 16], P('gx', 'gy', 'gz'), may hold values from 0 to 3
- neighbours: int32 [16, 16, 16, 16, 32], P('gx', 'gy', 'gz'), may hold values from 0 to 6143, as said below
- counts: int32 [16, 16, 16, 16], P('gx', 'gy', 'gz'), may hold values from 8 to 32, as said below
- embed: float32 [4, 128], replicated, may hold values from 0.25 to 1.75
- radial_a: float32 [8, 128], replicated, may hold values from -2 to 2
- mix_in: bfloat16 [384, 128], replicated, may hold values from -0.3125 to 0.3125
- proj_center: bfloat16 [128, 128], replicated, may hold values from -0.5 to 0.5
- proj_neigh: bfloat16 [128, 128], replicated, may hold values from -0.5 to 0.5
- radial_b: float32 [8, 128], replicated, may hold values from -2 to 2
- couple: float32 [3, 128], replicated, may hold values from -4 to 4
- latent_two: bfloat16 [128, 128], replicated, may hold values from -0.5 to 0.5
- latent_three: bfloat16 [128, 128], replicated, may hold values from -0.5 to 0.5
- readout: float32 [128], replicated, may hold values from -0.5 to 0.5
Outputs:
- forces: float32 [16, 16, 16, 3, 16], P('gx', 'gy', 'gz')
- atom_energy: float32 [16, 16, 16, 16], P('gx', 'gy', 'gz')
The draws below stay inside these ranges and needn't reach their ends.
Inputs may be any that keep to these rules, and one draw needn't show every extreme that they name: `neighbours`: entry s of an atom names an atom whose cell lies within two cells of the atom's own cell along each dimension, numbered in the atom's brick's block as in the reference program; it is never the atom itself and entries may repeat. Slots 0 to count - 1 of an atom are live; the level of the counts differs from brick to brick, and the first atom of each brick has all 32. `offsets`: each atom lies within 0.1 of its own site in its cell: x at 0.5 + (slot % 2), y at 0.5 + (slot // 2 % 2), z at (slot // 4 + 0.5) * 8 / 16.
All inputs are finite; a program needn't handle non-finite values.
Results may differ from the reference program's by a relative error of at most 0.014.
Values may be sent and summed in bfloat16 or wider, within the bound.
No kernel may reach another device: no remote copies, remote signals or barrier semaphores. Data moves between devices by JAX's collectives and lax.ppermute only.
A program may use at most 128 MiB of HBM per device.

```python
import math
import jax
import jax.numpy as jnp
from jax import lax

CX = 4
CY = 4
CZ = 2
PER_CELL = 16
SLOTS = 32
CH = 128
NBASIS = 8
SPECIES = 4
NX = 16
NY = 16
NZ = 16


def draw_offsets(key, part):
    key = jax.random.fold_in(key, 11)
    slot_ids = jnp.arange(PER_CELL, dtype=jnp.int32)
    layers_z = PER_CELL // 4
    site_x = (slot_ids % 2).astype(jnp.float32) + 0.5
    site_y = (slot_ids // 2 % 2).astype(jnp.float32) + 0.5
    site_z = ((slot_ids // 4).astype(jnp.float32) + 0.5) * (2.0 / layers_z)
    sites = jnp.stack([site_x, site_y, site_z], 0)
    shape_full = (NX, NY, NZ, 3, PER_CELL)
    jitter = jax.random.uniform(key, shape_full, jnp.float32, -0.1, 0.1)
    return sites + jitter


def draw_neighbours(key, part):
    key = jax.random.fold_in(key, 23)
    key_x, key_y, key_z, key_slot = jax.random.split(key, 4)
    shape_full = (NX, NY, NZ, PER_CELL, SLOTS)
    off_x = jax.random.randint(key_x, shape_full, -2, 3, dtype=jnp.int32)
    off_y = jax.random.randint(key_y, shape_full, -2, 3, dtype=jnp.int32)
    off_z = jax.random.randint(key_z, shape_full, -2, 3, dtype=jnp.int32)
    other_slot = jax.random.randint(key_slot, shape_full, 0, PER_CELL, dtype=jnp.int32)
    own_slot = jnp.arange(PER_CELL, dtype=jnp.int32)[None, None, None, :, None]
    slot_ids = jnp.arange(SLOTS, dtype=jnp.int32)[None, None, None, None, :]
    self_hit = (off_x == 0) & (off_y == 0) & (off_z == 0) & (other_slot == own_slot)
    other_slot = jnp.where(self_hit, (other_slot + 1) % PER_CELL, other_slot)
    cell_x = (jnp.arange(NX, dtype=jnp.int32) % CX)[:, None, None, None, None]
    cell_y = (jnp.arange(NY, dtype=jnp.int32) % CY)[None, :, None, None, None]
    cell_z = (jnp.arange(NZ, dtype=jnp.int32) % CZ)[None, None, :, None, None]
    ext_y = CY + 4
    ext_z = CZ + 4
    index = (((cell_x + 2 + off_x) * ext_y + cell_y + 2 + off_y) * ext_z + cell_z + 2 + off_z) * PER_CELL + other_slot
    lowest = (cell_x == 0) & (cell_y == 0) & (cell_z == 0) & (own_slot == 0) & (slot_ids == 0)
    highest = (cell_x == CX - 1) & (cell_y == CY - 1) & (cell_z == CZ - 1) & (own_slot == PER_CELL - 1) & (slot_ids == 0)
    index = jnp.where(lowest, 0, index)
    index = jnp.where(highest, (CX + 4) * (CY + 4) * (CZ + 4) * PER_CELL - 1, index)
    return index.astype(jnp.int32)


def draw_counts(key, part):
    key = jax.random.fold_in(key, 37)
    key_level, key_extra = jax.random.split(key, 2)
    level = jax.random.randint(key_level, (NX // CX, NY // CY, NZ // CZ), SLOTS // 4, 3 * SLOTS // 4 + 1, dtype=jnp.int32)
    level_full = jnp.repeat(jnp.repeat(jnp.repeat(level, CX, 0), CY, 1), CZ, 2)[:, :, :, None]
    extra = jax.random.randint(key_extra, (NX, NY, NZ, PER_CELL), 0, SLOTS // 4 + 1, dtype=jnp.int32)
    count_values = jnp.minimum(level_full + extra, SLOTS)
    cell_x = (jnp.arange(NX, dtype=jnp.int32) % CX)[:, None, None, None]
    cell_y = (jnp.arange(NY, dtype=jnp.int32) % CY)[None, :, None, None]
    cell_z = (jnp.arange(NZ, dtype=jnp.int32) % CZ)[None, None, :, None]
    own_slot = jnp.arange(PER_CELL, dtype=jnp.int32)[None, None, None, :]
    first_atom = (cell_x == 0) & (cell_y == 0) & (cell_z == 0) & (own_slot == 0)
    return jnp.where(first_atom, SLOTS, count_values).astype(jnp.int32)


def place_ends(array, own_key, smallest, largest):
    index_at = [jax.random.randint(jax.random.fold_in(own_key, axis), (), 0, length) for axis, length in enumerate(array.shape)]
    widest = array.shape.index(max(array.shape))
    beside = index_at[:widest] + [(index_at[widest] + 1) % array.shape[widest]] + index_at[widest + 1:]
    return array.at[tuple(index_at)].set(smallest).at[tuple(beside)].set(largest)


def scatter_about(stream_key, shape, scale, limit, kind=jnp.bfloat16):
    values = jax.random.normal(stream_key, shape, jnp.float32) * scale
    return jnp.minimum(jnp.maximum(values, -limit), limit).astype(kind)


def setup_inputs(seed: int = 0) -> dict:
    keys = jax.random.split(jax.random.key(seed), 15)
    return {
        "offsets": draw_offsets(jax.random.fold_in(keys[14], 71), 0),
        "species": place_ends(jax.random.randint(keys[1], (NX, NY, NZ, PER_CELL), 0, SPECIES), jax.random.fold_in(keys[1], 1), 0, SPECIES - 1).astype(jnp.int32),
        "neighbours": draw_neighbours(jax.random.fold_in(keys[14], 71), 0),
        "counts": draw_counts(jax.random.fold_in(keys[14], 71), 0),
        "embed": jnp.clip(1.0 + 0.15 * jax.random.normal(keys[4], (SPECIES, CH), jnp.float32), 0.25, 1.75),
        "radial_a": scatter_about(keys[5], (NBASIS, CH), NBASIS ** -0.5, 2.0, jnp.float32),
        "mix_in": scatter_about(keys[6], (3 * CH, CH), (3 * CH) ** -0.5, 0.3125),
        "proj_center": scatter_about(keys[7], (CH, CH), CH ** -0.5, 0.5),
        "proj_neigh": scatter_about(keys[8], (CH, CH), CH ** -0.5, 0.5),
        "radial_b": scatter_about(keys[9], (NBASIS, CH), NBASIS ** -0.5, 2.0, jnp.float32),
        "couple": scatter_about(keys[10], (3, CH), 1.0, 4.0, jnp.float32),
        "latent_two": scatter_about(keys[11], (CH, CH), CH ** -0.5, 0.5),
        "latent_three": scatter_about(keys[12], (CH, CH), CH ** -0.5, 0.5),
        "readout": scatter_about(keys[13], (CH,), CH ** -0.5, 0.5, jnp.float32),
    }


CELL_SIDE = 2.0
CUTOFF = 10.5
NORM_EPS = 1e-05

def harmonics(unit_x, unit_y, unit_z):
    root_three = math.sqrt(3.0)
    root_five = math.sqrt(5.0)
    root_fifteen = math.sqrt(15.0)
    return jnp.stack([jnp.ones_like(unit_x), root_three * unit_x, root_three * unit_y, root_three * unit_z, root_fifteen * unit_x * unit_y, root_fifteen * unit_y * unit_z, 0.5 * root_five * (3.0 * unit_z * unit_z - 1.0), root_fifteen * unit_x * unit_z, 0.5 * root_fifteen * (unit_x * unit_x - unit_y * unit_y)], 0)

def layer_geometry(flat_offsets, layer_nbr, layer_count, layer_index):
    ext_y = CY + 4
    ext_z = CZ + 4
    layer_rows = CY * CZ * PER_CELL
    atom_index = jnp.arange(layer_rows, dtype=jnp.int32)
    atom_slot = atom_index % PER_CELL
    cell_z = atom_index // PER_CELL % CZ
    cell_y = atom_index // (PER_CELL * CZ)
    self_ext = (((layer_index + 2) * ext_y + cell_y + 2) * ext_z + cell_z + 2) * PER_CELL + atom_slot
    own_place = flat_offsets[self_ext]
    other_place = flat_offsets[layer_nbr]
    other_cell = layer_nbr // PER_CELL
    shift_z = other_cell % ext_z - 2 - cell_z[:, None]
    shift_y = other_cell // ext_z % ext_y - 2 - cell_y[:, None]
    shift_x = other_cell // (ext_z * ext_y) - 2 - layer_index
    step_x = shift_x.astype(jnp.float32) * CELL_SIDE + other_place[:, :, 0] - own_place[:, None, 0]
    step_y = shift_y.astype(jnp.float32) * CELL_SIDE + other_place[:, :, 1] - own_place[:, None, 1]
    step_z = shift_z.astype(jnp.float32) * CELL_SIDE + other_place[:, :, 2] - own_place[:, None, 2]
    live_mask = (jnp.arange(SLOTS, dtype=jnp.int32)[None, :] < layer_count[:, None]).astype(jnp.float32)
    return (step_x, step_y, step_z, live_mask)

def pair_basis(step_x, step_y, step_z):
    distance = jnp.sqrt(step_x * step_x + step_y * step_y + step_z * step_z)
    harmonic_values = harmonics(step_x / distance, step_y / distance, step_z / distance)
    orders = jnp.arange(1, NBASIS + 1, dtype=jnp.int32).astype(jnp.float32)
    bessel = CELL_SIDE * jnp.sin(math.pi / CUTOFF * distance[:, :, None] * orders) / distance[:, :, None]
    scaled = distance / CUTOFF
    envelope = (1.0 - scaled * scaled) * (1.0 - scaled * scaled)
    return (harmonic_values, bessel, envelope)

def layer_environment(flat_offsets, layer_nbr, layer_count, layer_species, layer_index, embed, radial_a, mix_in):
    step_x, step_y, step_z, live_mask = layer_geometry(flat_offsets, layer_nbr, layer_count, layer_index)
    harmonic_values, bessel, envelope = pair_basis(step_x, step_y, step_z)
    radial = jnp.einsum('akn,nc->akc', bessel, radial_a, precision=lax.Precision.HIGHEST)
    weighted = (live_mask * envelope)[:, :, None] * radial
    species_hot = (layer_species[:, None] == jnp.arange(SPECIES, dtype=jnp.int32)[None, :]).astype(jnp.float32)
    scaling = jnp.dot(species_hot, embed, precision=lax.Precision.HIGHEST) / math.sqrt(SLOTS)
    environment = jnp.einsum('mak,akc->mac', harmonic_values, weighted, precision=lax.Precision.HIGHEST) * scaling[None]
    squares = environment * environment
    invariant = jnp.concatenate([squares[0], lax.optimization_barrier(jnp.sum(squares[1:4], 0)), lax.optimization_barrier(jnp.sum(squares[4:9], 0))], -1)
    normed = invariant * lax.rsqrt(lax.optimization_barrier(jnp.mean(invariant * invariant, -1, keepdims=True)) + NORM_EPS)
    hidden_full = jax.nn.silu(jnp.dot(normed.astype(jnp.bfloat16), mix_in, preferred_element_type=jnp.float32))
    return (hidden_full, environment)

def layer_energy(flat_offsets, layer_nbr, layer_count, layer_index, center_rows, neigh_rows, environment, couple, radial_b, latent_two, latent_three, readout):
    step_x, step_y, step_z, live_mask = layer_geometry(flat_offsets, layer_nbr, layer_count, layer_index)
    harmonic_values, bessel, envelope = pair_basis(step_x, step_y, step_z)
    gathered = neigh_rows[layer_nbr]
    couple_full = jnp.concatenate([couple[0:1], jnp.repeat(couple[1:2], 3, 0), jnp.repeat(couple[2:3], 5, 0)], 0)
    coupled = jnp.einsum('mak,mac->akc', harmonic_values, environment * couple_full[:, None, :], precision=lax.Precision.HIGHEST)
    radial = jnp.einsum('akn,nc->akc', bessel, radial_b, precision=lax.Precision.HIGHEST)
    hidden_one = jax.nn.silu(center_rows[:, None, :] + gathered + coupled + radial).astype(jnp.bfloat16)
    hidden_one = hidden_one.reshape(-1, CH)
    hidden_two = jax.nn.silu(jnp.dot(hidden_one, latent_two, preferred_element_type=jnp.float32)).astype(jnp.bfloat16)
    hidden_three = jax.nn.silu(jnp.dot(hidden_two, latent_three, preferred_element_type=jnp.float32))
    pair_out = jnp.dot(hidden_three, readout, precision=lax.Precision.HIGHEST).reshape(live_mask.shape)
    return lax.optimization_barrier(jnp.sum(live_mask * envelope * pair_out, -1))

def brick_environment(ext_offsets, nbr_layers, count_layers, species_layers, embed, radial_a, mix_in):
    flat_offsets = jnp.moveaxis(ext_offsets, 3, 4).reshape(-1, 3)

    def one_layer(layer_items):
        layer_index, layer_nbr, layer_count, layer_species = layer_items
        return layer_environment(flat_offsets, layer_nbr, layer_count, layer_species, layer_index, embed, radial_a, mix_in)
    return lax.map(jax.checkpoint(one_layer), (jnp.arange(CX, dtype=jnp.int32), nbr_layers, count_layers, species_layers))

def brick_energy(ext_offsets, center, neigh_rows, environment, nbr_layers, count_layers, couple, radial_b, latent_two, latent_three, readout):
    flat_offsets = jnp.moveaxis(ext_offsets, 3, 4).reshape(-1, 3)

    def one_layer(layer_items):
        layer_index, layer_nbr, layer_count, center_rows, layer_env = layer_items
        return layer_energy(flat_offsets, layer_nbr, layer_count, layer_index, center_rows, neigh_rows, layer_env, couple, radial_b, latent_two, latent_three, readout)
    return lax.map(jax.checkpoint(one_layer), (jnp.arange(CX, dtype=jnp.int32), nbr_layers, count_layers, center, environment))

def grid_slice(field, corner_x, corner_y, corner_z):
    part_x = lax.dynamic_slice_in_dim(field, corner_x, CX, 0)
    part_y = lax.dynamic_slice_in_dim(part_x, corner_y, CY, 1)
    return lax.dynamic_slice_in_dim(part_y, corner_z, CZ, 2)

def grid_block(field, corner_x, corner_y, corner_z):
    index_x = (corner_x - 2 + jnp.arange(CX + 4, dtype=jnp.int32)) % NX
    index_y = (corner_y - 2 + jnp.arange(CY + 4, dtype=jnp.int32)) % NY
    index_z = (corner_z - 2 + jnp.arange(CZ + 4, dtype=jnp.int32)) % NZ
    return jnp.take(jnp.take(jnp.take(field, index_x, axis=0), index_y, axis=1), index_z, axis=2)

def reference(offsets, species, neighbours, counts, embed, radial_a, mix_in, proj_center, proj_neigh, radial_b, couple, latent_two, latent_three, readout):
    bricks_x = NX // CX
    bricks_y = NY // CY
    bricks_z = NZ // CZ
    layer_rows = CY * CZ * PER_CELL
    brick_ids = jnp.arange(bricks_x * bricks_y * bricks_z, dtype=jnp.int32)

    def corners(brick):
        corner_x = brick // (bricks_y * bricks_z) * CX
        corner_y = brick // bricks_z % bricks_y * CY
        corner_z = brick % bricks_z * CZ
        return (corner_x, corner_y, corner_z)

    def brick_layers(field, brick):
        corner_x, corner_y, corner_z = corners(brick)
        part = grid_slice(field, corner_x, corner_y, corner_z)
        return part.reshape((CX, layer_rows) + field.shape[4:])

    def to_grid(values):
        tail_shape = values.shape[3:]
        shaped = values.reshape((bricks_x, bricks_y, bricks_z, CX, CY, CZ, PER_CELL) + tail_shape)
        axes_order = (0, 3, 1, 4, 2, 5) + tuple(range(6, 7 + len(tail_shape)))
        return jnp.transpose(shaped, axes_order).reshape((NX, NY, NZ, PER_CELL) + tail_shape)

    def to_bricks(values):
        tail_shape = values.shape[4:]
        shaped = values.reshape((bricks_x, CX, bricks_y, CY, bricks_z, CZ, PER_CELL) + tail_shape)
        axes_order = (0, 2, 4, 1, 3, 5) + tuple(range(6, 7 + len(tail_shape)))
        return jnp.transpose(shaped, axes_order).reshape((bricks_x * bricks_y * bricks_z, CX, layer_rows) + tail_shape)

    def environment_all(global_offsets):

        def per_brick(brick):
            corner_x, corner_y, corner_z = corners(brick)
            ext_offsets = grid_block(global_offsets, corner_x, corner_y, corner_z)
            return brick_environment(ext_offsets, brick_layers(neighbours, brick), brick_layers(counts, brick), brick_layers(species, brick), embed, radial_a, mix_in)
        return lax.map(per_brick, brick_ids)
    (hidden_full, environment), pull_env = jax.vjp(environment_all, offsets)
    hidden = hidden_full.astype(jnp.bfloat16)
    center = jnp.dot(hidden.reshape(-1, CH), proj_center, preferred_element_type=jnp.float32).reshape(hidden.shape)
    hidden_grid = to_grid(hidden)
    neigh_grid = jnp.dot(hidden_grid.reshape(-1, CH), proj_neigh, preferred_element_type=jnp.float32).reshape(hidden_grid.shape)

    def energy_all(global_offsets, center, neigh_grid, environment):

        def per_brick(brick_items):
            brick, brick_center, brick_env = brick_items
            corner_x, corner_y, corner_z = corners(brick)
            ext_offsets = grid_block(global_offsets, corner_x, corner_y, corner_z)
            neigh_rows = grid_block(neigh_grid, corner_x, corner_y, corner_z).reshape(-1, CH)
            return brick_energy(ext_offsets, brick_center, neigh_rows, brick_env, brick_layers(neighbours, brick), brick_layers(counts, brick), couple, radial_b, latent_two, latent_three, readout)
        return lax.map(per_brick, (brick_ids, center, environment))
    energy, pull_pairs = jax.vjp(energy_all, offsets, center, neigh_grid, environment)
    grad_offsets_b, grad_center, grad_neigh, grad_env = pull_pairs(jnp.ones_like(energy))
    from_center = jnp.dot(grad_center.reshape(-1, CH), proj_center.astype(jnp.float32).T, precision=lax.Precision.HIGHEST).reshape(hidden.shape)
    from_neigh = jnp.dot(grad_neigh.reshape(-1, CH), proj_neigh.astype(jnp.float32).T, precision=lax.Precision.HIGHEST).reshape(grad_neigh.shape)
    grad_hidden = from_center + to_bricks(from_neigh)
    grad_offsets_a, = pull_env((grad_hidden, grad_env))
    forces = -(grad_offsets_a + grad_offsets_b)
    return (forces, to_grid(energy))
```

```python
import math

import jax
import jax.numpy as jnp
from jax import lax
from jax.experimental import pallas as pl
from jax.experimental.pallas import tpu as pltpu
from jax.sharding import PartitionSpec as P

CX = 4
CY = 4
CZ = 2
PER_CELL = 16
SLOTS = 32
CH = 128
NBASIS = 8
SPECIES = 4

CELL_SIDE = 2.0
CUTOFF = 10.5
NORM_EPS = 1e-05

COLS = CX * CY
PAIRS = CZ * PER_CELL * SLOTS
CELL_PAIRS = PER_CELL * SLOTS
ATOMS = COLS * CZ * PER_CELL
RUN = 48
SLAB = 5 * RUN
CELL_ROWS = 40

F32 = jnp.float32
BF16 = jnp.bfloat16
DEGREE = (0, 1, 1, 1, 2, 2, 2, 2, 2)

F_Y = 0
F_W = 9
F_DW = 10
F_B = 11
F_DB = 19
F_INV = 27
F_COUNT = 28

G_B = 0
G_Y = 8
G_E = 17
G_COUNT = 24


def dims(a, b, ca, cb):
    return lax.dot_general(a, b, (((ca,), (cb,)), ((), ())), preferred_element_type=F32)


def halves(value):
    high = value.astype(BF16)
    return high, (value - high.astype(F32)).astype(BF16)


def dims_three(a, b, ca, cb):
    a_high, a_low = halves(a)
    b_high, b_low = halves(b)
    return dims(a_high, b_high, ca, cb) + (
        dims(a_high, b_low, ca, cb) + dims(a_low, b_high, ca, cb)
    )


def iota(shape, dim):
    return lax.broadcasted_iota(jnp.int32, shape, dim)


def one_hot(condition):
    return jnp.where(condition, 1.0, 0.0).astype(BF16)


def radial_blocks(radial):
    rows = []
    for m in range(9):
        before = [jnp.zeros((NBASIS, m * CH), F32)] if m else []
        after = [jnp.zeros((NBASIS, (8 - m) * CH), F32)] if m < 8 else []
        rows.append(jnp.concatenate(before + [radial] + after, 1))
    return jnp.concatenate(rows, 0)


def sigmoid_of(v):
    return 0.5 * jnp.tanh(0.5 * v) + 0.5


def feature_rows(ref, row, count, i):
    blocks = []
    for lane in range(PAIRS // 128):
        start = (lane * F_COUNT + row) * COLS + i
        blocks.append(ref[pl.ds(start, count, stride=COLS) if count > 1 else pl.ds(start, 1), :])
    return jnp.concatenate(blocks, 1)


def whole_feature(ref, row):
    blocks = []
    for lane in range(PAIRS // 128):
        start = (lane * F_COUNT + row) * COLS
        blocks.append(ref[start : start + COLS, :])
    return jnp.concatenate(blocks, 1)


def put_feature(ref, row, value):
    for lane in range(PAIRS // 128):
        start = (lane * F_COUNT + row) * COLS
        ref[start : start + COLS, :] = value[:, lane * 128 : (lane + 1) * 128]


def cell_window(ref, x, y):
    parts = []
    for dx in range(5):
        start = pl.multiple_of(((x + dx) * 8 + y) * 8, 8)
        parts.append(ref[pl.ds(start, CELL_ROWS), :])
    return jnp.concatenate(parts, 0)


def env_kernel(
    nbr_ref,
    ext_ref,
    own_ref,
    count_ref,
    species_ref,
    embed_ref,
    radial_ref,
    mix_ref,
    hidden_ref,
    env_ref,
    scale_ref,
    feat_ref,
    code_ref,
    near_ref,
    moment_ref,
):
    shape = (COLS, PAIRS)
    number = nbr_ref[...]
    slot = number & 15
    cell = number >> 4
    over = (cell * 43691) >> 18
    cell_z = cell - 6 * over
    cell_y = over & 7
    cell_x = over >> 3
    column = iota(shape, 0)
    lane = iota(shape, 1)
    dx = cell_x - (column >> 2)
    dy = cell_y - (column & 3)
    upper = (cell_z >= 3).astype(jnp.int32)
    code_ref[0] = (dx * 5 + dy) * RUN + (cell_z - 3 * upper) * PER_CELL + slot
    code_ref[1] = upper
    code_ref[2] = dx * CELL_ROWS + dy * 8 + cell_z
    code_ref[3] = slot

    row_cells = iota((5 * CELL_ROWS, PAIRS), 0)
    row_slots = iota((PER_CELL, PAIRS), 0)

    def fetch(i, carry):
        hot = one_hot(row_cells == code_ref[2, pl.ds(i, 1), :])
        high, low = halves(cell_window(ext_ref, i // CY, i % CY))
        places = dims(high, hot, 0, 0) + dims(low, hot, 0, 0)
        mask = row_slots == code_ref[3, pl.ds(i, 1), :]
        for c in range(3):
            part = places[c * PER_CELL : (c + 1) * PER_CELL]
            near_ref[c, pl.ds(i, 1), :] = jnp.sum(jnp.where(mask, part, 0.0), 0, keepdims=True)
        return carry

    lax.fori_loop(0, COLS, fetch, 0)

    spread = one_hot(iota((32, PAIRS), 0) == (iota((32, PAIRS), 1) >> 5))
    own_high, own_low = halves(own_ref[...])
    own = dims(own_high, spread, 1, 0) + dims(own_low, spread, 1, 0)
    count = dims(count_ref[...].astype(F32).astype(BF16), spread, 1, 0)
    live = ((lane & 31).astype(F32) < count).astype(F32)
    step_x = (dx - 2).astype(F32) * CELL_SIDE + near_ref[0] - own[0:COLS]
    step_y = (dy - 2).astype(F32) * CELL_SIDE + near_ref[1] - own[COLS : 2 * COLS]
    step_z = (
        (cell_z - 2 - (lane >> 9)).astype(F32) * CELL_SIDE + near_ref[2] - own[2 * COLS : 3 * COLS]
    )
    square = step_x * step_x + step_y * step_y + step_z * step_z
    distance = jnp.sqrt(square)
    inverse = 1.0 / distance
    nx, ny, nz = step_x * inverse, step_y * inverse, step_z * inverse

    def put(row, value):
        put_feature(feat_ref, row, value)

    three, five, fifteen = math.sqrt(3.0), math.sqrt(5.0), math.sqrt(15.0)
    put(F_Y, jnp.ones(shape, F32))
    put(F_Y + 1, three * nx)
    put(F_Y + 2, three * ny)
    put(F_Y + 3, three * nz)
    put(F_Y + 4, fifteen * nx * ny)
    put(F_Y + 5, fifteen * ny * nz)
    put(F_Y + 6, (0.5 * five) * (3.0 * nz * nz - 1.0))
    put(F_Y + 7, fifteen * nx * nz)
    put(F_Y + 8, (0.5 * fifteen) * (nx * nx - ny * ny))
    scaled = distance * (1.0 / CUTOFF)
    inside = 1.0 - scaled * scaled
    put(F_W, live * inside * inside)
    put(F_DW, live * (-4.0 / CUTOFF) * scaled * inside)
    put(F_INV, inverse)
    angle = distance * (math.pi / CUTOFF)
    sine, cosine = jnp.sin(angle), jnp.cos(angle)
    last_s, last_c = jnp.zeros(shape, F32), jnp.ones(shape, F32)
    now_s, now_c = sine, cosine
    for k in range(1, NBASIS + 1):
        basis = CELL_SIDE * now_s * inverse
        put(F_B + k - 1, basis)
        put(F_DB + k - 1, (CELL_SIDE * k * math.pi / CUTOFF * now_c - basis) * inverse)
        last_s, now_s = now_s, 2.0 * cosine * now_s - last_s
        last_c, now_c = now_c, 2.0 * cosine * now_c - last_c

    atoms = one_hot(iota((PER_CELL, CELL_PAIRS), 0) == (iota((PER_CELL, CELL_PAIRS), 1) >> 5))

    def moments(i, carry):
        harmonic = feature_rows(feat_ref, F_Y, 9, i)
        weighted = feature_rows(feat_ref, F_B, NBASIS, i) * feature_rows(feat_ref, F_W, 1, i)
        products = jnp.concatenate([harmonic[m : m + 1] * weighted for m in range(9)], 0)
        high, low = halves(products)
        for z in range(CZ):
            part = slice(z * CELL_PAIRS, (z + 1) * CELL_PAIRS)
            start = pl.multiple_of((i * CZ + z) * PER_CELL, PER_CELL)
            moment_ref[pl.ds(start, PER_CELL), :] = dims(atoms, high[:, part], 1, 1) + dims(
                atoms, low[:, part], 1, 1
            )
        return carry

    lax.fori_loop(0, COLS, moments, 0)

    kind = one_hot(iota((SPECIES, ATOMS), 0) == species_ref[...])
    embed_high, embed_low = halves(embed_ref[...] * (1.0 / math.sqrt(SLOTS)))
    scale = dims(kind, embed_high, 0, 0) + dims(kind, embed_low, 0, 0)
    scale_ref[...] = scale
    sums = dims_three(moment_ref[...], radial_blocks(radial_ref[...]), 1, 0)
    invariants = [None] * 3
    for m in range(9):
        value = sums[:, m * CH : (m + 1) * CH] * scale
        env_ref[m] = value
        degree = DEGREE[m]
        squared = value * value
        invariants[degree] = (
            squared if invariants[degree] is None else invariants[degree] + squared
        )
    normed, _ = normalised(invariants)
    mixed = dims(jnp.concatenate(normed, 1).astype(BF16), mix_ref[...], 1, 0)
    hidden_ref[...] = (mixed * sigmoid_of(mixed)).astype(BF16)


def normalised(invariants):
    total = sum(jnp.sum(q * q, 1, keepdims=True) for q in invariants)
    inverse = lax.rsqrt(total * (1.0 / (3 * CH)) + NORM_EPS)
    return [q * inverse for q in invariants], inverse


def pair_kernel(
    around_ref,
    hidden_ref,
    env_ref,
    feat_ref,
    code_ref,
    center_ref,
    neigh_ref,
    radial_ref,
    couple_ref,
    two_ref,
    three_ref,
    readout_ref,
    energy_ref,
    ghost_ref,
    grad_center_ref,
    grad_env_ref,
    grad_ref,
    table_ref,
    total_ref,
    hot_ref,
    own_ref,
    pair_ref,
):
    for h in range(2):
        rows = around_ref[:, h].reshape(64 * RUN, CH)
        table_ref[:, h * CH : (h + 1) * CH] = dims(rows, neigh_ref[...], 1, 0).astype(BF16)
    total_ref[...] = jnp.zeros_like(total_ref)
    own_ref[...] = dims(hidden_ref[...], center_ref[...], 1, 0)
    readout = jnp.transpose(jnp.broadcast_to(readout_ref[...], (CH, CH)))
    readout = jnp.concatenate([readout] * (PAIRS // CH), 1)
    radial_high, radial_low = halves(radial_ref[...])
    atom_mask = iota((PER_CELL, CELL_PAIRS), 0) == (iota((PER_CELL, CELL_PAIRS), 1) >> 5)
    atoms = one_hot(atom_mask)
    row_slab = iota((SLAB, PAIRS), 0)

    def column(i, carry):
        x, y = i // CY, i % CY
        harmonic = feature_rows(feat_ref, F_Y, 9, i)
        basis_high, basis_low = halves(feature_rows(feat_ref, F_B, NBASIS, i))
        weight = feature_rows(feat_ref, F_W, 1, i)
        code = code_ref[0, pl.ds(i, 1), :]
        upper = code_ref[1, pl.ds(i, 1), :] > 0

        features, tables, parts = [], [], []
        for z in range(CZ):
            part = slice(z * CELL_PAIRS, (z + 1) * CELL_PAIRS)
            start = pl.multiple_of((i * CZ + z) * PER_CELL, PER_CELL)
            blocks = [
                jnp.where(atom_mask, harmonic[m : m + 1, part], 0.0).astype(BF16) for m in range(9)
            ]
            feature = jnp.concatenate(
                blocks
                + [
                    atoms,
                    atoms,
                    basis_high[:, part],
                    basis_low[:, part],
                    basis_high[:, part],
                    jnp.zeros((8, CELL_PAIRS), BF16),
                ],
                0,
            )
            scaled = [
                (env_ref[m, pl.ds(start, PER_CELL), :] * couple_ref[DEGREE[m] : DEGREE[m] + 1]).astype(
                    BF16
                )
                for m in range(9)
            ]
            own_high, own_low = halves(own_ref[pl.ds(start, PER_CELL), :])
            table = jnp.concatenate(
                scaled
                + [
                    own_high,
                    own_low,
                    radial_high,
                    radial_high,
                    radial_low,
                    jnp.zeros((8, CH), BF16),
                ],
                0,
            )
            features.append(feature)
            tables.append(table)
            parts.append(dims(table, feature, 0, 0))
        fetched = None
        for dx in range(5):
            hot = one_hot(row_slab == code - dx * SLAB)
            hot_ref[dx * SLAB : (dx + 1) * SLAB, :] = hot
            rows = pl.multiple_of(((x + dx) * 8 + y) * RUN, RUN)
            found = dims(table_ref[pl.ds(rows, SLAB), :], hot, 0, 0)
            fetched = found if fetched is None else fetched + found
        value = jnp.concatenate(parts, 1) + jnp.where(upper, fetched[CH:], fetched[:CH])
        gate = sigmoid_of(value)
        one = value * gate
        slope_one = gate + one - one * gate
        value = dims(two_ref[...], one.astype(BF16), 0, 0)
        gate = sigmoid_of(value)
        two = value * gate
        slope_two = gate + two - two * gate
        value = dims(three_ref[...], two.astype(BF16), 0, 0)
        gate = sigmoid_of(value)
        top = value * gate
        slope_top = gate + top - top * gate
        pair_energy = jnp.sum(top * readout, 0, keepdims=True)
        pair_ref[pl.ds(i, 1), :] = pair_energy * weight
        grad = slope_top * readout * weight
        grad = dims(three_ref[...], grad.astype(BF16), 1, 0) * slope_two
        grad = dims(two_ref[...], grad.astype(BF16), 1, 0) * slope_one
        spread = jnp.concatenate(
            [jnp.where(upper, 0.0, grad), jnp.where(upper, grad, 0.0)], 0
        ).astype(BF16)
        grad = grad.astype(BF16)
        for dx in range(5):
            rows = pl.multiple_of(((x + dx) * 8 + y) * RUN, RUN)
            total_ref[pl.ds(rows, SLAB), :] += dims(
                hot_ref[dx * SLAB : (dx + 1) * SLAB, :], spread, 1, 1
            )
        for z in range(CZ):
            part = slice(z * CELL_PAIRS, (z + 1) * CELL_PAIRS)
            start = pl.multiple_of((i * CZ + z) * PER_CELL, PER_CELL)
            back = dims(features[z][: 10 * PER_CELL], grad[:, part], 1, 1)
            for m in range(9):
                grad_env_ref[m, pl.ds(start, PER_CELL), :] = back[
                    m * PER_CELL : (m + 1) * PER_CELL
                ]
            grad_center_ref[pl.ds(start, PER_CELL), :] = back[9 * PER_CELL :]
            down = dims(tables[z], grad[:, part], 1, 0)
            for m in range(9):
                kept = jnp.where(atom_mask, down[m * PER_CELL : (m + 1) * PER_CELL], 0.0)
                grad_ref[i, G_Y + m : G_Y + m + 1, part] = jnp.sum(kept, 0, keepdims=True)
            base = 11 * PER_CELL
            grad_ref[i, G_B : G_B + NBASIS, part] = (
                down[base : base + NBASIS] + down[base + 2 * NBASIS : base + 3 * NBASIS]
            )
        grad_ref[i, G_E : G_E + 1, :] = pair_energy
        return carry

    lax.fori_loop(0, COLS, column, 0)
    for h in range(2):
        ghost_ref[:, h] = total_ref[:, h * CH : (h + 1) * CH].astype(BF16).reshape(64, RUN, CH)
    gather = one_hot(iota((32, PAIRS), 0) == (iota((32, PAIRS), 1) >> 5))
    high, low = halves(pair_ref[...])
    energy_ref[...] = dims(high, gather, 1, 1) + dims(low, gather, 1, 1)


def force_kernel(
    neigh_ref,
    grad_center_ref,
    grad_env_ref,
    env_ref,
    scale_ref,
    feat_ref,
    code_ref,
    grad_ref,
    mix_ref,
    center_ref,
    proj_ref,
    radial_ref,
    couple_ref,
    own_ref,
    ghost_ref,
    moment_ref,
    chain_ref,
    pull_ref,
):
    invariants = [None] * 3
    for m in range(9):
        value = env_ref[m]
        squared = value * value
        degree = DEGREE[m]
        invariants[degree] = (
            squared if invariants[degree] is None else invariants[degree] + squared
        )
    normed, inverse = normalised(invariants)
    mixed = dims(jnp.concatenate(normed, 1).astype(BF16), mix_ref[...], 1, 0)
    gate = sigmoid_of(mixed)
    act = mixed * gate
    high, low = halves(grad_center_ref[...])
    grad = dims(high, center_ref[...], 1, 1) + dims(low, center_ref[...], 1, 1)
    high, low = halves(neigh_ref[...])
    grad = grad + dims(high, proj_ref[...], 1, 1) + dims(low, proj_ref[...], 1, 1)
    grad = grad * (gate + act - act * gate)
    grad = dims(grad.astype(BF16), mix_ref[...], 1, 1)
    grads = [grad[:, d * CH : (d + 1) * CH] for d in range(3)]
    mean = sum(jnp.sum(g * q, 1, keepdims=True) for g, q in zip(grads, normed)) * (1.0 / (3 * CH))
    grads = [2.0 * inverse * (g - q * mean) for g, q in zip(grads, normed)]
    scale = scale_ref[...]
    pulled = []
    for m in range(9):
        d = DEGREE[m]
        pulled.append(
            (grad_env_ref[m] * couple_ref[d : d + 1] + env_ref[m] * grads[d]) * scale
        )
    moment_ref[...] = dims_three(
        jnp.concatenate(pulled, 1), radial_blocks(radial_ref[...]), 1, 1
    )

    atoms = one_hot(iota((PER_CELL, CELL_PAIRS), 0) == (iota((PER_CELL, CELL_PAIRS), 1) >> 5))

    def column(i, carry):
        harmonic = feature_rows(feat_ref, F_Y, 9, i)
        basis = feature_rows(feat_ref, F_B, NBASIS, i)
        slope = feature_rows(feat_ref, F_DB, NBASIS, i)
        weight = feature_rows(feat_ref, F_W, 1, i)
        weight_slope = feature_rows(feat_ref, F_DW, 1, i)
        parts = []
        for z in range(CZ):
            start = pl.multiple_of((i * CZ + z) * PER_CELL, PER_CELL)
            high, low = halves(moment_ref[pl.ds(start, PER_CELL), :])
            parts.append(dims(high, atoms, 0, 0) + dims(low, atoms, 0, 0))
        back = jnp.concatenate(parts, 1)
        weighted = basis * weight
        grad_weighted = jnp.zeros((NBASIS, PAIRS), F32)
        for m in range(9):
            block = back[m * NBASIS : (m + 1) * NBASIS]
            grad_weighted += block * harmonic[m : m + 1]
            chain_ref[i, m : m + 1, :] = grad_ref[i, G_Y + m : G_Y + m + 1, :] + jnp.sum(
                block * weighted, 0, keepdims=True
            )
        grad_basis = grad_ref[i, G_B : G_B + NBASIS, :] + grad_weighted * weight
        grad_weight = grad_ref[i, G_E : G_E + 1, :] + jnp.sum(
            grad_weighted * basis, 0, keepdims=True
        )
        chain_ref[i, 9:10, :] = (
            jnp.sum(grad_basis * slope, 0, keepdims=True) + grad_weight * weight_slope
        )
        return carry

    lax.fori_loop(0, COLS, column, 0)

    def chain(row):
        return chain_ref[:, row, :]

    def feature(row):
        return whole_feature(feat_ref, row)

    three, five, fifteen = math.sqrt(3.0), math.sqrt(5.0), math.sqrt(15.0)
    nx, ny, nz = (feature(F_Y + 1 + c) * (1.0 / three) for c in range(3))
    grad_x = three * chain(1) + fifteen * (ny * chain(4) + nz * chain(7) + nx * chain(8))
    grad_y = three * chain(2) + fifteen * (nx * chain(4) + nz * chain(5) - ny * chain(8))
    grad_z = (
        three * chain(3) + fifteen * (ny * chain(5) + nx * chain(7)) + (3.0 * five) * nz * chain(6)
    )
    inverse = feature(F_INV)
    along = chain(9) - inverse * (nx * grad_x + ny * grad_y + nz * grad_z)
    pull_ref[0] = grad_x * inverse + nx * along
    pull_ref[1] = grad_y * inverse + ny * along
    pull_ref[2] = grad_z * inverse + nz * along

    gather = one_hot(iota((32, PAIRS), 0) == (iota((32, PAIRS), 1) >> 5))
    for c in range(3):
        high, low = halves(pull_ref[c])
        own_ref[c] = dims(high, gather, 1, 1) + dims(low, gather, 1, 1)

    row_cells = iota((5 * CELL_ROWS, PAIRS), 0)
    row_slots = iota((PER_CELL, PAIRS), 0)
    ghost_ref[...] = jnp.zeros_like(ghost_ref)

    def scatter(i, carry):
        x, y = i // CY, i % CY
        hot = one_hot(row_cells == code_ref[2, pl.ds(i, 1), :])
        mask = row_slots == code_ref[3, pl.ds(i, 1), :]
        kept = jnp.concatenate(
            [jnp.where(mask, pull_ref[c, pl.ds(i, 1), :], 0.0) for c in range(3)], 0
        )
        high, low = halves(kept)
        found = dims(hot, high, 1, 1) + dims(hot, low, 1, 1)
        for dx in range(5):
            start = pl.multiple_of(((x + dx) * 8 + y) * 8, 8)
            ghost_ref[pl.ds(start, CELL_ROWS), :] += found[dx * CELL_ROWS : (dx + 1) * CELL_ROWS]
        return carry

    lax.fori_loop(0, COLS, scatter, 0)


def call(kernel, outs, scratch, *args):
    return pl.pallas_call(
        kernel,
        out_shape=[jax.ShapeDtypeStruct(shape, dtype) for shape, dtype in outs],
        scratch_shapes=[pltpu.VMEM(shape, dtype) for shape, dtype in scratch],
        compiler_params=pltpu.CompilerParams(vmem_limit_bytes=56 * 2**20),
    )(*args)


def shifted(block, axis, distance):
    size = lax.axis_size(axis)
    return lax.ppermute(block, axis, [(i, (i + distance) % size) for i in range(size)])


def padded(array, axis, dim, tail=0):
    length = array.shape[dim]
    before = shifted(lax.slice_in_dim(array, length - 2, length, axis=dim), axis, 1)
    after = shifted(lax.slice_in_dim(array, 0, 2, axis=dim), axis, -1)
    parts = [before, array, after]
    if tail:
        parts.append(jnp.zeros(after.shape[:dim] + (tail,) + after.shape[dim + 1 :], array.dtype))
    return jnp.concatenate(parts, axis=dim)


def folded(array, axis, dim, length):
    lower = lax.slice_in_dim(array, 0, 2, axis=dim).astype(BF16)
    upper = lax.slice_in_dim(array, length + 2, length + 4, axis=dim).astype(BF16)
    core = lax.slice_in_dim(array, 2, length + 2, axis=dim).astype(F32)
    to_first = shifted(upper, axis, 1).astype(F32)
    to_last = shifted(lower, axis, -1).astype(F32)
    if length == 2:
        return core + to_first + to_last
    first = lax.slice_in_dim(core, 0, 2, axis=dim) + to_first
    last = lax.slice_in_dim(core, 2, 4, axis=dim) + to_last
    return jnp.concatenate([first, last], axis=dim)


def shards(
    offsets,
    species,
    neighbours,
    counts,
    embed,
    radial_a,
    mix_in,
    proj_center,
    proj_neigh,
    radial_b,
    couple,
    latent_two,
    latent_three,
    readout,
):
    numbers = neighbours.reshape(COLS, PAIRS)
    places = offsets.reshape(CX, CY, CZ, 48)
    around = padded(padded(padded(places, "gx", 0), "gy", 1), "gz", 2, tail=2)
    own = offsets.reshape(COLS, CZ, 3, PER_CELL).transpose(2, 0, 1, 3).reshape(3 * COLS, 32)
    hidden, env, scale, feats, codes = call(
        env_kernel,
        [
            ((ATOMS, CH), BF16),
            ((9, ATOMS, CH), F32),
            ((ATOMS, CH), F32),
            ((PAIRS // 128 * F_COUNT * COLS, 128), F32),
            ((4, COLS, PAIRS), jnp.int32),
        ],
        [((3, COLS, PAIRS), F32), ((ATOMS, 72), F32)],
        numbers,
        around.reshape(512, 48),
        own,
        counts.reshape(COLS, 32),
        species.reshape(1, ATOMS),
        embed,
        radial_a,
        mix_in,
    )
    grid = hidden.reshape(CX, CY, CZ, PER_CELL, CH)
    wide = padded(padded(padded(grid, "gx", 0), "gy", 1), "gz", 2)
    energy, ghost, grad_center, grad_env, grads = call(
        pair_kernel,
        [
            ((COLS, 32), F32),
            ((64, 2, RUN, CH), BF16),
            ((ATOMS, CH), F32),
            ((9, ATOMS, CH), F32),
            ((COLS, G_COUNT, PAIRS), F32),
        ],
        [
            ((64 * RUN, 2 * CH), BF16),
            ((64 * RUN, 2 * CH), F32),
            ((5 * SLAB, PAIRS), BF16),
            ((ATOMS, CH), F32),
            ((COLS, PAIRS), F32),
        ],
        wide.reshape(64, 2, RUN, CH),
        hidden,
        env,
        feats,
        codes,
        proj_center,
        proj_neigh,
        radial_b,
        couple,
        latent_two,
        latent_three,
        readout.reshape(1, CH),
    )
    ghost = ghost.reshape(CX + 4, CY + 4, CZ + 4, PER_CELL, CH)
    owned = folded(folded(folded(ghost, "gx", 0, CX), "gy", 1, CY), "gz", 2, CZ)
    own_pull, far_pull = call(
        force_kernel,
        [((3, COLS, 32), F32), ((512, 48), F32)],
        [((ATOMS, 72), F32), ((COLS, 16, PAIRS), F32), ((3, COLS, PAIRS), F32)],
        owned.reshape(ATOMS, CH),
        grad_center,
        grad_env,
        env,
        scale,
        feats,
        codes,
        grads,
        mix_in,
        proj_center,
        proj_neigh,
        radial_a,
        couple,
    )
    far = far_pull.reshape(CX + 4, CY + 4, 8, 48)
    far = folded(folded(folded(far, "gx", 0, CX), "gy", 1, CY), "gz", 2, CZ)
    near = own_pull.reshape(3, CX, CY, CZ, PER_CELL).transpose(1, 2, 3, 0, 4)
    forces = near - far.reshape(CX, CY, CZ, 3, PER_CELL)
    return (forces, energy.reshape(CX, CY, CZ, PER_CELL))


def solution(mesh):
    placed = (
        P("gx", "gy", "gz", None, None),
        P("gx", "gy", "gz", None),
        P("gx", "gy", "gz", None, None),
        P("gx", "gy", "gz", None),
    ) + (P(),) * 10
    return jax.shard_map(
        shards,
        mesh=mesh,
        in_specs=placed,
        out_specs=(P("gx", "gy", "gz", None, None), P("gx", "gy", "gz", None)),
        check_vma=False,
    )
```

```python
import math

import jax
import jax.numpy as jnp
from jax import lax
from jax.experimental import pallas as pl
from jax.experimental.pallas import tpu as pltpu
from jax.sharding import PartitionSpec as P

CX = 4
CY = 4
CZ = 2
PER_CELL = 16
SLOTS = 32
CH = 128
NBASIS = 8
SPECIES = 4

CELL_SIDE = 2.0
CUTOFF = 10.5
NORM_EPS = 1e-05

COLS = CX * CY
PAIRS = CZ * PER_CELL * SLOTS
CELL_PAIRS = PER_CELL * SLOTS
ATOMS = COLS * CZ * PER_CELL
RUN = 48
SLAB = 5 * RUN
CELL_ROWS = 40
OWN_RUNS = CY * (CX + 4)
RIM_RUNS = 2 * (CX + 4)
LANES = PAIRS // 128

F32 = jnp.float32
BF16 = jnp.bfloat16
DEGREE = (0, 1, 1, 1, 2, 2, 2, 2, 2)

F_Y = 0
F_W = 9
F_DW = 10
F_B = 11
F_DB = 19
F_INV = 27
F_COUNT = 28

G_B = 0
G_Y = 8
G_E = 17
G_COUNT = 24


def dims(a, b, ca, cb):
    return lax.dot_general(a, b, (((ca,), (cb,)), ((), ())), preferred_element_type=F32)


def halves(value):
    high = value.astype(BF16)
    return high, (value - high.astype(F32)).astype(BF16)


def dims_three(a, b, ca, cb):
    a_high, a_low = halves(a)
    b_high, b_low = halves(b)
    return dims(a_high, b_high, ca, cb) + (
        dims(a_high, b_low, ca, cb) + dims(a_low, b_high, ca, cb)
    )


def iota(shape, dim):
    return lax.broadcasted_iota(jnp.int32, shape, dim)


def one_hot(condition):
    return jnp.where(condition, 1.0, 0.0).astype(BF16)


def radial_blocks(radial):
    rows = []
    for m in range(9):
        before = [jnp.zeros((NBASIS, m * CH), F32)] if m else []
        after = [jnp.zeros((NBASIS, (8 - m) * CH), F32)] if m < 8 else []
        rows.append(jnp.concatenate(before + [radial] + after, 1))
    return jnp.concatenate(rows, 0)


def looped(count, body, unroll):
    def step(j, carry):
        for k in range(unroll):
            body(j * unroll + k)
        return carry

    lax.fori_loop(0, count // unroll, step, 0)


def sigmoid_of(v):
    return 0.5 * jnp.tanh(0.5 * v) + 0.5


def feature_rows(ref, row, count, i):
    blocks = []
    for lane in range(LANES):
        start = (lane * F_COUNT + row) * COLS + i
        blocks.append(ref[pl.ds(start, count, stride=COLS) if count > 1 else pl.ds(start, 1), :])
    return jnp.concatenate(blocks, 1)


def whole_feature(ref, row):
    blocks = []
    for lane in range(LANES):
        start = (lane * F_COUNT + row) * COLS
        blocks.append(ref[start : start + COLS, :])
    return jnp.concatenate(blocks, 1)


def put_feature(ref, row, value):
    for lane in range(LANES):
        start = (lane * F_COUNT + row) * COLS
        ref[start : start + COLS, :] = value[:, lane * 128 : (lane + 1) * 128]


def cell_window(ref, x, y):
    parts = []
    for dx in range(5):
        start = pl.multiple_of(((x + dx) * 8 + y) * 8, 8)
        parts.append(ref[pl.ds(start, CELL_ROWS), :])
    return jnp.concatenate(parts, 0)


def env_kernel(
    nbr_ref,
    ext_ref,
    own_ref,
    count_ref,
    species_ref,
    embed_ref,
    radial_ref,
    mix_ref,
    hidden_ref,
    env_ref,
    scale_ref,
    feat_ref,
    code_ref,
    near_ref,
    moment_ref,
):
    shape = (COLS, PAIRS)
    number = nbr_ref[...]
    slot = number & 15
    cell = number >> 4
    over = (cell * 43691) >> 18
    cell_z = cell - 6 * over
    cell_y = over & 7
    cell_x = over >> 3
    column = iota(shape, 0)
    lane = iota(shape, 1)
    dx = cell_x - (column >> 2)
    dy = cell_y - (column & 3)
    upper = (cell_z >= 3).astype(jnp.int32)
    code_ref[0] = (dy * 5 + dx) * RUN + (cell_z - 3 * upper) * PER_CELL + slot
    code_ref[1] = upper
    code_ref[2] = dx * CELL_ROWS + dy * 8 + cell_z
    code_ref[3] = slot

    row_cells = iota((5 * CELL_ROWS, PAIRS), 0)
    row_slots = iota((PER_CELL, PAIRS), 0)

    def fetch(i):
        hot = one_hot(row_cells == code_ref[2, pl.ds(i, 1), :])
        high, low = halves(cell_window(ext_ref, i // CY, i % CY))
        places = dims(high, hot, 0, 0) + dims(low, hot, 0, 0)
        mask = row_slots == code_ref[3, pl.ds(i, 1), :]
        for c in range(3):
            part = places[c * PER_CELL : (c + 1) * PER_CELL]
            near_ref[c, pl.ds(i, 1), :] = jnp.sum(jnp.where(mask, part, 0.0), 0, keepdims=True)

    looped(COLS, fetch, 2)

    spread = one_hot(iota((32, PAIRS), 0) == (iota((32, PAIRS), 1) >> 5))
    own_high, own_low = halves(own_ref[...])
    own = dims(own_high, spread, 1, 0) + dims(own_low, spread, 1, 0)
    count = dims(count_ref[...].astype(F32).astype(BF16), spread, 1, 0)
    live = ((lane & 31).astype(F32) < count).astype(F32)
    step_x = (dx - 2).astype(F32) * CELL_SIDE + near_ref[0] - own[0:COLS]
    step_y = (dy - 2).astype(F32) * CELL_SIDE + near_ref[1] - own[COLS : 2 * COLS]
    step_z = (
        (cell_z - 2 - (lane >> 9)).astype(F32) * CELL_SIDE + near_ref[2] - own[2 * COLS : 3 * COLS]
    )
    square = step_x * step_x + step_y * step_y + step_z * step_z
    distance = jnp.sqrt(square)
    inverse = 1.0 / distance
    nx, ny, nz = step_x * inverse, step_y * inverse, step_z * inverse

    def put(row, value):
        put_feature(feat_ref, row, value)

    three, five, fifteen = math.sqrt(3.0), math.sqrt(5.0), math.sqrt(15.0)
    put(F_Y, jnp.ones(shape, F32))
    put(F_Y + 1, three * nx)
    put(F_Y + 2, three * ny)
    put(F_Y + 3, three * nz)
    put(F_Y + 4, fifteen * nx * ny)
    put(F_Y + 5, fifteen * ny * nz)
    put(F_Y + 6, (0.5 * five) * (3.0 * nz * nz - 1.0))
    put(F_Y + 7, fifteen * nx * nz)
    put(F_Y + 8, (0.5 * fifteen) * (nx * nx - ny * ny))
    scaled = distance * (1.0 / CUTOFF)
    inside = 1.0 - scaled * scaled
    put(F_W, live * inside * inside)
    put(F_DW, live * (-4.0 / CUTOFF) * scaled * inside)
    put(F_INV, inverse)
    angle = distance * (math.pi / CUTOFF)
    sine, cosine = jnp.sin(angle), jnp.cos(angle)
    last_s, last_c = jnp.zeros(shape, F32), jnp.ones(shape, F32)
    now_s, now_c = sine, cosine
    for k in range(1, NBASIS + 1):
        basis = CELL_SIDE * now_s * inverse
        put(F_B + k - 1, basis)
        put(F_DB + k - 1, (CELL_SIDE * k * math.pi / CUTOFF * now_c - basis) * inverse)
        last_s, now_s = now_s, 2.0 * cosine * now_s - last_s
        last_c, now_c = now_c, 2.0 * cosine * now_c - last_c

    atoms = one_hot(iota((PER_CELL, CELL_PAIRS), 0) == (iota((PER_CELL, CELL_PAIRS), 1) >> 5))

    def moments(i):
        harmonic = feature_rows(feat_ref, F_Y, 9, i)
        weighted = feature_rows(feat_ref, F_B, NBASIS, i) * feature_rows(feat_ref, F_W, 1, i)
        products = jnp.concatenate([harmonic[m : m + 1] * weighted for m in range(9)], 0)
        high, low = halves(products)
        for z in range(CZ):
            part = slice(z * CELL_PAIRS, (z + 1) * CELL_PAIRS)
            start = pl.multiple_of((i * CZ + z) * PER_CELL, PER_CELL)
            moment_ref[pl.ds(start, PER_CELL), :] = dims(atoms, high[:, part], 1, 1) + dims(
                atoms, low[:, part], 1, 1
            )

    looped(COLS, moments, 2)

    kind = one_hot(iota((SPECIES, ATOMS), 0) == species_ref[...])
    embed_high, embed_low = halves(embed_ref[...] * (1.0 / math.sqrt(SLOTS)))
    scale = dims(kind, embed_high, 0, 0) + dims(kind, embed_low, 0, 0)
    scale_ref[...] = scale
    sums = dims_three(moment_ref[...], radial_blocks(radial_ref[...]), 1, 0)
    invariants = [None] * 3
    for m in range(9):
        value = sums[:, m * CH : (m + 1) * CH] * scale
        env_ref[m] = value
        degree = DEGREE[m]
        squared = value * value
        invariants[degree] = (
            squared if invariants[degree] is None else invariants[degree] + squared
        )
    normed, _ = normalised(invariants)
    mixed = dims(jnp.concatenate(normed, 1).astype(BF16), mix_ref[...], 1, 0)
    hidden = (mixed * sigmoid_of(mixed)).astype(BF16)
    for y in range(CY):
        for x in range(CX):
            hidden_ref[y, x] = hidden[(x * CY + y) * 32 : (x * CY + y + 1) * 32]


def normalised(invariants):
    total = sum(jnp.sum(q * q, 1, keepdims=True) for q in invariants)
    inverse = lax.rsqrt(total * (1.0 / (3 * CH)) + NORM_EPS)
    return [q * inverse for q in invariants], inverse


def spans(z):
    return slice(z * CELL_PAIRS, (z + 1) * CELL_PAIRS)


def rows_of(column, z):
    return pl.ds(pl.multiple_of((column * CZ + z) * PER_CELL, PER_CELL), PER_CELL)


def slab_rows(block, x):
    return pl.ds(pl.multiple_of((block * 8 + x) * RUN, RUN), SLAB)


def fill_table(table_ref, start, around, weights, runs):
    for h in range(2):
        rows = around[:, h].reshape(runs * RUN, CH)
        table_ref[start : start + runs * RUN, h * CH : (h + 1) * CH] = dims(
            rows, weights, 1, 0
        ).astype(BF16)


def atom_blocks():
    mask = iota((PER_CELL, CELL_PAIRS), 0) == (iota((PER_CELL, CELL_PAIRS), 1) >> 5)
    return mask, one_hot(mask)


def pair_features(harmonic, part, mask):
    return [jnp.where(mask, harmonic[m : m + 1, part], 0.0).astype(BF16) for m in range(9)]


def scaled_env(env_ref, couple_ref, column, z):
    rows = rows_of(column, z)
    return [
        (env_ref[m, rows, :] * couple_ref[DEGREE[m] : DEGREE[m] + 1]).astype(BF16)
        for m in range(9)
    ]


def early_kernel(
    around_ref,
    hidden_ref,
    env_ref,
    feat_ref,
    code_ref,
    center_ref,
    neigh_ref,
    radial_ref,
    couple_ref,
    early_ref,
    table_ref,
    own_ref,
):
    y = pl.program_id(0)

    @pl.when(y == 0)
    def _():
        fill_table(table_ref, 0, around_ref, neigh_ref[...], OWN_RUNS)
        for yy in range(CY):
            for x in range(CX):
                start = (x * CY + yy) * 32
                own_ref[start : start + 32, :] = dims(
                    hidden_ref[yy, x], center_ref[...], 1, 0
                )

    radial_high, radial_low = halves(radial_ref[...])
    mask, atoms = atom_blocks()
    row_slab = iota((SLAB, PAIRS), 0)

    def column(x, first, count, block):
        i = x * CY + y
        harmonic = feature_rows(feat_ref, F_Y, 9, i)
        basis_high, basis_low = halves(feature_rows(feat_ref, F_B, NBASIS, i))
        code = code_ref[0, pl.ds(i, 1), :]
        upper = code_ref[1, pl.ds(i, 1), :] > 0
        parts = []
        for z in range(CZ):
            part = spans(z)
            feature = jnp.concatenate(
                pair_features(harmonic, part, mask)
                + [
                    atoms,
                    atoms,
                    basis_high[:, part],
                    basis_low[:, part],
                    basis_high[:, part],
                    jnp.zeros((8, CELL_PAIRS), BF16),
                ],
                0,
            )
            own_high, own_low = halves(own_ref[rows_of(i, z), :])
            table = jnp.concatenate(
                scaled_env(env_ref, couple_ref, i, z)
                + [
                    own_high,
                    own_low,
                    radial_high,
                    radial_high,
                    radial_low,
                    jnp.zeros((8, CH), BF16),
                ],
                0,
            )
            parts.append(dims(table, feature, 0, 0))
        fetched = None
        for k in range(count):
            hot = one_hot(row_slab == code - (first + k) * SLAB)
            found = dims(table_ref[slab_rows(block + k, x), :], hot, 0, 0)
            fetched = found if fetched is None else fetched + found
        early_ref[x] = jnp.concatenate(parts, 1) + jnp.where(upper, fetched[CH:], fetched[:CH])

    @pl.when((y == 0) | (y == 3))
    def _():
        far = (y == 3).astype(jnp.int32)
        looped(CX, lambda x: column(x, 2 - 2 * far, 3, far), 1)

    @pl.when((y == 1) | (y == 2))
    def _():
        looped(CX, lambda x: column(x, 2 - y, 4, 0), 1)


def pair_kernel(
    early_ref,
    low_ref,
    up_ref,
    feat_ref,
    code_ref,
    neigh_ref,
    two_ref,
    three_ref,
    readout_ref,
    energy_ref,
    low_out_ref,
    up_out_ref,
    grad_ref,
    raw_ref,
    table_ref,
    total_ref,
    hot_ref,
):
    y = pl.program_id(0)

    @pl.when(y == 0)
    def _():
        fill_table(table_ref, 0, low_ref, neigh_ref[...], RIM_RUNS)
        fill_table(table_ref, RIM_RUNS * RUN, up_ref, neigh_ref[...], RIM_RUNS)
        total_ref[...] = jnp.zeros_like(total_ref)

    readout = jnp.transpose(jnp.broadcast_to(readout_ref[...], (CH, CH)))
    readout = jnp.concatenate([readout] * LANES, 1)
    row_slab = iota((SLAB, PAIRS), 0)

    def column(x, first, count, block):
        i = x * CY + y
        weight = feature_rows(feat_ref, F_W, 1, i)
        code = code_ref[0, pl.ds(i, 1), :]
        upper = code_ref[1, pl.ds(i, 1), :] > 0
        fetched = None
        for k in range(count):
            hot = one_hot(row_slab == code - (first + k) * SLAB)
            hot_ref[k * SLAB : (k + 1) * SLAB, :] = hot
            found = dims(table_ref[slab_rows(block + k, x), :], hot, 0, 0)
            fetched = found if fetched is None else fetched + found
        value = early_ref[x] + jnp.where(upper, fetched[CH:], fetched[:CH])
        gate = sigmoid_of(value)
        one = value * gate
        slope_one = gate + one - one * gate
        value = dims(two_ref[...], one.astype(BF16), 0, 0)
        gate = sigmoid_of(value)
        two = value * gate
        slope_two = gate + two - two * gate
        value = dims(three_ref[...], two.astype(BF16), 0, 0)
        gate = sigmoid_of(value)
        top = value * gate
        slope_top = gate + top - top * gate
        raw_ref[pl.ds(i, 1), :] = jnp.sum(top * readout, 0, keepdims=True)
        grad = slope_top * readout * weight
        grad = dims(three_ref[...], grad.astype(BF16), 1, 0) * slope_two
        grad = dims(two_ref[...], grad.astype(BF16), 1, 0) * slope_one
        spread = jnp.concatenate(
            [jnp.where(upper, 0.0, grad), jnp.where(upper, grad, 0.0)], 0
        ).astype(BF16)
        grad_ref[x] = grad.astype(BF16)
        found = dims(hot_ref[: count * SLAB, :], spread, 1, 1)
        for k in range(count):
            total_ref[slab_rows(block + k, x), :] += found[k * SLAB : (k + 1) * SLAB]

    @pl.when((y == 0) | (y == 3))
    def _():
        far = (y == 3).astype(jnp.int32)
        looped(CX, lambda x: column(x, 3 * far, 2, 2 * far), 1)

    @pl.when((y == 1) | (y == 2))
    def _():
        looped(CX, lambda x: column(x, 4 * (y - 1), 1, y), 1)

    @pl.when(y == CY - 1)
    def _():
        for h in range(2):
            rim = total_ref[:, h * CH : (h + 1) * CH].astype(BF16).reshape(2 * RIM_RUNS, RUN, CH)
            low_out_ref[:, h] = rim[:RIM_RUNS]
            up_out_ref[:, h] = rim[RIM_RUNS:]
        gather = one_hot(iota((32, PAIRS), 0) == (iota((32, PAIRS), 1) >> 5))
        high, low = halves(raw_ref[...] * whole_feature(feat_ref, F_W))
        energy_ref[...] = dims(high, gather, 1, 1) + dims(low, gather, 1, 1)


def spread_kernel(grad_ref, code_ref, ghost_ref, total_ref, hot_ref):
    y = pl.program_id(0)

    @pl.when(y == 0)
    def _():
        total_ref[...] = jnp.zeros_like(total_ref)

    row_slab = iota((SLAB, PAIRS), 0)

    def column(x, first, count, block):
        i = x * CY + y
        code = code_ref[0, pl.ds(i, 1), :]
        upper = jnp.where(code_ref[1, pl.ds(i, 1), :] > 0, 1.0, 0.0).astype(BF16)
        for k in range(count):
            hot_ref[k * SLAB : (k + 1) * SLAB, :] = one_hot(
                row_slab == code - (first + k) * SLAB
            )
        grad = grad_ref[x]
        high = grad * upper
        spread = jnp.concatenate([grad - high, high], 0)
        found = dims(hot_ref[: count * SLAB, :], spread, 1, 1)
        for k in range(count):
            total_ref[slab_rows(block + k, x), :] += found[k * SLAB : (k + 1) * SLAB]

    @pl.when((y == 0) | (y == 3))
    def _():
        far = (y == 3).astype(jnp.int32)
        looped(CX, lambda x: column(x, 2 - 2 * far, 3, far), 1)

    @pl.when((y == 1) | (y == 2))
    def _():
        looped(CX, lambda x: column(x, 2 - y, 4, 0), 1)

    @pl.when(y == CY - 1)
    def _():
        for h in range(2):
            ghost_ref[:, h] = (
                total_ref[:, h * CH : (h + 1) * CH].astype(BF16).reshape(OWN_RUNS, RUN, CH)
            )


def back_kernel(
    grad_ref,
    env_ref,
    scale_ref,
    feat_ref,
    mix_ref,
    center_ref,
    radial_a_ref,
    radial_ref,
    couple_ref,
    down_ref,
    base_ref,
    slope_ref,
    normed_ref,
    pull_ref,
    direct_ref,
    grad_env_ref,
    grad_center_ref,
):
    y = pl.program_id(0)
    mask, atoms = atom_blocks()
    radial = radial_ref[...].astype(BF16)

    def column(x):
        i = x * CY + y
        harmonic = feature_rows(feat_ref, F_Y, 9, i)
        for z in range(CZ):
            part = spans(z)
            grad = grad_ref[x, :, part]
            feature = jnp.concatenate(pair_features(harmonic, part, mask) + [atoms], 0)
            back = dims(feature, grad, 1, 1)
            for m in range(9):
                grad_env_ref[m, rows_of(i, z), :] = back[m * PER_CELL : (m + 1) * PER_CELL]
            grad_center_ref[rows_of(i, z), :] = back[9 * PER_CELL :]
            table = jnp.concatenate(
                scaled_env(env_ref, couple_ref, i, z) + [radial, jnp.zeros((8, CH), BF16)], 0
            )
            down = dims(table, grad, 1, 0)
            rows = [down[9 * PER_CELL : 9 * PER_CELL + NBASIS]]
            for m in range(9):
                kept = jnp.where(mask, down[m * PER_CELL : (m + 1) * PER_CELL], 0.0)
                rows.append(jnp.sum(kept, 0, keepdims=True))
            down_ref[i, 0 : NBASIS + 9, part] = jnp.concatenate(rows, 0)

    looped(CX, column, 1)

    @pl.when(y == CY - 1)
    def _():
        invariants = [None] * 3
        for m in range(9):
            value = env_ref[m]
            squared = value * value
            degree = DEGREE[m]
            invariants[degree] = (
                squared if invariants[degree] is None else invariants[degree] + squared
            )
        normed, inverse = normalised(invariants)
        mixed = dims(jnp.concatenate(normed, 1).astype(BF16), mix_ref[...], 1, 0)
        gate = sigmoid_of(mixed)
        act = mixed * gate
        slope_ref[...] = gate + act - act * gate
        for d in range(3):
            normed_ref[d] = normed[d]
        high, low = halves(grad_center_ref[...])
        base_ref[...] = dims(high, center_ref[...], 1, 1) + dims(low, center_ref[...], 1, 1)
        scale = scale_ref[...]
        for m in range(9):
            pull_ref[m] = 2.0 * env_ref[m] * scale * inverse
        pulled = [
            grad_env_ref[m] * couple_ref[DEGREE[m] : DEGREE[m] + 1] * scale for m in range(9)
        ]
        direct_ref[...] = dims_three(
            jnp.concatenate(pulled, 1), radial_blocks(radial_a_ref[...]), 1, 1
        )


def force_kernel(
    neigh_ref,
    base_ref,
    slope_ref,
    normed_ref,
    pull_env_ref,
    direct_ref,
    feat_ref,
    code_ref,
    down_ref,
    raw_ref,
    mix_ref,
    proj_ref,
    radial_ref,
    own_ref,
    ghost_ref,
    moment_ref,
    pull_ref,
):
    neigh = jnp.concatenate([neigh_ref[y, x] for x in range(CX) for y in range(CY)], 0)
    high, low = halves(neigh)
    grad = base_ref[...] + dims(high, proj_ref[...], 1, 1) + dims(low, proj_ref[...], 1, 1)
    grad = grad * slope_ref[...]
    grad = dims(grad.astype(BF16), mix_ref[...], 1, 1)
    grads = [grad[:, d * CH : (d + 1) * CH] for d in range(3)]
    normed = [normed_ref[d] for d in range(3)]
    mean = sum(jnp.sum(g * q, 1, keepdims=True) for g, q in zip(grads, normed)) * (1.0 / (3 * CH))
    grads = [g - q * mean for g, q in zip(grads, normed)]
    pulled = [pull_env_ref[m] * grads[DEGREE[m]] for m in range(9)]
    moment_ref[...] = direct_ref[...] + dims_three(
        jnp.concatenate(pulled, 1), radial_blocks(radial_ref[...]), 1, 1
    )

    _, atoms = atom_blocks()
    row_cells = iota((5 * CELL_ROWS, PAIRS), 0)
    row_slots = iota((PER_CELL, PAIRS), 0)
    ghost_ref[...] = jnp.zeros_like(ghost_ref)
    three, five, fifteen = math.sqrt(3.0), math.sqrt(5.0), math.sqrt(15.0)

    def column(i):
        harmonic = feature_rows(feat_ref, F_Y, 9, i)
        basis = feature_rows(feat_ref, F_B, NBASIS, i)
        slope = feature_rows(feat_ref, F_DB, NBASIS, i)
        weight = feature_rows(feat_ref, F_W, 1, i)
        weight_slope = feature_rows(feat_ref, F_DW, 1, i)
        inverse = feature_rows(feat_ref, F_INV, 1, i)
        parts = []
        for z in range(CZ):
            high, low = halves(moment_ref[rows_of(i, z), :])
            parts.append(dims(high, atoms, 0, 0) + dims(low, atoms, 0, 0))
        back = jnp.concatenate(parts, 1)
        weighted = basis * weight
        grad_weighted = jnp.zeros((NBASIS, PAIRS), F32)
        chain = []
        for m in range(9):
            block = back[m * NBASIS : (m + 1) * NBASIS]
            grad_weighted += block * harmonic[m : m + 1]
            if m:
                chain.append(
                    down_ref[i, NBASIS + m : NBASIS + m + 1, :]
                    + jnp.sum(block * weighted, 0, keepdims=True)
                )
        y1, y2, y3, y4, y5, y6, y7, y8 = chain
        grad_basis = down_ref[i, 0:NBASIS, :] + grad_weighted * weight
        grad_weight = raw_ref[pl.ds(i, 1), :] + jnp.sum(grad_weighted * basis, 0, keepdims=True)
        radial = jnp.sum(grad_basis * slope, 0, keepdims=True) + grad_weight * weight_slope
        nx, ny, nz = (harmonic[c : c + 1] * (1.0 / three) for c in range(1, 4))
        grad_x = three * y1 + fifteen * (ny * y4 + nz * y7 + nx * y8)
        grad_y = three * y2 + fifteen * (nx * y4 + nz * y5 - ny * y8)
        grad_z = three * y3 + fifteen * (ny * y5 + nx * y7) + (3.0 * five) * nz * y6
        along = radial - inverse * (nx * grad_x + ny * grad_y + nz * grad_z)
        pulls = (
            grad_x * inverse + nx * along,
            grad_y * inverse + ny * along,
            grad_z * inverse + nz * along,
        )
        x, y = i // CY, i % CY
        hot = one_hot(row_cells == code_ref[2, pl.ds(i, 1), :])
        mask = row_slots == code_ref[3, pl.ds(i, 1), :]
        for c in range(3):
            pull_ref[c, pl.ds(i, 1), :] = pulls[c]
        kept = jnp.concatenate([jnp.where(mask, pull, 0.0) for pull in pulls], 0)
        found = dims(hot, kept.astype(BF16), 1, 1)
        for dx in range(5):
            start = pl.multiple_of(((x + dx) * 8 + y) * 8, 8)
            ghost_ref[pl.ds(start, CELL_ROWS), :] += found[dx * CELL_ROWS : (dx + 1) * CELL_ROWS]

    looped(COLS, column, 2)

    gather = one_hot(iota((32, PAIRS), 0) == (iota((32, PAIRS), 1) >> 5))
    for c in range(3):
        high, low = halves(pull_ref[c])
        own_ref[c] = dims(high, gather, 1, 1) + dims(low, gather, 1, 1)


def call(kernel, outs, scratch, *args, by_y=(), by_y_out=(), micros=20):
    def spec(shape, moving):
        zeros = (0,) * len(shape)
        if not moving:
            return pl.BlockSpec(shape, lambda y: zeros)
        return pl.BlockSpec((shape[0] // CY,) + shape[1:], lambda y: (y,) + zeros[1:])

    grid = {}
    if by_y or by_y_out:
        grid = dict(
            grid=(CY,),
            in_specs=[spec(a.shape, k in by_y) for k, a in enumerate(args)],
            out_specs=[spec(shape, k in by_y_out) for k, (shape, _) in enumerate(outs)],
        )
    return pl.pallas_call(
        kernel,
        out_shape=[jax.ShapeDtypeStruct(shape, dtype) for shape, dtype in outs],
        scratch_shapes=[pltpu.VMEM(shape, dtype) for shape, dtype in scratch],
        compiler_params=pltpu.CompilerParams(vmem_limit_bytes=56 * 2**20),
        cost_estimate=pl.CostEstimate(
            flops=micros * 10**9, bytes_accessed=micros * 3 * 10**6, transcendentals=0
        ),
        **grid,
    )(*args)


def shifted(block, axis, distance):
    size = lax.axis_size(axis)
    return lax.ppermute(block, axis, [(i, (i + distance) % size) for i in range(size)])


def rims(array, axis, dim):
    length = array.shape[dim]
    before = shifted(lax.slice_in_dim(array, length - 2, length, axis=dim), axis, 1)
    after = shifted(lax.slice_in_dim(array, 0, 2, axis=dim), axis, -1)
    return before, after


def padded(array, axis, dim, tail=0):
    before, after = rims(array, axis, dim)
    parts = [before, array, after]
    if tail:
        parts.append(jnp.zeros(after.shape[:dim] + (tail,) + after.shape[dim + 1 :], array.dtype))
    return jnp.concatenate(parts, axis=dim)


def folded(array, axis, dim, length):
    lower = lax.slice_in_dim(array, 0, 2, axis=dim).astype(BF16)
    upper = lax.slice_in_dim(array, length + 2, length + 4, axis=dim).astype(BF16)
    core = lax.slice_in_dim(array, 2, length + 2, axis=dim).astype(F32)
    to_first = shifted(upper, axis, 1).astype(F32)
    to_last = shifted(lower, axis, -1).astype(F32)
    if length == 2:
        return core + to_first + to_last
    return core + jnp.concatenate([to_first, to_last], axis=dim)


def shards(
    offsets,
    species,
    neighbours,
    counts,
    embed,
    radial_a,
    mix_in,
    proj_center,
    proj_neigh,
    radial_b,
    couple,
    latent_two,
    latent_three,
    readout,
):
    numbers = neighbours.reshape(COLS, PAIRS)
    places = offsets.reshape(CX, CY, CZ, 48)
    around = padded(padded(padded(places, "gx", 0), "gy", 1), "gz", 2, tail=2)
    own = offsets.reshape(COLS, CZ, 3, PER_CELL).transpose(2, 0, 1, 3).reshape(3 * COLS, 32)
    hidden, env, scale, feats, codes = call(
        env_kernel,
        [
            ((CY, CX, 32, CH), BF16),
            ((9, ATOMS, CH), F32),
            ((ATOMS, CH), F32),
            ((LANES * F_COUNT * COLS, 128), F32),
            ((4, COLS, PAIRS), jnp.int32),
        ],
        [((3, COLS, PAIRS), F32), ((ATOMS, 72), F32)],
        numbers,
        around.reshape(512, 48),
        own,
        counts.reshape(COLS, 32),
        species.reshape(1, ATOMS),
        embed,
        radial_a,
        mix_in,
    )
    grid = hidden.reshape(CY, CX, CZ, PER_CELL, CH)
    wide = padded(padded(grid, "gz", 2), "gx", 1)
    low, up = rims(wide, "gy", 0)
    (early,) = call(
        early_kernel,
        [((COLS, CH, PAIRS), F32)],
        [((OWN_RUNS * RUN, 2 * CH), BF16), ((ATOMS, CH), F32)],
        wide.reshape(OWN_RUNS, 2, RUN, CH),
        hidden,
        env,
        feats,
        codes,
        proj_center,
        proj_neigh,
        radial_b,
        couple,
        by_y_out=(0,),
    )
    energy, low_back, up_back, grads, raw = call(
        pair_kernel,
        [
            ((COLS, 32), F32),
            ((RIM_RUNS, 2, RUN, CH), BF16),
            ((RIM_RUNS, 2, RUN, CH), BF16),
            ((COLS, CH, PAIRS), BF16),
            ((COLS, PAIRS), F32),
        ],
        [
            ((2 * RIM_RUNS * RUN, 2 * CH), BF16),
            ((2 * RIM_RUNS * RUN, 2 * CH), F32),
            ((2 * SLAB, PAIRS), BF16),
        ],
        early,
        low.reshape(RIM_RUNS, 2, RUN, CH),
        up.reshape(RIM_RUNS, 2, RUN, CH),
        feats,
        codes,
        proj_neigh,
        latent_two,
        latent_three,
        readout.reshape(1, CH),
        by_y=(0,),
        by_y_out=(3,),
    )
    to_first = shifted(up_back, "gy", 1)
    to_last = shifted(low_back, "gy", -1)
    (ghost,) = call(
        spread_kernel,
        [((OWN_RUNS, 2, RUN, CH), BF16)],
        [((OWN_RUNS * RUN, 2 * CH), F32), ((4 * SLAB, PAIRS), BF16)],
        grads,
        codes,
        by_y=(0,),
    )
    ghost = ghost.astype(F32) + jnp.concatenate([to_first, to_last], 0).astype(F32)
    ghost = ghost.reshape(CY, CX + 4, CZ + 4, PER_CELL, CH)
    owned = folded(folded(ghost, "gx", 1, CX), "gz", 2, CZ)
    down, base, slope, normed, pull, direct = call(
        back_kernel,
        [
            ((COLS, 24, PAIRS), F32),
            ((ATOMS, CH), F32),
            ((ATOMS, CH), F32),
            ((3, ATOMS, CH), F32),
            ((9, ATOMS, CH), F32),
            ((ATOMS, 72), F32),
        ],
        [((9, ATOMS, CH), F32), ((ATOMS, CH), F32)],
        grads,
        env,
        scale,
        feats,
        mix_in,
        proj_center,
        radial_a,
        radial_b,
        couple,
        by_y=(0,),
    )
    own_pull, far_pull = call(
        force_kernel,
        [((3, COLS, 32), F32), ((512, 48), F32)],
        [((ATOMS, 72), F32), ((3, COLS, PAIRS), F32)],
        owned.reshape(CY, CX, 32, CH),
        base,
        slope,
        normed,
        pull,
        direct,
        feats,
        codes,
        down,
        raw,
        mix_in,
        proj_neigh,
        radial_a,
    )
    far = far_pull.reshape(CX + 4, CY + 4, 8, 48)
    far = folded(folded(folded(far, "gx", 0, CX), "gy", 1, CY), "gz", 2, CZ)
    near = own_pull.reshape(3, CX, CY, CZ, PER_CELL).transpose(1, 2, 3, 0, 4)
    forces = near - far.reshape(CX, CY, CZ, 3, PER_CELL)
    return (forces, energy.reshape(CX, CY, CZ, PER_CELL))


def solution(mesh):
    placed = (
        P("gx", "gy", "gz", None, None),
        P("gx", "gy", "gz", None),
        P("gx", "gy", "gz", None, None),
        P("gx", "gy", "gz", None),
    ) + (P(),) * 10
    return jax.shard_map(
        shards,
        mesh=mesh,
        in_specs=placed,
        out_specs=(P("gx", "gy", "gz", None, None), P("gx", "gy", "gz", None)),
        check_vma=False,
    )
```

```python
import math

import jax
import jax.numpy as jnp
from jax import lax
from jax.experimental import pallas as pl
from jax.experimental.pallas import tpu as pltpu
from jax.sharding import PartitionSpec as P

CX = 4
CY = 4
CZ = 2
PER_CELL = 16
SLOTS = 32
CH = 128
NBASIS = 8
SPECIES = 4

CELL_SIDE = 2.0
CUTOFF = 10.5
NORM_EPS = 1e-05

COLS = CX * CY
PAIRS = CZ * PER_CELL * SLOTS
CELL_PAIRS = PER_CELL * SLOTS
ATOMS = COLS * CZ * PER_CELL
RUN = 48
SLAB = 5 * RUN
CELL_ROWS = 40
OWN_RUNS = CY * (CX + 4)
RIM_RUNS = 2 * (CX + 4)
LANES = PAIRS // 128

F32 = jnp.float32
BF16 = jnp.bfloat16
DEGREE = (0, 1, 1, 1, 2, 2, 2, 2, 2)

F_Y = 0
F_W = 9
F_DW = 10
F_B = 11
F_DB = 19
F_INV = 27
F_COUNT = 28

G_B = 0
G_Y = 8
G_E = 17
G_COUNT = 24


def dims(a, b, ca, cb):
    return lax.dot_general(a, b, (((ca,), (cb,)), ((), ())), preferred_element_type=F32)


def halves(value):
    high = value.astype(BF16)
    return high, (value - high.astype(F32)).astype(BF16)


def dims_three(a, b, ca, cb):
    a_high, a_low = halves(a)
    b_high, b_low = halves(b)
    return dims(a_high, b_high, ca, cb) + (
        dims(a_high, b_low, ca, cb) + dims(a_low, b_high, ca, cb)
    )


def iota(shape, dim):
    return lax.broadcasted_iota(jnp.int32, shape, dim)


def one_hot(condition):
    return jnp.where(condition, 1.0, 0.0).astype(BF16)


def radial_blocks(radial):
    rows = []
    for m in range(9):
        before = [jnp.zeros((NBASIS, m * CH), F32)] if m else []
        after = [jnp.zeros((NBASIS, (8 - m) * CH), F32)] if m < 8 else []
        rows.append(jnp.concatenate(before + [radial] + after, 1))
    return jnp.concatenate(rows, 0)


def looped(count, body, unroll):
    def step(j, carry):
        for k in range(unroll):
            body(j * unroll + k)
        return carry

    lax.fori_loop(0, count // unroll, step, 0)


def sigmoid_of(v):
    return 0.5 * jnp.tanh(0.5 * v) + 0.5


def feature_rows(ref, row, count, i):
    blocks = []
    for lane in range(LANES):
        start = (lane * F_COUNT + row) * COLS + i
        blocks.append(ref[pl.ds(start, count, stride=COLS) if count > 1 else pl.ds(start, 1), :])
    return jnp.concatenate(blocks, 1)


def whole_feature(ref, row):
    blocks = []
    for lane in range(LANES):
        start = (lane * F_COUNT + row) * COLS
        blocks.append(ref[start : start + COLS, :])
    return jnp.concatenate(blocks, 1)


def put_feature(ref, row, value):
    for lane in range(LANES):
        start = (lane * F_COUNT + row) * COLS
        ref[start : start + COLS, :] = value[:, lane * 128 : (lane + 1) * 128]


def cell_window(ref, x, y):
    parts = []
    for dx in range(5):
        start = pl.multiple_of(((x + dx) * 8 + y) * 8, 8)
        parts.append(ref[pl.ds(start, CELL_ROWS), :])
    return jnp.concatenate(parts, 0)


def env_kernel(
    nbr_ref,
    ext_ref,
    own_ref,
    count_ref,
    species_ref,
    embed_ref,
    radial_ref,
    mix_ref,
    hidden_ref,
    env_ref,
    scale_ref,
    feat_ref,
    code_ref,
    near_ref,
    moment_ref,
):
    shape = (COLS, PAIRS)
    number = nbr_ref[...]
    slot = number & 15
    cell = number >> 4
    over = (cell * 43691) >> 18
    cell_z = cell - 6 * over
    cell_y = over & 7
    cell_x = over >> 3
    column = iota(shape, 0)
    lane = iota(shape, 1)
    dx = cell_x - (column >> 2)
    dy = cell_y - (column & 3)
    upper = (cell_z >= 3).astype(jnp.int32)
    code_ref[0] = (dy * 5 + dx) * RUN + (cell_z - 3 * upper) * PER_CELL + slot
    code_ref[1] = upper
    code_ref[2] = dx * CELL_ROWS + dy * 8 + cell_z
    code_ref[3] = slot

    row_cells = iota((5 * CELL_ROWS, PAIRS), 0)
    row_slots = iota((PER_CELL, PAIRS), 0)

    def fetch(i):
        hot = one_hot(row_cells == code_ref[2, pl.ds(i, 1), :])
        high, low = halves(cell_window(ext_ref, i // CY, i % CY))
        places = dims(high, hot, 0, 0) + dims(low, hot, 0, 0)
        mask = row_slots == code_ref[3, pl.ds(i, 1), :]
        for c in range(3):
            part = places[c * PER_CELL : (c + 1) * PER_CELL]
            near_ref[c, pl.ds(i, 1), :] = jnp.sum(jnp.where(mask, part, 0.0), 0, keepdims=True)

    looped(COLS, fetch, 4)

    spread = one_hot(iota((32, PAIRS), 0) == (iota((32, PAIRS), 1) >> 5))
    own_high, own_low = halves(own_ref[...])
    own = dims(own_high, spread, 1, 0) + dims(own_low, spread, 1, 0)
    count = dims(count_ref[...].astype(F32).astype(BF16), spread, 1, 0)
    live = ((lane & 31).astype(F32) < count).astype(F32)
    step_x = (dx - 2).astype(F32) * CELL_SIDE + near_ref[0] - own[0:COLS]
    step_y = (dy - 2).astype(F32) * CELL_SIDE + near_ref[1] - own[COLS : 2 * COLS]
    step_z = (
        (cell_z - 2 - (lane >> 9)).astype(F32) * CELL_SIDE + near_ref[2] - own[2 * COLS : 3 * COLS]
    )
    square = step_x * step_x + step_y * step_y + step_z * step_z
    distance = jnp.sqrt(square)
    inverse = 1.0 / distance
    nx, ny, nz = step_x * inverse, step_y * inverse, step_z * inverse

    def put(row, value):
        put_feature(feat_ref, row, value)

    three, five, fifteen = math.sqrt(3.0), math.sqrt(5.0), math.sqrt(15.0)
    put(F_Y, jnp.ones(shape, F32))
    put(F_Y + 1, three * nx)
    put(F_Y + 2, three * ny)
    put(F_Y + 3, three * nz)
    put(F_Y + 4, fifteen * nx * ny)
    put(F_Y + 5, fifteen * ny * nz)
    put(F_Y + 6, (0.5 * five) * (3.0 * nz * nz - 1.0))
    put(F_Y + 7, fifteen * nx * nz)
    put(F_Y + 8, (0.5 * fifteen) * (nx * nx - ny * ny))
    scaled = distance * (1.0 / CUTOFF)
    inside = 1.0 - scaled * scaled
    put(F_W, live * inside * inside)
    put(F_DW, live * (-4.0 / CUTOFF) * scaled * inside)
    put(F_INV, inverse)
    angle = distance * (math.pi / CUTOFF)
    sine, cosine = jnp.sin(angle), jnp.cos(angle)
    last_s, last_c = jnp.zeros(shape, F32), jnp.ones(shape, F32)
    now_s, now_c = sine, cosine
    for k in range(1, NBASIS + 1):
        basis = CELL_SIDE * now_s * inverse
        put(F_B + k - 1, basis)
        put(F_DB + k - 1, (CELL_SIDE * k * math.pi / CUTOFF * now_c - basis) * inverse)
        last_s, now_s = now_s, 2.0 * cosine * now_s - last_s
        last_c, now_c = now_c, 2.0 * cosine * now_c - last_c

    atoms = one_hot(iota((PER_CELL, CELL_PAIRS), 0) == (iota((PER_CELL, CELL_PAIRS), 1) >> 5))

    def moments(i):
        harmonic = feature_rows(feat_ref, F_Y, 9, i)
        weighted = feature_rows(feat_ref, F_B, NBASIS, i) * feature_rows(feat_ref, F_W, 1, i)
        products = jnp.concatenate([harmonic[m : m + 1] * weighted for m in range(9)], 0)
        high, low = halves(products)
        for z in range(CZ):
            part = slice(z * CELL_PAIRS, (z + 1) * CELL_PAIRS)
            start = pl.multiple_of((i * CZ + z) * PER_CELL, PER_CELL)
            moment_ref[pl.ds(start, PER_CELL), :] = dims(atoms, high[:, part], 1, 1) + dims(
                atoms, low[:, part], 1, 1
            )

    looped(COLS, moments, 4)

    kind = one_hot(iota((SPECIES, ATOMS), 0) == species_ref[...])
    embed_high, embed_low = halves(embed_ref[...] * (1.0 / math.sqrt(SLOTS)))
    scale = dims(kind, embed_high, 0, 0) + dims(kind, embed_low, 0, 0)
    scale_ref[...] = scale
    sums = dims_three(moment_ref[...], radial_blocks(radial_ref[...]), 1, 0)
    invariants = [None] * 3
    for m in range(9):
        value = sums[:, m * CH : (m + 1) * CH] * scale
        env_ref[m] = value
        degree = DEGREE[m]
        squared = value * value
        invariants[degree] = (
            squared if invariants[degree] is None else invariants[degree] + squared
        )
    normed, _ = normalised(invariants)
    mixed = dims(jnp.concatenate(normed, 1).astype(BF16), mix_ref[...], 1, 0)
    hidden = (mixed * sigmoid_of(mixed)).astype(BF16)
    for y in range(CY):
        for x in range(CX):
            hidden_ref[y, x] = hidden[(x * CY + y) * 32 : (x * CY + y + 1) * 32]


def normalised(invariants):
    total = sum(jnp.sum(q * q, 1, keepdims=True) for q in invariants)
    inverse = lax.rsqrt(total * (1.0 / (3 * CH)) + NORM_EPS)
    return [q * inverse for q in invariants], inverse


def spans(z):
    return slice(z * CELL_PAIRS, (z + 1) * CELL_PAIRS)


def rows_of(column, z):
    return pl.ds(pl.multiple_of((column * CZ + z) * PER_CELL, PER_CELL), PER_CELL)


def slab_rows(block, x):
    return pl.ds(pl.multiple_of((block * 8 + x) * RUN, RUN), SLAB)


def fill_table(table_ref, start, around, weights, runs):
    for h in range(2):
        rows = around[:, h].reshape(runs * RUN, CH)
        table_ref[start : start + runs * RUN, h * CH : (h + 1) * CH] = dims(
            rows, weights, 1, 0
        ).astype(BF16)


def atom_blocks():
    mask = iota((PER_CELL, CELL_PAIRS), 0) == (iota((PER_CELL, CELL_PAIRS), 1) >> 5)
    return mask, one_hot(mask)


def pair_features(harmonic, part, mask):
    return [jnp.where(mask, harmonic[m : m + 1, part], 0.0).astype(BF16) for m in range(9)]


def scaled_env(env_ref, couple_ref, column, z):
    rows = rows_of(column, z)
    return [
        (env_ref[m, rows, :] * couple_ref[DEGREE[m] : DEGREE[m] + 1]).astype(BF16)
        for m in range(9)
    ]


def early_kernel(
    around_ref,
    hidden_ref,
    env_ref,
    feat_ref,
    code_ref,
    center_ref,
    neigh_ref,
    radial_ref,
    couple_ref,
    early_ref,
    table_ref,
    own_ref,
):
    y = pl.program_id(0)

    @pl.when(y == 0)
    def _():
        fill_table(table_ref, 0, around_ref, neigh_ref[...], OWN_RUNS)
        for yy in range(CY):
            for x in range(CX):
                start = (x * CY + yy) * 32
                own_ref[start : start + 32, :] = dims(
                    hidden_ref[yy, x], center_ref[...], 1, 0
                )

    radial_high, radial_low = halves(radial_ref[...])
    mask, atoms = atom_blocks()
    row_slab = iota((SLAB, PAIRS), 0)

    def column(x, first, count, block):
        i = x * CY + y
        harmonic = feature_rows(feat_ref, F_Y, 9, i)
        basis_high, basis_low = halves(feature_rows(feat_ref, F_B, NBASIS, i))
        code = code_ref[0, pl.ds(i, 1), :]
        upper = code_ref[1, pl.ds(i, 1), :] > 0
        parts = []
        for z in range(CZ):
            part = spans(z)
            feature = jnp.concatenate(
                pair_features(harmonic, part, mask)
                + [
                    atoms,
                    atoms,
                    basis_high[:, part],
                    basis_low[:, part],
                    basis_high[:, part],
                    jnp.zeros((8, CELL_PAIRS), BF16),
                ],
                0,
            )
            own_high, own_low = halves(own_ref[rows_of(i, z), :])
            table = jnp.concatenate(
                scaled_env(env_ref, couple_ref, i, z)
                + [
                    own_high,
                    own_low,
                    radial_high,
                    radial_high,
                    radial_low,
                    jnp.zeros((8, CH), BF16),
                ],
                0,
            )
            parts.append(dims(table, feature, 0, 0))
        fetched = None
        for k in range(count):
            hot = one_hot(row_slab == code - (first + k) * SLAB)
            found = dims(table_ref[slab_rows(block + k, x), :], hot, 0, 0)
            fetched = found if fetched is None else fetched + found
        early_ref[x] = jnp.concatenate(parts, 1) + jnp.where(upper, fetched[CH:], fetched[:CH])

    @pl.when((y == 0) | (y == 3))
    def _():
        far = (y == 3).astype(jnp.int32)
        looped(CX, lambda x: column(x, 2 - 2 * far, 3, far), 4)

    @pl.when((y == 1) | (y == 2))
    def _():
        looped(CX, lambda x: column(x, 2 - y, 4, 0), 4)


def pair_kernel(
    early_ref,
    low_ref,
    up_ref,
    feat_ref,
    code_ref,
    neigh_ref,
    two_ref,
    three_ref,
    readout_ref,
    energy_ref,
    low_out_ref,
    up_out_ref,
    grad_ref,
    raw_ref,
    table_ref,
    total_ref,
    hot_ref,
):
    y = pl.program_id(0)

    @pl.when(y == 0)
    def _():
        fill_table(table_ref, 0, low_ref, neigh_ref[...], RIM_RUNS)
        fill_table(table_ref, RIM_RUNS * RUN, up_ref, neigh_ref[...], RIM_RUNS)
        total_ref[...] = jnp.zeros_like(total_ref)

    readout = jnp.transpose(jnp.broadcast_to(readout_ref[...], (CH, CH)))
    readout = jnp.concatenate([readout] * LANES, 1)
    row_slab = iota((SLAB, PAIRS), 0)

    def column(x, first, count, block):
        i = x * CY + y
        weight = feature_rows(feat_ref, F_W, 1, i)
        code = code_ref[0, pl.ds(i, 1), :]
        upper = code_ref[1, pl.ds(i, 1), :] > 0
        fetched = None
        for k in range(count):
            hot = one_hot(row_slab == code - (first + k) * SLAB)
            hot_ref[k * SLAB : (k + 1) * SLAB, :] = hot
            found = dims(table_ref[slab_rows(block + k, x), :], hot, 0, 0)
            fetched = found if fetched is None else fetched + found
        value = early_ref[x] + jnp.where(upper, fetched[CH:], fetched[:CH])
        gate = sigmoid_of(value)
        one = value * gate
        slope_one = gate + one - one * gate
        value = dims(two_ref[...], one.astype(BF16), 0, 0)
        gate = sigmoid_of(value)
        two = value * gate
        slope_two = gate + two - two * gate
        value = dims(three_ref[...], two.astype(BF16), 0, 0)
        gate = sigmoid_of(value)
        top = value * gate
        slope_top = gate + top - top * gate
        raw_ref[pl.ds(i, 1), :] = jnp.sum(top * readout, 0, keepdims=True)
        grad = slope_top * readout * weight
        grad = dims(three_ref[...], grad.astype(BF16), 1, 0) * slope_two
        grad = dims(two_ref[...], grad.astype(BF16), 1, 0) * slope_one
        spread = jnp.concatenate(
            [jnp.where(upper, 0.0, grad), jnp.where(upper, grad, 0.0)], 0
        ).astype(BF16)
        grad_ref[x] = grad.astype(BF16)
        found = dims(hot_ref[: count * SLAB, :], spread, 1, 1)
        for k in range(count):
            total_ref[slab_rows(block + k, x), :] += found[k * SLAB : (k + 1) * SLAB]

    @pl.when((y == 0) | (y == 3))
    def _():
        far = (y == 3).astype(jnp.int32)
        looped(CX, lambda x: column(x, 3 * far, 2, 2 * far), 4)

    @pl.when((y == 1) | (y == 2))
    def _():
        looped(CX, lambda x: column(x, 4 * (y - 1), 1, y), 4)

    @pl.when(y == CY - 1)
    def _():
        for h in range(2):
            rim = total_ref[:, h * CH : (h + 1) * CH].astype(BF16).reshape(2 * RIM_RUNS, RUN, CH)
            low_out_ref[:, h] = rim[:RIM_RUNS]
            up_out_ref[:, h] = rim[RIM_RUNS:]
        gather = one_hot(iota((32, PAIRS), 0) == (iota((32, PAIRS), 1) >> 5))
        high, low = halves(raw_ref[...] * whole_feature(feat_ref, F_W))
        energy_ref[...] = dims(high, gather, 1, 1) + dims(low, gather, 1, 1)


def spread_kernel(grad_ref, code_ref, ghost_ref, total_ref, hot_ref):
    y = pl.program_id(0)

    @pl.when(y == 0)
    def _():
        total_ref[...] = jnp.zeros_like(total_ref)

    row_slab = iota((SLAB, PAIRS), 0)

    def column(x, first, count, block):
        i = x * CY + y
        code = code_ref[0, pl.ds(i, 1), :]
        upper = jnp.where(code_ref[1, pl.ds(i, 1), :] > 0, 1.0, 0.0).astype(BF16)
        for k in range(count):
            hot_ref[k * SLAB : (k + 1) * SLAB, :] = one_hot(
                row_slab == code - (first + k) * SLAB
            )
        grad = grad_ref[x]
        high = grad * upper
        spread = jnp.concatenate([grad - high, high], 0)
        found = dims(hot_ref[: count * SLAB, :], spread, 1, 1)
        for k in range(count):
            total_ref[slab_rows(block + k, x), :] += found[k * SLAB : (k + 1) * SLAB]

    @pl.when((y == 0) | (y == 3))
    def _():
        far = (y == 3).astype(jnp.int32)
        looped(CX, lambda x: column(x, 2 - 2 * far, 3, far), 4)

    @pl.when((y == 1) | (y == 2))
    def _():
        looped(CX, lambda x: column(x, 2 - y, 4, 0), 4)

    @pl.when(y == CY - 1)
    def _():
        for h in range(2):
            ghost_ref[:, h] = (
                total_ref[:, h * CH : (h + 1) * CH].astype(BF16).reshape(OWN_RUNS, RUN, CH)
            )


def back_kernel(
    grad_ref,
    env_ref,
    scale_ref,
    feat_ref,
    mix_ref,
    center_ref,
    radial_a_ref,
    radial_ref,
    couple_ref,
    down_ref,
    base_ref,
    slope_ref,
    normed_ref,
    pull_ref,
    direct_ref,
    grad_env_ref,
    grad_center_ref,
):
    y = pl.program_id(0)
    mask, atoms = atom_blocks()
    radial = radial_ref[...].astype(BF16)

    def column(x):
        i = x * CY + y
        harmonic = feature_rows(feat_ref, F_Y, 9, i)
        for z in range(CZ):
            part = spans(z)
            grad = grad_ref[x, :, part]
            feature = jnp.concatenate(pair_features(harmonic, part, mask) + [atoms], 0)
            back = dims(feature, grad, 1, 1)
            for m in range(9):
                grad_env_ref[m, rows_of(i, z), :] = back[m * PER_CELL : (m + 1) * PER_CELL]
            grad_center_ref[rows_of(i, z), :] = back[9 * PER_CELL :]
            table = jnp.concatenate(
                scaled_env(env_ref, couple_ref, i, z) + [radial, jnp.zeros((8, CH), BF16)], 0
            )
            down = dims(table, grad, 1, 0)
            rows = [down[9 * PER_CELL : 9 * PER_CELL + NBASIS]]
            for m in range(9):
                kept = jnp.where(mask, down[m * PER_CELL : (m + 1) * PER_CELL], 0.0)
                rows.append(jnp.sum(kept, 0, keepdims=True))
            down_ref[i, 0 : NBASIS + 9, part] = jnp.concatenate(rows, 0)

    looped(CX, column, 4)

    @pl.when(y == CY - 1)
    def _():
        invariants = [None] * 3
        for m in range(9):
            value = env_ref[m]
            squared = value * value
            degree = DEGREE[m]
            invariants[degree] = (
                squared if invariants[degree] is None else invariants[degree] + squared
            )
        normed, inverse = normalised(invariants)
        mixed = dims(jnp.concatenate(normed, 1).astype(BF16), mix_ref[...], 1, 0)
        gate = sigmoid_of(mixed)
        act = mixed * gate
        slope_ref[...] = gate + act - act * gate
        for d in range(3):
            normed_ref[d] = normed[d]
        high, low = halves(grad_center_ref[...])
        base_ref[...] = dims(high, center_ref[...], 1, 1) + dims(low, center_ref[...], 1, 1)
        scale = scale_ref[...]
        for m in range(9):
            pull_ref[m] = 2.0 * env_ref[m] * scale * inverse
        pulled = [
            grad_env_ref[m] * couple_ref[DEGREE[m] : DEGREE[m] + 1] * scale for m in range(9)
        ]
        direct_ref[...] = dims_three(
            jnp.concatenate(pulled, 1), radial_blocks(radial_a_ref[...]), 1, 1
        )


def force_kernel(
    neigh_ref,
    base_ref,
    slope_ref,
    normed_ref,
    pull_env_ref,
    direct_ref,
    feat_ref,
    code_ref,
    down_ref,
    raw_ref,
    mix_ref,
    proj_ref,
    radial_ref,
    own_ref,
    ghost_ref,
    moment_ref,
    pull_ref,
):
    neigh = jnp.concatenate([neigh_ref[y, x] for x in range(CX) for y in range(CY)], 0)
    high, low = halves(neigh)
    grad = base_ref[...] + dims(high, proj_ref[...], 1, 1) + dims(low, proj_ref[...], 1, 1)
    grad = grad * slope_ref[...]
    grad = dims(grad.astype(BF16), mix_ref[...], 1, 1)
    grads = [grad[:, d * CH : (d + 1) * CH] for d in range(3)]
    normed = [normed_ref[d] for d in range(3)]
    mean = sum(jnp.sum(g * q, 1, keepdims=True) for g, q in zip(grads, normed)) * (1.0 / (3 * CH))
    grads = [g - q * mean for g, q in zip(grads, normed)]
    pulled = [pull_env_ref[m] * grads[DEGREE[m]] for m in range(9)]
    moment_ref[...] = direct_ref[...] + dims_three(
        jnp.concatenate(pulled, 1), radial_blocks(radial_ref[...]), 1, 1
    )

    _, atoms = atom_blocks()
    row_cells = iota((5 * CELL_ROWS, PAIRS), 0)
    row_slots = iota((PER_CELL, PAIRS), 0)
    ghost_ref[...] = jnp.zeros_like(ghost_ref)
    three, five, fifteen = math.sqrt(3.0), math.sqrt(5.0), math.sqrt(15.0)

    def column(i):
        harmonic = feature_rows(feat_ref, F_Y, 9, i)
        basis = feature_rows(feat_ref, F_B, NBASIS, i)
        slope = feature_rows(feat_ref, F_DB, NBASIS, i)
        weight = feature_rows(feat_ref, F_W, 1, i)
        weight_slope = feature_rows(feat_ref, F_DW, 1, i)
        inverse = feature_rows(feat_ref, F_INV, 1, i)
        parts = []
        for z in range(CZ):
            high, low = halves(moment_ref[rows_of(i, z), :])
            parts.append(dims(high, atoms, 0, 0) + dims(low, atoms, 0, 0))
        back = jnp.concatenate(parts, 1)
        weighted = basis * weight
        grad_weighted = jnp.zeros((NBASIS, PAIRS), F32)
        chain = []
        for m in range(9):
            block = back[m * NBASIS : (m + 1) * NBASIS]
            grad_weighted += block * harmonic[m : m + 1]
            if m:
                chain.append(
                    down_ref[i, NBASIS + m : NBASIS + m + 1, :]
                    + jnp.sum(block * weighted, 0, keepdims=True)
                )
        y1, y2, y3, y4, y5, y6, y7, y8 = chain
        grad_basis = down_ref[i, 0:NBASIS, :] + grad_weighted * weight
        grad_weight = raw_ref[pl.ds(i, 1), :] + jnp.sum(grad_weighted * basis, 0, keepdims=True)
        radial = jnp.sum(grad_basis * slope, 0, keepdims=True) + grad_weight * weight_slope
        nx, ny, nz = (harmonic[c : c + 1] * (1.0 / three) for c in range(1, 4))
        grad_x = three * y1 + fifteen * (ny * y4 + nz * y7 + nx * y8)
        grad_y = three * y2 + fifteen * (nx * y4 + nz * y5 - ny * y8)
        grad_z = three * y3 + fifteen * (ny * y5 + nx * y7) + (3.0 * five) * nz * y6
        along = radial - inverse * (nx * grad_x + ny * grad_y + nz * grad_z)
        pulls = (
            grad_x * inverse + nx * along,
            grad_y * inverse + ny * along,
            grad_z * inverse + nz * along,
        )
        x, y = i // CY, i % CY
        hot = one_hot(row_cells == code_ref[2, pl.ds(i, 1), :])
        mask = row_slots == code_ref[3, pl.ds(i, 1), :]
        for c in range(3):
            pull_ref[c, pl.ds(i, 1), :] = pulls[c]
        kept = jnp.concatenate([jnp.where(mask, pull, 0.0) for pull in pulls], 0)
        found = dims(hot, kept.astype(BF16), 1, 1)
        for dx in range(5):
            start = pl.multiple_of(((x + dx) * 8 + y) * 8, 8)
            ghost_ref[pl.ds(start, CELL_ROWS), :] += found[dx * CELL_ROWS : (dx + 1) * CELL_ROWS]

    looped(COLS, column, 4)

    gather = one_hot(iota((32, PAIRS), 0) == (iota((32, PAIRS), 1) >> 5))
    for c in range(3):
        high, low = halves(pull_ref[c])
        own_ref[c] = dims(high, gather, 1, 1) + dims(low, gather, 1, 1)


def call(kernel, outs, scratch, *args, by_y=(), by_y_out=(), micros=20):
    def spec(shape, moving):
        zeros = (0,) * len(shape)
        if not moving:
            return pl.BlockSpec(shape, lambda y: zeros)
        return pl.BlockSpec((shape[0] // CY,) + shape[1:], lambda y: (y,) + zeros[1:])

    grid = {}
    if by_y or by_y_out:
        grid = dict(
            grid=(CY,),
            in_specs=[spec(a.shape, k in by_y) for k, a in enumerate(args)],
            out_specs=[spec(shape, k in by_y_out) for k, (shape, _) in enumerate(outs)],
        )
    return pl.pallas_call(
        kernel,
        out_shape=[jax.ShapeDtypeStruct(shape, dtype) for shape, dtype in outs],
        scratch_shapes=[pltpu.VMEM(shape, dtype) for shape, dtype in scratch],
        compiler_params=pltpu.CompilerParams(vmem_limit_bytes=32 * 2**20),
        cost_estimate=pl.CostEstimate(
            flops=micros * 10**9, bytes_accessed=micros * 3 * 10**6, transcendentals=0
        ),
        **grid,
    )(*args)


def shifted(block, axis, distance):
    size = lax.axis_size(axis)
    return lax.ppermute(block, axis, [(i, (i + distance) % size) for i in range(size)])


def rims(array, axis, dim):
    length = array.shape[dim]
    before = shifted(lax.slice_in_dim(array, length - 2, length, axis=dim), axis, 1)
    after = shifted(lax.slice_in_dim(array, 0, 2, axis=dim), axis, -1)
    return before, after


def padded(array, axis, dim, tail=0):
    before, after = rims(array, axis, dim)
    parts = [before, array, after]
    if tail:
        parts.append(jnp.zeros(after.shape[:dim] + (tail,) + after.shape[dim + 1 :], array.dtype))
    return jnp.concatenate(parts, axis=dim)


def folded(array, axis, dim, length):
    lower = lax.slice_in_dim(array, 0, 2, axis=dim).astype(BF16)
    upper = lax.slice_in_dim(array, length + 2, length + 4, axis=dim).astype(BF16)
    core = lax.slice_in_dim(array, 2, length + 2, axis=dim).astype(F32)
    to_first = shifted(upper, axis, 1).astype(F32)
    to_last = shifted(lower, axis, -1).astype(F32)
    if length == 2:
        return core + to_first + to_last
    return core + jnp.concatenate([to_first, to_last], axis=dim)


def shards(
    offsets,
    species,
    neighbours,
    counts,
    embed,
    radial_a,
    mix_in,
    proj_center,
    proj_neigh,
    radial_b,
    couple,
    latent_two,
    latent_three,
    readout,
):
    numbers = neighbours.reshape(COLS, PAIRS)
    places = offsets.reshape(CX, CY, CZ, 48)
    around = padded(padded(padded(places, "gx", 0), "gy", 1), "gz", 2, tail=2)
    own = offsets.reshape(COLS, CZ, 3, PER_CELL).transpose(2, 0, 1, 3).reshape(3 * COLS, 32)
    hidden, env, scale, feats, codes = call(
        env_kernel,
        [
            ((CY, CX, 32, CH), BF16),
            ((9, ATOMS, CH), F32),
            ((ATOMS, CH), F32),
            ((LANES * F_COUNT * COLS, 128), F32),
            ((4, COLS, PAIRS), jnp.int32),
        ],
        [((3, COLS, PAIRS), F32), ((ATOMS, 72), F32)],
        numbers,
        around.reshape(512, 48),
        own,
        counts.reshape(COLS, 32),
        species.reshape(1, ATOMS),
        embed,
        radial_a,
        mix_in,
    )
    grid = hidden.reshape(CY, CX, CZ, PER_CELL, CH)
    wide = padded(padded(grid, "gz", 2), "gx", 1)
    low, up = rims(wide, "gy", 0)
    (early,) = call(
        early_kernel,
        [((COLS, CH, PAIRS), F32)],
        [((OWN_RUNS * RUN, 2 * CH), BF16), ((ATOMS, CH), F32)],
        wide.reshape(OWN_RUNS, 2, RUN, CH),
        hidden,
        env,
        feats,
        codes,
        proj_center,
        proj_neigh,
        radial_b,
        couple,
        by_y_out=(0,),
    )
    energy, low_back, up_back, grads, raw = call(
        pair_kernel,
        [
            ((COLS, 32), F32),
            ((RIM_RUNS, 2, RUN, CH), BF16),
            ((RIM_RUNS, 2, RUN, CH), BF16),
            ((COLS, CH, PAIRS), BF16),
            ((COLS, PAIRS), F32),
        ],
        [
            ((2 * RIM_RUNS * RUN, 2 * CH), BF16),
            ((2 * RIM_RUNS * RUN, 2 * CH), F32),
            ((2 * SLAB, PAIRS), BF16),
        ],
        early,
        low.reshape(RIM_RUNS, 2, RUN, CH),
        up.reshape(RIM_RUNS, 2, RUN, CH),
        feats,
        codes,
        proj_neigh,
        latent_two,
        latent_three,
        readout.reshape(1, CH),
        by_y=(0,),
        by_y_out=(3,),
    )
    to_first = shifted(up_back, "gy", 1)
    to_last = shifted(low_back, "gy", -1)
    (ghost,) = call(
        spread_kernel,
        [((OWN_RUNS, 2, RUN, CH), BF16)],
        [((OWN_RUNS * RUN, 2 * CH), F32), ((4 * SLAB, PAIRS), BF16)],
        grads,
        codes,
        by_y=(0,),
    )
    ghost = ghost.astype(F32) + jnp.concatenate([to_first, to_last], 0).astype(F32)
    ghost = ghost.reshape(CY, CX + 4, CZ + 4, PER_CELL, CH)
    owned = folded(folded(ghost, "gx", 1, CX), "gz", 2, CZ)
    down, base, slope, normed, pull, direct = call(
        back_kernel,
        [
            ((COLS, 24, PAIRS), F32),
            ((ATOMS, CH), F32),
            ((ATOMS, CH), F32),
            ((3, ATOMS, CH), F32),
            ((9, ATOMS, CH), F32),
            ((ATOMS, 72), F32),
        ],
        [((9, ATOMS, CH), F32), ((ATOMS, CH), F32)],
        grads,
        env,
        scale,
        feats,
        mix_in,
        proj_center,
        radial_a,
        radial_b,
        couple,
        by_y=(0,),
    )
    own_pull, far_pull = call(
        force_kernel,
        [((3, COLS, 32), F32), ((512, 48), F32)],
        [((ATOMS, 72), F32), ((3, COLS, PAIRS), F32)],
        owned.reshape(CY, CX, 32, CH),
        base,
        slope,
        normed,
        pull,
        direct,
        feats,
        codes,
        down,
        raw,
        mix_in,
        proj_neigh,
        radial_a,
    )
    far = far_pull.reshape(CX + 4, CY + 4, 8, 48)
    far = folded(folded(folded(far, "gx", 0, CX), "gy", 1, CY), "gz", 2, CZ)
    near = own_pull.reshape(3, CX, CY, CZ, PER_CELL).transpose(1, 2, 3, 0, 4)
    forces = near - far.reshape(CX, CY, CZ, 3, PER_CELL)
    return (forces, energy.reshape(CX, CY, CZ, PER_CELL))


def solution(mesh):
    placed = (
        P("gx", "gy", "gz", None, None),
        P("gx", "gy", "gz", None),
        P("gx", "gy", "gz", None, None),
        P("gx", "gy", "gz", None),
    ) + (P(),) * 10
    return jax.shard_map(
        shards,
        mesh=mesh,
        in_specs=placed,
        out_specs=(P("gx", "gy", "gz", None, None), P("gx", "gy", "gz", None)),
        check_vma=False,
    )
```

```python
import math

import jax
import jax.numpy as jnp
from jax import lax
from jax.experimental import pallas as pl
from jax.experimental.pallas import tpu as pltpu
from jax.sharding import PartitionSpec as P

CX = 4
CY = 4
CZ = 2
PER_CELL = 16
SLOTS = 32
CH = 128
NBASIS = 8
SPECIES = 4

CELL_SIDE = 2.0
CUTOFF = 10.5
NORM_EPS = 1e-05

COLS = CX * CY
PAIRS = CZ * PER_CELL * SLOTS
CELL_PAIRS = PER_CELL * SLOTS
ATOMS = COLS * CZ * PER_CELL
RUN = 48
SLAB = 5 * RUN
CELL_ROWS = 40
OWN_RUNS = CY * (CX + 4)
RIM_RUNS = 2 * (CX + 4)
LANES = PAIRS // 128

F32 = jnp.float32
BF16 = jnp.bfloat16
DEGREE = (0, 1, 1, 1, 2, 2, 2, 2, 2)

F_Y = 0
F_W = 9
F_DW = 10
F_B = 11
F_DB = 19
F_INV = 27
F_COUNT = 28

G_B = 0
G_Y = 8
G_E = 17
G_COUNT = 24


def dims(a, b, ca, cb):
    return lax.dot_general(a, b, (((ca,), (cb,)), ((), ())), preferred_element_type=F32)


def halves(value):
    high = value.astype(BF16)
    return high, (value - high.astype(F32)).astype(BF16)


def dims_three(a, b, ca, cb):
    a_high, a_low = halves(a)
    b_high, b_low = halves(b)
    return dims(a_high, b_high, ca, cb) + (
        dims(a_high, b_low, ca, cb) + dims(a_low, b_high, ca, cb)
    )


def iota(shape, dim):
    return lax.broadcasted_iota(jnp.int32, shape, dim)


def one_hot(condition):
    return jnp.where(condition, 1.0, 0.0).astype(BF16)


def hot_rows(count, code):
    rows = iota((count, PAIRS), 0).astype(F32).astype(BF16)
    return jnp.where(
        rows == code.astype(F32).astype(BF16), jnp.ones((), BF16), jnp.zeros((), BF16)
    )


def radial_blocks(radial):
    rows = []
    for m in range(9):
        before = [jnp.zeros((NBASIS, m * CH), F32)] if m else []
        after = [jnp.zeros((NBASIS, (8 - m) * CH), F32)] if m < 8 else []
        rows.append(jnp.concatenate(before + [radial] + after, 1))
    return jnp.concatenate(rows, 0)


def looped(count, body, group):
    def step(j, carry):
        running = [body(j * group + k, k) for k in range(group)]
        while running:
            running = [one for one in running if next(one, True) is None]
        return carry

    lax.fori_loop(0, count // group, step, 0)


def gated(half):
    t = jnp.tanh(half)
    up = t + 1.0
    act = half * up
    return act, up + act * (1.0 - t)


def sigmoid_of(v):
    return 0.5 * jnp.tanh(0.5 * v) + 0.5


def feature_rows(ref, row, count, i):
    blocks = []
    for lane in range(LANES):
        start = (lane * F_COUNT + row) * COLS + i
        blocks.append(ref[pl.ds(start, count, stride=COLS) if count > 1 else pl.ds(start, 1), :])
    return jnp.concatenate(blocks, 1)


def whole_feature(ref, row):
    blocks = []
    for lane in range(LANES):
        start = (lane * F_COUNT + row) * COLS
        blocks.append(ref[start : start + COLS, :])
    return jnp.concatenate(blocks, 1)


def put_feature(ref, row, value):
    for lane in range(LANES):
        start = (lane * F_COUNT + row) * COLS
        ref[start : start + COLS, :] = value[:, lane * 128 : (lane + 1) * 128]


def cell_window(ref, x, y):
    parts = []
    for dx in range(5):
        start = pl.multiple_of(((x + dx) * 8 + y) * 8, 8)
        parts.append(ref[pl.ds(start, CELL_ROWS), :])
    return jnp.concatenate(parts, 0)


def env_kernel(
    nbr_ref,
    ext_ref,
    own_ref,
    count_ref,
    species_ref,
    embed_ref,
    radial_ref,
    mix_ref,
    hidden_ref,
    env_ref,
    scale_ref,
    feat_ref,
    code_ref,
    near_ref,
    moment_ref,
):
    shape = (COLS, PAIRS)
    number = nbr_ref[...]
    slot = number & 15
    cell = number >> 4
    over = (cell * 43691) >> 18
    cell_z = cell - 6 * over
    cell_y = over & 7
    cell_x = over >> 3
    column = iota(shape, 0)
    lane = iota(shape, 1)
    dx = cell_x - (column >> 2)
    dy = cell_y - (column & 3)
    upper = (cell_z >= 3).astype(jnp.int32)
    code_ref[0] = (dy * 5 + dx) * RUN + (cell_z - 3 * upper) * PER_CELL + slot
    code_ref[1] = upper
    code_ref[2] = dx * CELL_ROWS + dy * 8 + cell_z
    code_ref[3] = slot

    row_slots = iota((PER_CELL, PAIRS), 0)

    def fetch(i, k):
        hot = hot_rows(5 * CELL_ROWS, code_ref[2, pl.ds(i, 1), :])
        high, low = halves(cell_window(ext_ref, i // CY, i % CY))
        places = dims(high, hot, 0, 0) + dims(low, hot, 0, 0)
        yield
        mask = row_slots == code_ref[3, pl.ds(i, 1), :]
        for c in range(3):
            part = places[c * PER_CELL : (c + 1) * PER_CELL]
            near_ref[c, pl.ds(i, 1), :] = jnp.sum(jnp.where(mask, part, 0.0), 0, keepdims=True)

    looped(COLS, fetch, 8)

    spread = one_hot(iota((32, PAIRS), 0) == (iota((32, PAIRS), 1) >> 5))
    own_high, own_low = halves(own_ref[...])
    own = dims(own_high, spread, 1, 0) + dims(own_low, spread, 1, 0)
    count = dims(count_ref[...].astype(F32).astype(BF16), spread, 1, 0)
    live = ((lane & 31).astype(F32) < count).astype(F32)
    step_x = (dx - 2).astype(F32) * CELL_SIDE + near_ref[0] - own[0:COLS]
    step_y = (dy - 2).astype(F32) * CELL_SIDE + near_ref[1] - own[COLS : 2 * COLS]
    step_z = (
        (cell_z - 2 - (lane >> 9)).astype(F32) * CELL_SIDE + near_ref[2] - own[2 * COLS : 3 * COLS]
    )
    square = step_x * step_x + step_y * step_y + step_z * step_z
    distance = jnp.sqrt(square)
    inverse = 1.0 / distance
    nx, ny, nz = step_x * inverse, step_y * inverse, step_z * inverse

    def put(row, value):
        put_feature(feat_ref, row, value)

    three, five, fifteen = math.sqrt(3.0), math.sqrt(5.0), math.sqrt(15.0)
    put(F_Y, jnp.ones(shape, F32))
    put(F_Y + 1, three * nx)
    put(F_Y + 2, three * ny)
    put(F_Y + 3, three * nz)
    put(F_Y + 4, fifteen * nx * ny)
    put(F_Y + 5, fifteen * ny * nz)
    put(F_Y + 6, (0.5 * five) * (3.0 * nz * nz - 1.0))
    put(F_Y + 7, fifteen * nx * nz)
    put(F_Y + 8, (0.5 * fifteen) * (nx * nx - ny * ny))
    scaled = distance * (1.0 / CUTOFF)
    inside = 1.0 - scaled * scaled
    put(F_W, live * inside * inside)
    put(F_DW, live * (-4.0 / CUTOFF) * scaled * inside)
    put(F_INV, inverse)
    angle = distance * (math.pi / CUTOFF)
    sine, cosine = jnp.sin(angle), jnp.cos(angle)
    last_s, last_c = jnp.zeros(shape, F32), jnp.ones(shape, F32)
    now_s, now_c = sine, cosine
    for k in range(1, NBASIS + 1):
        basis = CELL_SIDE * now_s * inverse
        put(F_B + k - 1, basis)
        put(F_DB + k - 1, (CELL_SIDE * k * math.pi / CUTOFF * now_c - basis) * inverse)
        last_s, now_s = now_s, 2.0 * cosine * now_s - last_s
        last_c, now_c = now_c, 2.0 * cosine * now_c - last_c

    atoms = one_hot(iota((PER_CELL, CELL_PAIRS), 0) == (iota((PER_CELL, CELL_PAIRS), 1) >> 5))

    def moments(i, k):
        harmonic = feature_rows(feat_ref, F_Y, 9, i)
        weighted = feature_rows(feat_ref, F_B, NBASIS, i) * feature_rows(feat_ref, F_W, 1, i)
        products = jnp.concatenate([harmonic[m : m + 1] * weighted for m in range(9)], 0)
        high, low = halves(products)
        yield
        for z in range(CZ):
            part = slice(z * CELL_PAIRS, (z + 1) * CELL_PAIRS)
            start = pl.multiple_of((i * CZ + z) * PER_CELL, PER_CELL)
            moment_ref[pl.ds(start, PER_CELL), :] = dims(atoms, high[:, part], 1, 1) + dims(
                atoms, low[:, part], 1, 1
            )

    looped(COLS, moments, 8)

    kind = one_hot(iota((SPECIES, ATOMS), 0) == species_ref[...])
    embed_high, embed_low = halves(embed_ref[...] * (1.0 / math.sqrt(SLOTS)))
    scale = dims(kind, embed_high, 0, 0) + dims(kind, embed_low, 0, 0)
    scale_ref[...] = scale
    sums = dims_three(moment_ref[...], radial_blocks(radial_ref[...]), 1, 0)
    invariants = [None] * 3
    for m in range(9):
        value = sums[:, m * CH : (m + 1) * CH] * scale
        env_ref[m] = value
        degree = DEGREE[m]
        squared = value * value
        invariants[degree] = (
            squared if invariants[degree] is None else invariants[degree] + squared
        )
    normed, _ = normalised(invariants)
    mixed = dims(jnp.concatenate(normed, 1).astype(BF16), mix_ref[...], 1, 0)
    hidden = (mixed * sigmoid_of(mixed)).astype(BF16)
    for y in range(CY):
        for x in range(CX):
            hidden_ref[y, x] = hidden[(x * CY + y) * 32 : (x * CY + y + 1) * 32]


def normalised(invariants):
    total = sum(jnp.sum(q * q, 1, keepdims=True) for q in invariants)
    inverse = lax.rsqrt(total * (1.0 / (3 * CH)) + NORM_EPS)
    return [q * inverse for q in invariants], inverse


def spans(z):
    return slice(z * CELL_PAIRS, (z + 1) * CELL_PAIRS)


def rows_of(column, z):
    return pl.ds(pl.multiple_of((column * CZ + z) * PER_CELL, PER_CELL), PER_CELL)


def slab_rows(block, x):
    return pl.ds(pl.multiple_of((block * 8 + x) * RUN, RUN), SLAB)


def fill_table(table_ref, start, around, weights, runs):
    for h in range(2):
        rows = around[:, h].reshape(runs * RUN, CH)
        table_ref[start : start + runs * RUN, h * CH : (h + 1) * CH] = dims(
            rows, weights, 1, 0
        ).astype(BF16) * jnp.asarray(0.5, BF16)


def atom_blocks():
    mask = iota((PER_CELL, CELL_PAIRS), 0) == (iota((PER_CELL, CELL_PAIRS), 1) >> 5)
    return mask, one_hot(mask)


def pair_features(harmonic, part, mask):
    return [jnp.where(mask, harmonic[m : m + 1, part], 0.0).astype(BF16) for m in range(9)]


def scaled_env(env_ref, couple, column, z):
    rows = rows_of(column, z)
    return [
        (env_ref[m, rows, :] * couple[DEGREE[m] : DEGREE[m] + 1]).astype(BF16)
        for m in range(9)
    ]


def early_kernel(
    around_ref,
    hidden_ref,
    env_ref,
    feat_ref,
    code_ref,
    center_ref,
    neigh_ref,
    radial_ref,
    couple_ref,
    early_ref,
    table_ref,
    own_ref,
):
    y = pl.program_id(0)

    @pl.when(y == 0)
    def _():
        fill_table(table_ref, 0, around_ref, neigh_ref[...], OWN_RUNS)
        for yy in range(CY):
            for x in range(CX):
                start = (x * CY + yy) * 32
                own_ref[start : start + 32, :] = dims(
                    hidden_ref[yy, x], center_ref[...], 1, 0
                ) * 0.5

    radial_high, radial_low = halves(radial_ref[...] * 0.5)
    couple = couple_ref[...] * 0.5
    mask, atoms = atom_blocks()

    def column(x, place, first, count, block):
        i = x * CY + y
        harmonic = feature_rows(feat_ref, F_Y, 9, i)
        basis_high, basis_low = halves(feature_rows(feat_ref, F_B, NBASIS, i))
        code = code_ref[0, pl.ds(i, 1), :]
        upper = code_ref[1, pl.ds(i, 1), :] > 0
        parts = []
        for z in range(CZ):
            part = spans(z)
            feature = jnp.concatenate(
                pair_features(harmonic, part, mask)
                + [
                    atoms,
                    atoms,
                    basis_high[:, part],
                    basis_low[:, part],
                    basis_high[:, part],
                    jnp.zeros((8, CELL_PAIRS), BF16),
                ],
                0,
            )
            own_high, own_low = halves(own_ref[rows_of(i, z), :])
            table = jnp.concatenate(
                scaled_env(env_ref, couple, i, z)
                + [
                    own_high,
                    own_low,
                    radial_high,
                    radial_high,
                    radial_low,
                    jnp.zeros((8, CH), BF16),
                ],
                0,
            )
            parts.append(dims(table, feature, 0, 0))
        yield
        fetched = None
        for k in range(count):
            hot = hot_rows(SLAB, code - (first + k) * SLAB)
            found = dims(table_ref[slab_rows(block + k, x), :], hot, 0, 0)
            fetched = found if fetched is None else fetched + found
        yield
        early_ref[x] = jnp.concatenate(parts, 1) + jnp.where(upper, fetched[CH:], fetched[:CH])

    @pl.when((y == 0) | (y == 3))
    def _():
        far = (y == 3).astype(jnp.int32)
        looped(CX, lambda x, k: column(x, k, 2 - 2 * far, 3, far), 4)

    @pl.when((y == 1) | (y == 2))
    def _():
        looped(CX, lambda x, k: column(x, k, 2 - y, 4, 0), 4)


def pair_kernel(
    early_ref,
    low_ref,
    up_ref,
    feat_ref,
    code_ref,
    neigh_ref,
    two_ref,
    three_ref,
    readout_ref,
    energy_ref,
    low_out_ref,
    up_out_ref,
    grad_ref,
    raw_ref,
    table_ref,
    total_ref,
    hot_ref,
):
    y = pl.program_id(0)

    @pl.when(y == 0)
    def _():
        fill_table(table_ref, 0, low_ref, neigh_ref[...], RIM_RUNS)
        fill_table(table_ref, RIM_RUNS * RUN, up_ref, neigh_ref[...], RIM_RUNS)
        total_ref[...] = jnp.zeros_like(total_ref)

    readout = jnp.transpose(jnp.broadcast_to(0.5 * readout_ref[...], (CH, CH)))
    readout = jnp.concatenate([readout] * LANES, 1)
    two_half = two_ref[...] * jnp.asarray(0.5, BF16)
    three_half = three_ref[...] * jnp.asarray(0.5, BF16)

    def column(x, place, first, count, block):
        i = x * CY + y
        weight = feature_rows(feat_ref, F_W, 1, i)
        code = code_ref[0, pl.ds(i, 1), :]
        upper = code_ref[1, pl.ds(i, 1), :] > 0
        fetched = None
        for k in range(count):
            hot = hot_rows(SLAB, code - (first + k) * SLAB)
            hot_ref[place, k * SLAB : (k + 1) * SLAB, :] = hot
            found = dims(table_ref[slab_rows(block + k, x), :], hot, 0, 0)
            fetched = found if fetched is None else fetched + found
        yield
        value = early_ref[x] + jnp.where(upper, fetched[CH:], fetched[:CH])
        one, slope_one = gated(value)
        value = dims(two_half, one.astype(BF16), 0, 0)
        yield
        two, slope_two = gated(value)
        value = dims(three_half, two.astype(BF16), 0, 0)
        yield
        top, slope_top = gated(value)
        raw_ref[pl.ds(i, 1), :] = 2.0 * jnp.sum(top * readout, 0, keepdims=True)
        grad = slope_top * (readout * weight)
        grad = dims(three_half, grad.astype(BF16), 1, 0)
        yield
        grad = dims(two_half, (grad * slope_two).astype(BF16), 1, 0)
        yield
        grad = grad * slope_one
        grad = grad.astype(BF16)
        high = grad * jnp.where(upper, 1.0, 0.0).astype(BF16)
        spread = jnp.concatenate([grad - high, high], 0)
        grad_ref[x] = grad
        found = dims(hot_ref[place, : count * SLAB, :], spread, 1, 1)
        yield
        for k in range(count):
            total_ref[slab_rows(block + k, x), :] += found[k * SLAB : (k + 1) * SLAB]

    @pl.when((y == 0) | (y == 3))
    def _():
        far = (y == 3).astype(jnp.int32)
        looped(CX, lambda x, k: column(x, k, 3 * far, 2, 2 * far), 4)

    @pl.when((y == 1) | (y == 2))
    def _():
        looped(CX, lambda x, k: column(x, k, 4 * (y - 1), 1, y), 4)

    @pl.when(y == CY - 1)
    def _():
        for h in range(2):
            rim = total_ref[:, h * CH : (h + 1) * CH].astype(BF16).reshape(2 * RIM_RUNS, RUN, CH)
            low_out_ref[:, h] = rim[:RIM_RUNS]
            up_out_ref[:, h] = rim[RIM_RUNS:]
        gather = one_hot(iota((32, PAIRS), 0) == (iota((32, PAIRS), 1) >> 5))
        high, low = halves(raw_ref[...] * whole_feature(feat_ref, F_W))
        energy_ref[...] = dims(high, gather, 1, 1) + dims(low, gather, 1, 1)


def spread_kernel(grad_ref, code_ref, ghost_ref, total_ref, hot_ref):
    y = pl.program_id(0)

    @pl.when(y == 0)
    def _():
        total_ref[...] = jnp.zeros_like(total_ref)


    def column(x, place, first, count, block):
        i = x * CY + y
        code = code_ref[0, pl.ds(i, 1), :]
        upper = jnp.where(code_ref[1, pl.ds(i, 1), :] > 0, 1.0, 0.0).astype(BF16)
        for k in range(count):
            hot_ref[place, k * SLAB : (k + 1) * SLAB, :] = hot_rows(
                SLAB, code - (first + k) * SLAB
            )
        grad = grad_ref[x]
        high = grad * upper
        spread = jnp.concatenate([grad - high, high], 0)
        found = dims(hot_ref[place, : count * SLAB, :], spread, 1, 1)
        for k in range(count):
            total_ref[slab_rows(block + k, x), :] += found[k * SLAB : (k + 1) * SLAB]
        yield

    @pl.when((y == 0) | (y == 3))
    def _():
        far = (y == 3).astype(jnp.int32)
        looped(CX, lambda x, k: column(x, k, 2 - 2 * far, 3, far), 4)

    @pl.when((y == 1) | (y == 2))
    def _():
        looped(CX, lambda x, k: column(x, k, 2 - y, 4, 0), 4)

    @pl.when(y == CY - 1)
    def _():
        for h in range(2):
            ghost_ref[:, h] = (
                total_ref[:, h * CH : (h + 1) * CH].astype(BF16).reshape(OWN_RUNS, RUN, CH)
            )


def back_kernel(
    grad_ref,
    env_ref,
    scale_ref,
    feat_ref,
    mix_ref,
    center_ref,
    radial_a_ref,
    radial_ref,
    couple_ref,
    down_ref,
    base_ref,
    slope_ref,
    normed_ref,
    pull_ref,
    direct_ref,
    grad_env_ref,
    grad_center_ref,
):
    y = pl.program_id(0)
    mask, atoms = atom_blocks()
    radial = radial_ref[...].astype(BF16)

    def column(x, k):
        i = x * CY + y
        harmonic = feature_rows(feat_ref, F_Y, 9, i)
        found = []
        for z in range(CZ):
            part = spans(z)
            grad = grad_ref[x, :, part]
            feature = jnp.concatenate(pair_features(harmonic, part, mask) + [atoms], 0)
            back = dims(feature, grad, 1, 1)
            table = jnp.concatenate(
                scaled_env(env_ref, couple_ref, i, z) + [radial, jnp.zeros((8, CH), BF16)], 0
            )
            found.append((back, dims(table, grad, 1, 0)))
        yield
        for z in range(CZ):
            part = spans(z)
            back, down = found[z]
            for m in range(9):
                grad_env_ref[m, rows_of(i, z), :] = back[m * PER_CELL : (m + 1) * PER_CELL]
            grad_center_ref[rows_of(i, z), :] = back[9 * PER_CELL :]
            rows = [down[9 * PER_CELL : 9 * PER_CELL + NBASIS]]
            for m in range(9):
                kept = jnp.where(mask, down[m * PER_CELL : (m + 1) * PER_CELL], 0.0)
                rows.append(jnp.sum(kept, 0, keepdims=True))
            down_ref[i, 0 : NBASIS + 9, part] = jnp.concatenate(rows, 0)

    looped(CX, column, 4)

    @pl.when(y == CY - 1)
    def _():
        invariants = [None] * 3
        for m in range(9):
            value = env_ref[m]
            squared = value * value
            degree = DEGREE[m]
            invariants[degree] = (
                squared if invariants[degree] is None else invariants[degree] + squared
            )
        normed, inverse = normalised(invariants)
        mixed = dims(jnp.concatenate(normed, 1).astype(BF16), mix_ref[...], 1, 0)
        gate = sigmoid_of(mixed)
        act = mixed * gate
        slope_ref[...] = gate + act - act * gate
        for d in range(3):
            normed_ref[d] = normed[d]
        high, low = halves(grad_center_ref[...])
        base_ref[...] = dims(high, center_ref[...], 1, 1) + dims(low, center_ref[...], 1, 1)
        scale = scale_ref[...]
        for m in range(9):
            pull_ref[m] = 2.0 * env_ref[m] * scale * inverse
        pulled = [
            grad_env_ref[m] * couple_ref[DEGREE[m] : DEGREE[m] + 1] * scale for m in range(9)
        ]
        direct_ref[...] = dims(
            jnp.concatenate(pulled, 1).astype(BF16),
            radial_blocks(radial_a_ref[...]).astype(BF16),
            1,
            1,
        )


def force_kernel(
    neigh_ref,
    base_ref,
    slope_ref,
    normed_ref,
    pull_env_ref,
    direct_ref,
    feat_ref,
    code_ref,
    down_ref,
    raw_ref,
    mix_ref,
    proj_ref,
    radial_ref,
    own_ref,
    ghost_ref,
    moment_ref,
    pull_ref,
):
    neigh = jnp.concatenate([neigh_ref[y, x] for x in range(CX) for y in range(CY)], 0)
    grad = base_ref[...] + dims(neigh.astype(BF16), proj_ref[...], 1, 1)
    grad = grad * slope_ref[...]
    grad = dims(grad.astype(BF16), mix_ref[...], 1, 1)
    grads = [grad[:, d * CH : (d + 1) * CH] for d in range(3)]
    normed = [normed_ref[d] for d in range(3)]
    mean = sum(jnp.sum(g * q, 1, keepdims=True) for g, q in zip(grads, normed)) * (1.0 / (3 * CH))
    grads = [g - q * mean for g, q in zip(grads, normed)]
    pulled = [pull_env_ref[m] * grads[DEGREE[m]] for m in range(9)]
    moment_ref[...] = direct_ref[...] + dims(
        jnp.concatenate(pulled, 1).astype(BF16),
        radial_blocks(radial_ref[...]).astype(BF16),
        1,
        1,
    )

    _, atoms = atom_blocks()
    row_slots = iota((PER_CELL, PAIRS), 0)
    ghost_ref[...] = jnp.zeros_like(ghost_ref)
    three, five, fifteen = math.sqrt(3.0), math.sqrt(5.0), math.sqrt(15.0)

    def column(i, k):
        harmonic = feature_rows(feat_ref, F_Y, 9, i)
        basis = feature_rows(feat_ref, F_B, NBASIS, i)
        slope = feature_rows(feat_ref, F_DB, NBASIS, i)
        weight = feature_rows(feat_ref, F_W, 1, i)
        weight_slope = feature_rows(feat_ref, F_DW, 1, i)
        inverse = feature_rows(feat_ref, F_INV, 1, i)
        parts = []
        for z in range(CZ):
            parts.append(dims(moment_ref[rows_of(i, z), :].astype(BF16), atoms, 0, 0))
        back = jnp.concatenate(parts, 1)
        yield
        weighted = basis * weight
        grad_weighted = jnp.zeros((NBASIS, PAIRS), F32)
        chain = []
        for m in range(9):
            block = back[m * NBASIS : (m + 1) * NBASIS]
            grad_weighted += block * harmonic[m : m + 1]
            if m:
                chain.append(
                    down_ref[i, NBASIS + m : NBASIS + m + 1, :]
                    + jnp.sum(block * weighted, 0, keepdims=True)
                )
        y1, y2, y3, y4, y5, y6, y7, y8 = chain
        grad_basis = down_ref[i, 0:NBASIS, :] + grad_weighted * weight
        grad_weight = raw_ref[pl.ds(i, 1), :] + jnp.sum(grad_weighted * basis, 0, keepdims=True)
        radial = jnp.sum(grad_basis * slope, 0, keepdims=True) + grad_weight * weight_slope
        nx, ny, nz = (harmonic[c : c + 1] * (1.0 / three) for c in range(1, 4))
        grad_x = three * y1 + fifteen * (ny * y4 + nz * y7 + nx * y8)
        grad_y = three * y2 + fifteen * (nx * y4 + nz * y5 - ny * y8)
        grad_z = three * y3 + fifteen * (ny * y5 + nx * y7) + (3.0 * five) * nz * y6
        along = radial - inverse * (nx * grad_x + ny * grad_y + nz * grad_z)
        pulls = (
            grad_x * inverse + nx * along,
            grad_y * inverse + ny * along,
            grad_z * inverse + nz * along,
        )
        yield
        x, y = i // CY, i % CY
        hot = hot_rows(5 * CELL_ROWS, code_ref[2, pl.ds(i, 1), :])
        mask = row_slots == code_ref[3, pl.ds(i, 1), :]
        for c in range(3):
            pull_ref[c, pl.ds(i, 1), :] = pulls[c]
        kept = jnp.concatenate([jnp.where(mask, pull, 0.0) for pull in pulls], 0)
        found = dims(hot, kept.astype(BF16), 1, 1)
        yield
        for dx in range(5):
            start = pl.multiple_of(((x + dx) * 8 + y) * 8, 8)
            ghost_ref[pl.ds(start, CELL_ROWS), :] += found[dx * CELL_ROWS : (dx + 1) * CELL_ROWS]

    looped(COLS, column, 8)

    gather = one_hot(iota((32, PAIRS), 0) == (iota((32, PAIRS), 1) >> 5))
    for c in range(3):
        high, low = halves(pull_ref[c])
        own_ref[c] = dims(high, gather, 1, 1) + dims(low, gather, 1, 1)


def call(kernel, outs, scratch, *args, by_y=(), by_y_out=(), micros=20):
    def spec(shape, moving):
        zeros = (0,) * len(shape)
        if not moving:
            return pl.BlockSpec(shape, lambda y: zeros)
        return pl.BlockSpec((shape[0] // CY,) + shape[1:], lambda y: (y,) + zeros[1:])

    grid = {}
    if by_y or by_y_out:
        grid = dict(
            grid=(CY,),
            in_specs=[spec(a.shape, k in by_y) for k, a in enumerate(args)],
            out_specs=[spec(shape, k in by_y_out) for k, (shape, _) in enumerate(outs)],
        )
    return pl.pallas_call(
        kernel,
        out_shape=[jax.ShapeDtypeStruct(shape, dtype) for shape, dtype in outs],
        scratch_shapes=[pltpu.VMEM(shape, dtype) for shape, dtype in scratch],
        compiler_params=pltpu.CompilerParams(vmem_limit_bytes=32 * 2**20),
        cost_estimate=pl.CostEstimate(
            flops=micros * 10**9, bytes_accessed=micros * 3 * 10**6, transcendentals=0
        ),
        **grid,
    )(*args)


def shifted(block, axis, distance):
    size = lax.axis_size(axis)
    return lax.ppermute(block, axis, [(i, (i + distance) % size) for i in range(size)])


def rims(array, axis, dim):
    length = array.shape[dim]
    before = shifted(lax.slice_in_dim(array, length - 2, length, axis=dim), axis, 1)
    after = shifted(lax.slice_in_dim(array, 0, 2, axis=dim), axis, -1)
    return before, after


def padded(array, axis, dim, tail=0, beside=None):
    before, after = rims(array, axis, dim)
    if beside is not None:
        before, beside = lax.optimization_barrier((before, beside))
    parts = [before, array, after]
    if tail:
        parts.append(jnp.zeros(after.shape[:dim] + (tail,) + after.shape[dim + 1 :], array.dtype))
    whole = jnp.concatenate(parts, axis=dim)
    return whole if beside is None else (whole, beside)


def folded(array, axis, dim, length):
    lower = lax.slice_in_dim(array, 0, 2, axis=dim).astype(BF16)
    upper = lax.slice_in_dim(array, length + 2, length + 4, axis=dim).astype(BF16)
    core = lax.slice_in_dim(array, 2, length + 2, axis=dim).astype(F32)
    to_first = shifted(upper, axis, 1).astype(F32)
    to_last = shifted(lower, axis, -1).astype(F32)
    if length == 2:
        return core + to_first + to_last
    return core + jnp.concatenate([to_first, to_last], axis=dim)


def shards(
    offsets,
    species,
    neighbours,
    counts,
    embed,
    radial_a,
    mix_in,
    proj_center,
    proj_neigh,
    radial_b,
    couple,
    latent_two,
    latent_three,
    readout,
):
    places = offsets.reshape(CX, CY, CZ, 48)
    numbers = neighbours.reshape(COLS, PAIRS)
    around, numbers = padded(places, "gx", 0, beside=numbers)
    rows = (counts.reshape(COLS, 32), species.reshape(1, ATOMS))
    around, rows = padded(around, "gy", 1, beside=rows)
    own = offsets.reshape(COLS, CZ, 3, PER_CELL).transpose(2, 0, 1, 3).reshape(3 * COLS, 32)
    around = padded(around, "gz", 2, tail=2)
    hidden, env, scale, feats, codes = call(
        env_kernel,
        [
            ((CY, CX, 32, CH), BF16),
            ((9, ATOMS, CH), F32),
            ((ATOMS, CH), F32),
            ((LANES * F_COUNT * COLS, 128), F32),
            ((4, COLS, PAIRS), jnp.int32),
        ],
        [((3, COLS, PAIRS), F32), ((ATOMS, 72), F32)],
        numbers,
        around.reshape(512, 48),
        own,
        *rows,
        embed,
        radial_a,
        mix_in,
    )
    grid = hidden.reshape(CY, CX, CZ, PER_CELL, CH)
    wide = padded(padded(grid, "gz", 2), "gx", 1)
    low, up = rims(wide, "gy", 0)
    (early,) = call(
        early_kernel,
        [((COLS, CH, PAIRS), F32)],
        [((OWN_RUNS * RUN, 2 * CH), BF16), ((ATOMS, CH), F32)],
        wide.reshape(OWN_RUNS, 2, RUN, CH),
        hidden,
        env,
        feats,
        codes,
        proj_center,
        proj_neigh,
        radial_b,
        couple,
        by_y_out=(0,),
    )
    energy, low_back, up_back, grads, raw = call(
        pair_kernel,
        [
            ((COLS, 32), F32),
            ((RIM_RUNS, 2, RUN, CH), BF16),
            ((RIM_RUNS, 2, RUN, CH), BF16),
            ((COLS, CH, PAIRS), BF16),
            ((COLS, PAIRS), F32),
        ],
        [
            ((2 * RIM_RUNS * RUN, 2 * CH), BF16),
            ((2 * RIM_RUNS * RUN, 2 * CH), F32),
            ((CX, 2 * SLAB, PAIRS), BF16),
        ],
        early,
        low.reshape(RIM_RUNS, 2, RUN, CH),
        up.reshape(RIM_RUNS, 2, RUN, CH),
        feats,
        codes,
        proj_neigh,
        latent_two,
        latent_three,
        readout.reshape(1, CH),
        by_y=(0,),
        by_y_out=(3,),
    )
    to_first = shifted(up_back, "gy", 1)
    to_last = shifted(low_back, "gy", -1)
    (ghost,) = call(
        spread_kernel,
        [((OWN_RUNS, 2, RUN, CH), BF16)],
        [((OWN_RUNS * RUN, 2 * CH), F32), ((CX, 4 * SLAB, PAIRS), BF16)],
        grads,
        codes,
        by_y=(0,),
    )
    ghost = ghost.astype(F32) + jnp.concatenate([to_first, to_last], 0).astype(F32)
    ghost = ghost.reshape(CY, CX + 4, CZ + 4, PER_CELL, CH)
    owned = folded(folded(ghost, "gx", 1, CX), "gz", 2, CZ)
    down, base, slope, normed, pull, direct = call(
        back_kernel,
        [
            ((COLS, 24, PAIRS), F32),
            ((ATOMS, CH), F32),
            ((ATOMS, CH), F32),
            ((3, ATOMS, CH), F32),
            ((9, ATOMS, CH), F32),
            ((ATOMS, 72), F32),
        ],
        [((9, ATOMS, CH), F32), ((ATOMS, CH), F32)],
        grads,
        env,
        scale,
        feats,
        mix_in,
        proj_center,
        radial_a,
        radial_b,
        couple,
        by_y=(0,),
    )
    own_pull, far_pull = call(
        force_kernel,
        [((3, COLS, 32), F32), ((512, 48), F32)],
        [((ATOMS, 72), F32), ((3, COLS, PAIRS), F32)],
        owned.reshape(CY, CX, 32, CH),
        base,
        slope,
        normed,
        pull,
        direct,
        feats,
        codes,
        down,
        raw,
        mix_in,
        proj_neigh,
        radial_a,
    )
    far = far_pull.reshape(CX + 4, CY + 4, 8, 48)
    far = folded(folded(folded(far, "gx", 0, CX), "gy", 1, CY), "gz", 2, CZ)
    near = own_pull.reshape(3, CX, CY, CZ, PER_CELL).transpose(1, 2, 3, 0, 4)
    forces = near - far.reshape(CX, CY, CZ, 3, PER_CELL)
    return (forces, energy.reshape(CX, CY, CZ, PER_CELL))


def solution(mesh):
    placed = (
        P("gx", "gy", "gz", None, None),
        P("gx", "gy", "gz", None),
        P("gx", "gy", "gz", None, None),
        P("gx", "gy", "gz", None),
    ) + (P(),) * 10
    return jax.shard_map(
        shards,
        mesh=mesh,
        in_specs=placed,
        out_specs=(P("gx", "gy", "gz", None, None), P("gx", "gy", "gz", None)),
        check_vma=False,
    )
```

```python
import math

import jax
import jax.numpy as jnp
from jax import lax
from jax.experimental import pallas as pl
from jax.experimental.pallas import tpu as pltpu
from jax.sharding import PartitionSpec as P

CX = 4
CY = 4
CZ = 2
PER_CELL = 16
SLOTS = 32
CH = 128
NBASIS = 8
SPECIES = 4

CELL_SIDE = 2.0
CUTOFF = 10.5
NORM_EPS = 1e-05

COLS = CX * CY
PAIRS = CZ * PER_CELL * SLOTS
CELL_PAIRS = PER_CELL * SLOTS
ATOMS = COLS * CZ * PER_CELL
RUN = 48
SLAB = 5 * RUN
CELL_ROWS = 40
OWN_RUNS = CY * (CX + 4)
RIM_RUNS = 2 * (CX + 4)
LANES = PAIRS // 128

F32 = jnp.float32
BF16 = jnp.bfloat16
DEGREE = (0, 1, 1, 1, 2, 2, 2, 2, 2)

F_Y = 0
F_W = 9
F_DW = 10
F_B = 11
F_DB = 19
F_INV = 27
F_COUNT = 28

G_B = 0
G_Y = 8
G_E = 17
G_COUNT = 24


def dims(a, b, ca, cb):
    return lax.dot_general(a, b, (((ca,), (cb,)), ((), ())), preferred_element_type=F32)


def halves(value):
    high = value.astype(BF16)
    return high, (value - high.astype(F32)).astype(BF16)


def dims_three(a, b, ca, cb):
    a_high, a_low = halves(a)
    b_high, b_low = halves(b)
    return dims(a_high, b_high, ca, cb) + (
        dims(a_high, b_low, ca, cb) + dims(a_low, b_high, ca, cb)
    )


def iota(shape, dim):
    return lax.broadcasted_iota(jnp.int32, shape, dim)


def one_hot(condition):
    return jnp.where(condition, 1.0, 0.0).astype(BF16)


def hot_rows(count, code):
    rows = iota((count, PAIRS), 0).astype(F32).astype(BF16)
    return jnp.where(
        rows == code.astype(F32).astype(BF16), jnp.ones((), BF16), jnp.zeros((), BF16)
    )


def radial_blocks(radial):
    rows = []
    for m in range(9):
        before = [jnp.zeros((NBASIS, m * CH), F32)] if m else []
        after = [jnp.zeros((NBASIS, (8 - m) * CH), F32)] if m < 8 else []
        rows.append(jnp.concatenate(before + [radial] + after, 1))
    return jnp.concatenate(rows, 0)


def looped(count, body, group):
    def step(j, carry):
        running = [body(j * group + k, k) for k in range(group)]
        while running:
            running = [one for one in running if next(one, True) is None]
        return carry

    lax.fori_loop(0, count // group, step, 0)


def gated(half):
    half = half.astype(BF16)
    t = jnp.tanh(half)
    up = t + 1
    act = half * up
    return act, up + act * (1 - t)


def sigmoid_of(v):
    return 0.5 * jnp.tanh(0.5 * v) + 0.5


def feature_rows(ref, row, count, i):
    blocks = []
    for lane in range(LANES):
        start = (lane * F_COUNT + row) * COLS + i
        blocks.append(ref[pl.ds(start, count, stride=COLS) if count > 1 else pl.ds(start, 1), :])
    return jnp.concatenate(blocks, 1)


def whole_feature(ref, row):
    blocks = []
    for lane in range(LANES):
        start = (lane * F_COUNT + row) * COLS
        blocks.append(ref[start : start + COLS, :])
    return jnp.concatenate(blocks, 1)


def put_feature(ref, row, value):
    for lane in range(LANES):
        start = (lane * F_COUNT + row) * COLS
        ref[start : start + COLS, :] = value[:, lane * 128 : (lane + 1) * 128]


def cell_window(ref, x, y):
    parts = []
    for dx in range(5):
        start = pl.multiple_of(((x + dx) * 8 + y) * 8, 8)
        parts.append(ref[pl.ds(start, CELL_ROWS), :])
    return jnp.concatenate(parts, 0)


def env_kernel(
    nbr_ref,
    ext_ref,
    own_ref,
    count_ref,
    species_ref,
    embed_ref,
    radial_ref,
    mix_ref,
    hidden_ref,
    env_ref,
    scale_ref,
    feat_ref,
    code_ref,
    near_ref,
    moment_ref,
):
    shape = (COLS, PAIRS)
    number = nbr_ref[...]
    slot = number & 15
    cell = number >> 4
    over = (cell * 43691) >> 18
    cell_z = cell - 6 * over
    cell_y = over & 7
    cell_x = over >> 3
    column = iota(shape, 0)
    lane = iota(shape, 1)
    dx = cell_x - (column >> 2)
    dy = cell_y - (column & 3)
    upper = (cell_z >= 3).astype(jnp.int32)
    code_ref[0] = (dy * 5 + dx) * RUN + (cell_z - 3 * upper) * PER_CELL + slot
    code_ref[1] = upper
    code_ref[2] = dx * CELL_ROWS + dy * 8 + cell_z
    code_ref[3] = slot

    row_slots = iota((PER_CELL, PAIRS), 0)

    def fetch(i, k):
        hot = hot_rows(5 * CELL_ROWS, code_ref[2, pl.ds(i, 1), :])
        high, low = halves(cell_window(ext_ref, i // CY, i % CY))
        places = dims(high, hot, 0, 0) + dims(low, hot, 0, 0)
        yield
        mask = row_slots == code_ref[3, pl.ds(i, 1), :]
        for c in range(3):
            part = places[c * PER_CELL : (c + 1) * PER_CELL]
            near_ref[c, pl.ds(i, 1), :] = jnp.sum(jnp.where(mask, part, 0.0), 0, keepdims=True)

    looped(COLS, fetch, 8)

    spread = one_hot(iota((32, PAIRS), 0) == (iota((32, PAIRS), 1) >> 5))
    own_high, own_low = halves(own_ref[...])
    own = dims(own_high, spread, 1, 0) + dims(own_low, spread, 1, 0)
    count = dims(count_ref[...].astype(F32).astype(BF16), spread, 1, 0)
    live = ((lane & 31).astype(F32) < count).astype(F32)
    step_x = (dx - 2).astype(F32) * CELL_SIDE + near_ref[0] - own[0:COLS]
    step_y = (dy - 2).astype(F32) * CELL_SIDE + near_ref[1] - own[COLS : 2 * COLS]
    step_z = (
        (cell_z - 2 - (lane >> 9)).astype(F32) * CELL_SIDE + near_ref[2] - own[2 * COLS : 3 * COLS]
    )
    square = step_x * step_x + step_y * step_y + step_z * step_z
    distance = jnp.sqrt(square)
    inverse = 1.0 / distance
    nx, ny, nz = step_x * inverse, step_y * inverse, step_z * inverse

    def put(row, value):
        put_feature(feat_ref, row, value)

    three, five, fifteen = math.sqrt(3.0), math.sqrt(5.0), math.sqrt(15.0)
    put(F_Y, jnp.ones(shape, F32))
    put(F_Y + 1, three * nx)
    put(F_Y + 2, three * ny)
    put(F_Y + 3, three * nz)
    put(F_Y + 4, fifteen * nx * ny)
    put(F_Y + 5, fifteen * ny * nz)
    put(F_Y + 6, (0.5 * five) * (3.0 * nz * nz - 1.0))
    put(F_Y + 7, fifteen * nx * nz)
    put(F_Y + 8, (0.5 * fifteen) * (nx * nx - ny * ny))
    scaled = distance * (1.0 / CUTOFF)
    inside = 1.0 - scaled * scaled
    put(F_W, live * inside * inside)
    put(F_DW, live * (-4.0 / CUTOFF) * scaled * inside)
    put(F_INV, inverse)
    angle = distance * (math.pi / CUTOFF)
    sine, cosine = jnp.sin(angle), jnp.cos(angle)
    last_s, last_c = jnp.zeros(shape, F32), jnp.ones(shape, F32)
    now_s, now_c = sine, cosine
    for k in range(1, NBASIS + 1):
        basis = CELL_SIDE * now_s * inverse
        put(F_B + k - 1, basis)
        put(F_DB + k - 1, (CELL_SIDE * k * math.pi / CUTOFF * now_c - basis) * inverse)
        last_s, now_s = now_s, 2.0 * cosine * now_s - last_s
        last_c, now_c = now_c, 2.0 * cosine * now_c - last_c

    atoms = one_hot(iota((PER_CELL, CELL_PAIRS), 0) == (iota((PER_CELL, CELL_PAIRS), 1) >> 5))

    def moments(i, k):
        harmonic = feature_rows(feat_ref, F_Y, 9, i)
        weighted = feature_rows(feat_ref, F_B, NBASIS, i) * feature_rows(feat_ref, F_W, 1, i)
        products = jnp.concatenate([harmonic[m : m + 1] * weighted for m in range(9)], 0)
        high, low = halves(products)
        yield
        for z in range(CZ):
            part = slice(z * CELL_PAIRS, (z + 1) * CELL_PAIRS)
            start = pl.multiple_of((i * CZ + z) * PER_CELL, PER_CELL)
            moment_ref[pl.ds(start, PER_CELL), :] = dims(atoms, high[:, part], 1, 1) + dims(
                atoms, low[:, part], 1, 1
            )

    looped(COLS, moments, 8)

    kind = one_hot(iota((SPECIES, ATOMS), 0) == species_ref[...])
    embed_high, embed_low = halves(embed_ref[...] * (1.0 / math.sqrt(SLOTS)))
    scale = dims(kind, embed_high, 0, 0) + dims(kind, embed_low, 0, 0)
    scale_ref[...] = scale
    sums = dims_three(moment_ref[...], radial_blocks(radial_ref[...]), 1, 0)
    invariants = [None] * 3
    for m in range(9):
        value = sums[:, m * CH : (m + 1) * CH] * scale
        env_ref[m] = value
        degree = DEGREE[m]
        squared = value * value
        invariants[degree] = (
            squared if invariants[degree] is None else invariants[degree] + squared
        )
    normed, _ = normalised(invariants)
    mixed = dims(jnp.concatenate(normed, 1).astype(BF16), mix_ref[...], 1, 0)
    hidden = (mixed * sigmoid_of(mixed)).astype(BF16)
    for y in range(CY):
        for x in range(CX):
            hidden_ref[y, x] = hidden[(x * CY + y) * 32 : (x * CY + y + 1) * 32]


def normalised(invariants):
    total = sum(jnp.sum(q * q, 1, keepdims=True) for q in invariants)
    inverse = lax.rsqrt(total * (1.0 / (3 * CH)) + NORM_EPS)
    return [q * inverse for q in invariants], inverse


def spans(z):
    return slice(z * CELL_PAIRS, (z + 1) * CELL_PAIRS)


def rows_of(column, z):
    return pl.ds(pl.multiple_of((column * CZ + z) * PER_CELL, PER_CELL), PER_CELL)


def slab_rows(block, x):
    return pl.ds(pl.multiple_of((block * 8 + x) * RUN, RUN), SLAB)


def fill_table(table_ref, start, around, weights, runs):
    for h in range(2):
        rows = around[:, h].reshape(runs * RUN, CH)
        table_ref[start : start + runs * RUN, h * CH : (h + 1) * CH] = dims(
            rows, weights, 1, 0
        ).astype(BF16) * jnp.asarray(0.5, BF16)


def atom_blocks():
    mask = iota((PER_CELL, CELL_PAIRS), 0) == (iota((PER_CELL, CELL_PAIRS), 1) >> 5)
    return mask, one_hot(mask)


def pair_features(harmonic, part, mask):
    return [jnp.where(mask, harmonic[m : m + 1, part], 0.0).astype(BF16) for m in range(9)]


def scaled_env(env_ref, couple, column, z):
    rows = rows_of(column, z)
    return [
        (env_ref[m, rows, :] * couple[DEGREE[m] : DEGREE[m] + 1]).astype(BF16)
        for m in range(9)
    ]


def early_kernel(
    around_ref,
    hidden_ref,
    env_ref,
    feat_ref,
    code_ref,
    center_ref,
    neigh_ref,
    radial_ref,
    couple_ref,
    early_ref,
    table_ref,
    own_ref,
):
    y = pl.program_id(0)

    @pl.when(y == 0)
    def _():
        fill_table(table_ref, 0, around_ref, neigh_ref[...], OWN_RUNS)
        for yy in range(CY):
            for x in range(CX):
                start = (x * CY + yy) * 32
                own_ref[start : start + 32, :] = dims(
                    hidden_ref[yy, x], center_ref[...], 1, 0
                ) * 0.5

    radial_high, radial_low = halves(radial_ref[...] * 0.5)
    couple = couple_ref[...] * 0.5
    mask, atoms = atom_blocks()

    def column(x, place, first, count, block):
        i = x * CY + y
        harmonic = feature_rows(feat_ref, F_Y, 9, i)
        basis_high, basis_low = halves(feature_rows(feat_ref, F_B, NBASIS, i))
        code = code_ref[0, pl.ds(i, 1), :]
        upper = code_ref[1, pl.ds(i, 1), :] > 0
        parts = []
        for z in range(CZ):
            part = spans(z)
            feature = jnp.concatenate(
                pair_features(harmonic, part, mask)
                + [
                    atoms,
                    atoms,
                    basis_high[:, part],
                    basis_low[:, part],
                    basis_high[:, part],
                    jnp.zeros((8, CELL_PAIRS), BF16),
                ],
                0,
            )
            own_high, own_low = halves(own_ref[rows_of(i, z), :])
            table = jnp.concatenate(
                scaled_env(env_ref, couple, i, z)
                + [
                    own_high,
                    own_low,
                    radial_high,
                    radial_high,
                    radial_low,
                    jnp.zeros((8, CH), BF16),
                ],
                0,
            )
            parts.append(dims(table, feature, 0, 0))
        yield
        fetched = None
        for k in range(count):
            hot = hot_rows(SLAB, code - (first + k) * SLAB)
            found = dims(table_ref[slab_rows(block + k, x), :], hot, 0, 0)
            fetched = found if fetched is None else fetched + found
        yield
        early_ref[x] = jnp.concatenate(parts, 1) + jnp.where(upper, fetched[CH:], fetched[:CH])

    @pl.when((y == 0) | (y == 3))
    def _():
        far = (y == 3).astype(jnp.int32)
        looped(CX, lambda x, k: column(x, k, 2 - 2 * far, 3, far), 4)

    @pl.when((y == 1) | (y == 2))
    def _():
        looped(CX, lambda x, k: column(x, k, 2 - y, 4, 0), 4)


def pair_kernel(
    early_ref,
    low_ref,
    up_ref,
    feat_ref,
    code_ref,
    neigh_ref,
    two_ref,
    three_ref,
    readout_ref,
    energy_ref,
    low_out_ref,
    up_out_ref,
    grad_ref,
    raw_ref,
    table_ref,
    total_ref,
    hot_ref,
):
    y = pl.program_id(0)

    @pl.when(y == 0)
    def _():
        fill_table(table_ref, 0, low_ref, neigh_ref[...], RIM_RUNS)
        fill_table(table_ref, RIM_RUNS * RUN, up_ref, neigh_ref[...], RIM_RUNS)
        total_ref[...] = jnp.zeros_like(total_ref)

    readout = jnp.transpose(jnp.broadcast_to(0.5 * readout_ref[...], (CH, CH)))
    readout = jnp.concatenate([readout] * LANES, 1)
    two_half = two_ref[...] * jnp.asarray(0.5, BF16)
    three_half = three_ref[...] * jnp.asarray(0.5, BF16)

    def column(x, place, first, count, block):
        i = x * CY + y
        weight = feature_rows(feat_ref, F_W, 1, i)
        code = code_ref[0, pl.ds(i, 1), :]
        upper = code_ref[1, pl.ds(i, 1), :] > 0
        fetched = None
        for k in range(count):
            hot = hot_rows(SLAB, code - (first + k) * SLAB)
            hot_ref[place, k * SLAB : (k + 1) * SLAB, :] = hot
            found = dims(table_ref[slab_rows(block + k, x), :], hot, 0, 0)
            fetched = found if fetched is None else fetched + found
        yield
        value = early_ref[x] + jnp.where(upper, fetched[CH:], fetched[:CH])
        one, slope_one = gated(value)
        value = dims(two_half, one, 0, 0)
        yield
        two, slope_two = gated(value)
        value = dims(three_half, two, 0, 0)
        yield
        top, slope_top = gated(value)
        raw_ref[pl.ds(i, 1), :] = 2.0 * jnp.sum(top.astype(F32) * readout, 0, keepdims=True)
        grad = slope_top * (readout * weight).astype(BF16)
        grad = dims(three_half, grad, 1, 0)
        yield
        grad = dims(two_half, grad.astype(BF16) * slope_two, 1, 0)
        yield
        grad = grad.astype(BF16) * slope_one
        high = grad * jnp.where(upper, 1.0, 0.0).astype(BF16)
        spread = jnp.concatenate([grad - high, high], 0)
        grad_ref[x] = grad
        found = dims(hot_ref[place, : count * SLAB, :], spread, 1, 1)
        yield
        for k in range(count):
            total_ref[slab_rows(block + k, x), :] += found[k * SLAB : (k + 1) * SLAB]

    @pl.when((y == 0) | (y == 3))
    def _():
        far = (y == 3).astype(jnp.int32)
        looped(CX, lambda x, k: column(x, k, 3 * far, 2, 2 * far), 4)

    @pl.when((y == 1) | (y == 2))
    def _():
        looped(CX, lambda x, k: column(x, k, 4 * (y - 1), 1, y), 4)

    @pl.when(y == CY - 1)
    def _():
        for h in range(2):
            rim = total_ref[:, h * CH : (h + 1) * CH].astype(BF16).reshape(2 * RIM_RUNS, RUN, CH)
            low_out_ref[:, h] = rim[:RIM_RUNS]
            up_out_ref[:, h] = rim[RIM_RUNS:]
        gather = one_hot(iota((32, PAIRS), 0) == (iota((32, PAIRS), 1) >> 5))
        high, low = halves(raw_ref[...] * whole_feature(feat_ref, F_W))
        energy_ref[...] = dims(high, gather, 1, 1) + dims(low, gather, 1, 1)


def spread_kernel(grad_ref, code_ref, ghost_ref, total_ref, hot_ref):
    y = pl.program_id(0)

    @pl.when(y == 0)
    def _():
        total_ref[...] = jnp.zeros_like(total_ref)


    def column(x, place, first, count, block):
        i = x * CY + y
        code = code_ref[0, pl.ds(i, 1), :]
        upper = jnp.where(code_ref[1, pl.ds(i, 1), :] > 0, 1.0, 0.0).astype(BF16)
        for k in range(count):
            hot_ref[place, k * SLAB : (k + 1) * SLAB, :] = hot_rows(
                SLAB, code - (first + k) * SLAB
            )
        grad = grad_ref[x]
        high = grad * upper
        spread = jnp.concatenate([grad - high, high], 0)
        found = dims(hot_ref[place, : count * SLAB, :], spread, 1, 1)
        for k in range(count):
            total_ref[slab_rows(block + k, x), :] += found[k * SLAB : (k + 1) * SLAB]
        yield

    @pl.when((y == 0) | (y == 3))
    def _():
        far = (y == 3).astype(jnp.int32)
        looped(CX, lambda x, k: column(x, k, 2 - 2 * far, 3, far), 4)

    @pl.when((y == 1) | (y == 2))
    def _():
        looped(CX, lambda x, k: column(x, k, 2 - y, 4, 0), 4)

    @pl.when(y == CY - 1)
    def _():
        for h in range(2):
            ghost_ref[:, h] = (
                total_ref[:, h * CH : (h + 1) * CH].astype(BF16).reshape(OWN_RUNS, RUN, CH)
            )


def back_kernel(
    grad_ref,
    env_ref,
    scale_ref,
    feat_ref,
    mix_ref,
    center_ref,
    radial_a_ref,
    radial_ref,
    couple_ref,
    down_ref,
    base_ref,
    slope_ref,
    normed_ref,
    pull_ref,
    direct_ref,
    grad_env_ref,
    grad_center_ref,
):
    y = pl.program_id(0)
    mask, atoms = atom_blocks()
    radial = radial_ref[...].astype(BF16)

    def column(x, k):
        i = x * CY + y
        harmonic = feature_rows(feat_ref, F_Y, 9, i)
        found = []
        for z in range(CZ):
            part = spans(z)
            grad = grad_ref[x, :, part]
            feature = jnp.concatenate(pair_features(harmonic, part, mask) + [atoms], 0)
            back = dims(feature, grad, 1, 1)
            table = jnp.concatenate(
                scaled_env(env_ref, couple_ref, i, z) + [radial, jnp.zeros((8, CH), BF16)], 0
            )
            found.append((back, dims(table, grad, 1, 0)))
        yield
        for z in range(CZ):
            part = spans(z)
            back, down = found[z]
            for m in range(9):
                grad_env_ref[m, rows_of(i, z), :] = back[m * PER_CELL : (m + 1) * PER_CELL]
            grad_center_ref[rows_of(i, z), :] = back[9 * PER_CELL :]
            rows = [down[9 * PER_CELL : 9 * PER_CELL + NBASIS]]
            for m in range(9):
                kept = jnp.where(mask, down[m * PER_CELL : (m + 1) * PER_CELL], 0.0)
                rows.append(jnp.sum(kept, 0, keepdims=True))
            down_ref[i, 0 : NBASIS + 9, part] = jnp.concatenate(rows, 0)

    looped(CX, column, 4)

    @pl.when(y == CY - 1)
    def _():
        invariants = [None] * 3
        for m in range(9):
            value = env_ref[m]
            squared = value * value
            degree = DEGREE[m]
            invariants[degree] = (
                squared if invariants[degree] is None else invariants[degree] + squared
            )
        normed, inverse = normalised(invariants)
        mixed = dims(jnp.concatenate(normed, 1).astype(BF16), mix_ref[...], 1, 0)
        gate = sigmoid_of(mixed)
        act = mixed * gate
        slope_ref[...] = gate + act - act * gate
        for d in range(3):
            normed_ref[d] = normed[d]
        high, low = halves(grad_center_ref[...])
        base_ref[...] = dims(high, center_ref[...], 1, 1) + dims(low, center_ref[...], 1, 1)
        scale = scale_ref[...]
        for m in range(9):
            pull_ref[m] = 2.0 * env_ref[m] * scale * inverse
        pulled = [
            grad_env_ref[m] * couple_ref[DEGREE[m] : DEGREE[m] + 1] * scale for m in range(9)
        ]
        direct_ref[...] = dims(
            jnp.concatenate(pulled, 1).astype(BF16),
            radial_blocks(radial_a_ref[...]).astype(BF16),
            1,
            1,
        )


def force_kernel(
    neigh_ref,
    base_ref,
    slope_ref,
    normed_ref,
    pull_env_ref,
    direct_ref,
    feat_ref,
    code_ref,
    down_ref,
    raw_ref,
    mix_ref,
    proj_ref,
    radial_ref,
    low_out_ref,
    core_ref,
    up_out_ref,
    moment_ref,
    ghost_ref,
):
    neigh = jnp.concatenate([neigh_ref[y, x] for x in range(CX) for y in range(CY)], 0)
    grad = base_ref[...] + dims(neigh.astype(BF16), proj_ref[...], 1, 1)
    grad = grad * slope_ref[...]
    grad = dims(grad.astype(BF16), mix_ref[...], 1, 1)
    grads = [grad[:, d * CH : (d + 1) * CH] for d in range(3)]
    normed = [normed_ref[d] for d in range(3)]
    mean = sum(jnp.sum(g * q, 1, keepdims=True) for g, q in zip(grads, normed)) * (1.0 / (3 * CH))
    grads = [g - q * mean for g, q in zip(grads, normed)]
    pulled = [pull_env_ref[m] * grads[DEGREE[m]] for m in range(9)]
    moment_ref[...] = direct_ref[...] + dims(
        jnp.concatenate(pulled, 1).astype(BF16),
        radial_blocks(radial_ref[...]).astype(BF16),
        1,
        1,
    )

    _, atoms = atom_blocks()
    row_slots = iota((PER_CELL, PAIRS), 0)
    own_slots = row_slots == ((iota((PER_CELL, PAIRS), 1) & (CELL_PAIRS - 1)) >> 5)
    own_cells = one_hot(iota((8, PAIRS), 0) == 2 + (iota((8, PAIRS), 1) >> 9))
    ghost_ref[...] = jnp.zeros_like(ghost_ref)
    three, five, fifteen = math.sqrt(3.0), math.sqrt(5.0), math.sqrt(15.0)

    def column(i, k):
        harmonic = feature_rows(feat_ref, F_Y, 9, i)
        basis = feature_rows(feat_ref, F_B, NBASIS, i)
        slope = feature_rows(feat_ref, F_DB, NBASIS, i)
        weight = feature_rows(feat_ref, F_W, 1, i)
        weight_slope = feature_rows(feat_ref, F_DW, 1, i)
        inverse = feature_rows(feat_ref, F_INV, 1, i)
        parts = []
        for z in range(CZ):
            parts.append(dims(moment_ref[rows_of(i, z), :].astype(BF16), atoms, 0, 0))
        back = jnp.concatenate(parts, 1)
        yield
        weighted = basis * weight
        grad_weighted = jnp.zeros((NBASIS, PAIRS), F32)
        chain = []
        for m in range(9):
            block = back[m * NBASIS : (m + 1) * NBASIS]
            grad_weighted += block * harmonic[m : m + 1]
            if m:
                chain.append(
                    down_ref[i, NBASIS + m : NBASIS + m + 1, :]
                    + jnp.sum(block * weighted, 0, keepdims=True)
                )
        y1, y2, y3, y4, y5, y6, y7, y8 = chain
        grad_basis = down_ref[i, 0:NBASIS, :] + grad_weighted * weight
        grad_weight = raw_ref[pl.ds(i, 1), :] + jnp.sum(grad_weighted * basis, 0, keepdims=True)
        radial = jnp.sum(grad_basis * slope, 0, keepdims=True) + grad_weight * weight_slope
        nx, ny, nz = (harmonic[c : c + 1] * (1.0 / three) for c in range(1, 4))
        grad_x = three * y1 + fifteen * (ny * y4 + nz * y7 + nx * y8)
        grad_y = three * y2 + fifteen * (nx * y4 + nz * y5 - ny * y8)
        grad_z = three * y3 + fifteen * (ny * y5 + nx * y7) + (3.0 * five) * nz * y6
        along = radial - inverse * (nx * grad_x + ny * grad_y + nz * grad_z)
        pulls = (
            grad_x * inverse + nx * along,
            grad_y * inverse + ny * along,
            grad_z * inverse + nz * along,
        )
        yield
        x, y = i // CY, i % CY
        hot = hot_rows(5 * CELL_ROWS, code_ref[2, pl.ds(i, 1), :])
        mask = row_slots == code_ref[3, pl.ds(i, 1), :]
        owned = jnp.concatenate([jnp.where(own_slots, pull, 0.0) for pull in pulls], 0)
        own_found = dims(own_cells, owned.astype(BF16), 1, 1)
        kept = jnp.concatenate([jnp.where(mask, pull, 0.0) for pull in pulls], 0)
        found = dims(hot, kept.astype(BF16), 1, 1)
        yield
        for dx in range(5):
            start = pl.multiple_of(((x + dx) * 8 + y) * 8, 8)
            ghost_ref[pl.ds(start, CELL_ROWS), :] -= found[dx * CELL_ROWS : (dx + 1) * CELL_ROWS]
        start = pl.multiple_of(((x + 2) * 8 + y + 2) * 8, 8)
        ghost_ref[pl.ds(start, 8), :] += own_found

    looped(COLS, column, 8)

    low_out_ref[...] = ghost_ref[:128].astype(BF16)
    core_ref[...] = ghost_ref[128:384]
    up_out_ref[...] = ghost_ref[384:].astype(BF16)


def call(kernel, outs, scratch, *args, by_y=(), by_y_out=(), micros=20):
    def spec(shape, moving):
        zeros = (0,) * len(shape)
        if not moving:
            return pl.BlockSpec(shape, lambda y: zeros)
        return pl.BlockSpec((shape[0] // CY,) + shape[1:], lambda y: (y,) + zeros[1:])

    grid = {}
    if by_y or by_y_out:
        grid = dict(
            grid=(CY,),
            in_specs=[spec(a.shape, k in by_y) for k, a in enumerate(args)],
            out_specs=[spec(shape, k in by_y_out) for k, (shape, _) in enumerate(outs)],
        )
    return pl.pallas_call(
        kernel,
        out_shape=[jax.ShapeDtypeStruct(shape, dtype) for shape, dtype in outs],
        scratch_shapes=[pltpu.VMEM(shape, dtype) for shape, dtype in scratch],
        compiler_params=pltpu.CompilerParams(vmem_limit_bytes=32 * 2**20),
        cost_estimate=pl.CostEstimate(
            flops=micros * 10**9, bytes_accessed=micros * 3 * 10**6, transcendentals=0
        ),
        **grid,
    )(*args)


def shifted(block, axis, distance):
    size = lax.axis_size(axis)
    return lax.ppermute(block, axis, [(i, (i + distance) % size) for i in range(size)])


def rims(array, axis, dim):
    length = array.shape[dim]
    before = shifted(lax.slice_in_dim(array, length - 2, length, axis=dim), axis, 1)
    after = shifted(lax.slice_in_dim(array, 0, 2, axis=dim), axis, -1)
    return before, after


def padded(array, axis, dim, tail=0, beside=None):
    before, after = rims(array, axis, dim)
    if beside is not None:
        before, beside = lax.optimization_barrier((before, beside))
    parts = [before, array, after]
    if tail:
        parts.append(jnp.zeros(after.shape[:dim] + (tail,) + after.shape[dim + 1 :], array.dtype))
    whole = jnp.concatenate(parts, axis=dim)
    return whole if beside is None else (whole, beside)


def folded(array, axis, dim, length):
    lower = lax.slice_in_dim(array, 0, 2, axis=dim).astype(BF16)
    upper = lax.slice_in_dim(array, length + 2, length + 4, axis=dim).astype(BF16)
    core = lax.slice_in_dim(array, 2, length + 2, axis=dim).astype(F32)
    to_first = shifted(upper, axis, 1).astype(F32)
    to_last = shifted(lower, axis, -1).astype(F32)
    if length == 2:
        return core + to_first + to_last
    return core + jnp.concatenate([to_first, to_last], axis=dim)


def shards(
    offsets,
    species,
    neighbours,
    counts,
    embed,
    radial_a,
    mix_in,
    proj_center,
    proj_neigh,
    radial_b,
    couple,
    latent_two,
    latent_three,
    readout,
):
    places = offsets.reshape(CX, CY, CZ, 48)
    numbers = neighbours.reshape(COLS, PAIRS)
    around, numbers = padded(places, "gx", 0, beside=numbers)
    rows = (counts.reshape(COLS, 32), species.reshape(1, ATOMS))
    around, rows = padded(around, "gy", 1, beside=rows)
    own = offsets.reshape(COLS, CZ, 3, PER_CELL).transpose(2, 0, 1, 3).reshape(3 * COLS, 32)
    around = padded(around, "gz", 2, tail=2)
    hidden, env, scale, feats, codes = call(
        env_kernel,
        [
            ((CY, CX, 32, CH), BF16),
            ((9, ATOMS, CH), F32),
            ((ATOMS, CH), F32),
            ((LANES * F_COUNT * COLS, 128), F32),
            ((4, COLS, PAIRS), jnp.int32),
        ],
        [((3, COLS, PAIRS), F32), ((ATOMS, 72), F32)],
        numbers,
        around.reshape(512, 48),
        own,
        *rows,
        embed,
        radial_a,
        mix_in,
    )
    grid = hidden.reshape(CY, CX, CZ, PER_CELL, CH)
    wide = padded(padded(grid, "gz", 2), "gx", 1)
    low, up = rims(wide, "gy", 0)
    (early,) = call(
        early_kernel,
        [((COLS, CH, PAIRS), F32)],
        [((OWN_RUNS * RUN, 2 * CH), BF16), ((ATOMS, CH), F32)],
        wide.reshape(OWN_RUNS, 2, RUN, CH),
        hidden,
        env,
        feats,
        codes,
        proj_center,
        proj_neigh,
        radial_b,
        couple,
        by_y_out=(0,),
    )
    energy, low_back, up_back, grads, raw = call(
        pair_kernel,
        [
            ((COLS, 32), F32),
            ((RIM_RUNS, 2, RUN, CH), BF16),
            ((RIM_RUNS, 2, RUN, CH), BF16),
            ((COLS, CH, PAIRS), BF16),
            ((COLS, PAIRS), F32),
        ],
        [
            ((2 * RIM_RUNS * RUN, 2 * CH), BF16),
            ((2 * RIM_RUNS * RUN, 2 * CH), F32),
            ((CX, 2 * SLAB, PAIRS), BF16),
        ],
        early,
        low.reshape(RIM_RUNS, 2, RUN, CH),
        up.reshape(RIM_RUNS, 2, RUN, CH),
        feats,
        codes,
        proj_neigh,
        latent_two,
        latent_three,
        readout.reshape(1, CH),
        by_y=(0,),
        by_y_out=(3,),
    )
    to_first = shifted(up_back, "gy", 1)
    to_last = shifted(low_back, "gy", -1)
    (ghost,) = call(
        spread_kernel,
        [((OWN_RUNS, 2, RUN, CH), BF16)],
        [((OWN_RUNS * RUN, 2 * CH), F32), ((CX, 4 * SLAB, PAIRS), BF16)],
        grads,
        codes,
        by_y=(0,),
    )
    ghost = ghost.astype(F32) + jnp.concatenate([to_first, to_last], 0).astype(F32)
    ghost = ghost.reshape(CY, CX + 4, CZ + 4, PER_CELL, CH)
    owned = folded(folded(ghost, "gx", 1, CX), "gz", 2, CZ)
    down, base, slope, normed, pull, direct = call(
        back_kernel,
        [
            ((COLS, 24, PAIRS), F32),
            ((ATOMS, CH), F32),
            ((ATOMS, CH), F32),
            ((3, ATOMS, CH), F32),
            ((9, ATOMS, CH), F32),
            ((ATOMS, 72), F32),
        ],
        [((9, ATOMS, CH), F32), ((ATOMS, CH), F32)],
        grads,
        env,
        scale,
        feats,
        mix_in,
        proj_center,
        radial_a,
        radial_b,
        couple,
        by_y=(0,),
    )
    low, core, up = call(
        force_kernel,
        [((128, 48), BF16), ((256, 48), F32), ((128, 48), BF16)],
        [((ATOMS, 72), F32), ((512, 48), F32)],
        owned.reshape(CY, CX, 32, CH),
        base,
        slope,
        normed,
        pull,
        direct,
        feats,
        codes,
        down,
        raw,
        mix_in,
        proj_neigh,
        radial_a,
    )
    to_first = shifted(up, "gx", 1)
    to_last = shifted(low, "gx", -1)
    pulls = core + jnp.concatenate([to_first, to_last], 0).astype(F32)
    pulls = pulls.reshape(CX, CY + 4, 8, 48)
    pulls = folded(folded(pulls, "gy", 1, CY), "gz", 2, CZ)
    forces = pulls.reshape(CX, CY, CZ, 3, PER_CELL)
    return (forces, energy.reshape(CX, CY, CZ, PER_CELL))


def solution(mesh):
    placed = (
        P("gx", "gy", "gz", None, None),
        P("gx", "gy", "gz", None),
        P("gx", "gy", "gz", None, None),
        P("gx", "gy", "gz", None),
    ) + (P(),) * 10
    return jax.shard_map(
        shards,
        mesh=mesh,
        in_specs=placed,
        out_specs=(P("gx", "gy", "gz", None, None), P("gx", "gy", "gz", None)),
        check_vma=False,
    )
```

```python
import math

import jax
import jax.numpy as jnp
from jax import lax
from jax.experimental import pallas as pl
from jax.experimental.pallas import tpu as pltpu
from jax.sharding import PartitionSpec as P

CX = 4
CY = 4
CZ = 2
PER_CELL = 16
SLOTS = 32
CH = 128
NBASIS = 8
SPECIES = 4

CELL_SIDE = 2.0
CUTOFF = 10.5
NORM_EPS = 1e-05

COLS = CX * CY
PAIRS = CZ * PER_CELL * SLOTS
CELL_PAIRS = PER_CELL * SLOTS
ATOMS = COLS * CZ * PER_CELL
RUN = 48
SLAB = 5 * RUN
CELL_ROWS = 40
OWN_RUNS = CY * (CX + 4)
RIM_RUNS = 2 * (CX + 4)
LANES = PAIRS // 128

F32 = jnp.float32
BF16 = jnp.bfloat16
DEGREE = (0, 1, 1, 1, 2, 2, 2, 2, 2)

F_Y = 0
F_W = 9
F_DW = 10
F_B = 11
F_DB = 19
F_INV = 27
F_COUNT = 28

G_B = 0
G_Y = 8
G_E = 17
G_COUNT = 24


def dims(a, b, ca, cb):
    return lax.dot_general(a, b, (((ca,), (cb,)), ((), ())), preferred_element_type=F32)


def halves(value):
    high = value.astype(BF16)
    return high, (value - high.astype(F32)).astype(BF16)


def dims_three(a, b, ca, cb):
    a_high, a_low = halves(a)
    b_high, b_low = halves(b)
    return dims(a_high, b_high, ca, cb) + (
        dims(a_high, b_low, ca, cb) + dims(a_low, b_high, ca, cb)
    )


def iota(shape, dim):
    return lax.broadcasted_iota(jnp.int32, shape, dim)


def one_hot(condition):
    return jnp.where(condition, 1.0, 0.0).astype(BF16)


def hot_rows(count, code):
    rows = iota((count, PAIRS), 0).astype(F32).astype(BF16)
    return jnp.where(
        rows == code.astype(F32).astype(BF16), jnp.ones((), BF16), jnp.zeros((), BF16)
    )


def radial_blocks(radial):
    rows = []
    for m in range(9):
        before = [jnp.zeros((NBASIS, m * CH), F32)] if m else []
        after = [jnp.zeros((NBASIS, (8 - m) * CH), F32)] if m < 8 else []
        rows.append(jnp.concatenate(before + [radial] + after, 1))
    return jnp.concatenate(rows, 0)


def looped(count, body, group):
    def step(j, carry):
        running = [body(j * group + k, k) for k in range(group)]
        while running:
            running = [one for one in running if next(one, True) is None]
        return carry

    lax.fori_loop(0, count // group, step, 0)


def gated(half):
    half = half.astype(BF16)
    t = jnp.tanh(half)
    up = t + 1
    act = half * up
    return act, up + act * (1 - t)


def sigmoid_of(v):
    return 0.5 * jnp.tanh(0.5 * v) + 0.5


def feature_rows(ref, row, count, i):
    blocks = []
    for lane in range(LANES):
        start = (lane * F_COUNT + row) * COLS + i
        blocks.append(ref[pl.ds(start, count, stride=COLS) if count > 1 else pl.ds(start, 1), :])
    return jnp.concatenate(blocks, 1)


def whole_feature(ref, row):
    blocks = []
    for lane in range(LANES):
        start = (lane * F_COUNT + row) * COLS
        blocks.append(ref[start : start + COLS, :])
    return jnp.concatenate(blocks, 1)


def put_feature(ref, row, value):
    for lane in range(LANES):
        start = (lane * F_COUNT + row) * COLS
        ref[start : start + COLS, :] = value[:, lane * 128 : (lane + 1) * 128]


def cell_window(ref, x, y):
    parts = []
    for dx in range(5):
        start = pl.multiple_of(((x + dx) * 8 + y) * 8, 8)
        parts.append(ref[pl.ds(start, CELL_ROWS), :])
    return jnp.concatenate(parts, 0)


def env_kernel(
    nbr_ref,
    ext_ref,
    own_ref,
    count_ref,
    species_ref,
    embed_ref,
    radial_ref,
    mix_ref,
    hidden_ref,
    env_ref,
    scale_ref,
    feat_ref,
    code_ref,
    near_ref,
    moment_ref,
):
    shape = (COLS, PAIRS)
    number = nbr_ref[...]
    slot = number & 15
    cell = number >> 4
    over = (cell * 43691) >> 18
    cell_z = cell - 6 * over
    cell_y = over & 7
    cell_x = over >> 3
    column = iota(shape, 0)
    lane = iota(shape, 1)
    dx = cell_x - (column >> 2)
    dy = cell_y - (column & 3)
    upper = (cell_z >= 3).astype(jnp.int32)
    code_ref[0] = (dy * 5 + dx) * RUN + (cell_z - 3 * upper) * PER_CELL + slot
    code_ref[1] = upper
    code_ref[2] = dx * CELL_ROWS + dy * 8 + cell_z
    code_ref[3] = slot

    row_slots = iota((PER_CELL, PAIRS), 0)

    def fetch(i, k):
        hot = hot_rows(5 * CELL_ROWS, code_ref[2, pl.ds(i, 1), :])
        high, low = halves(cell_window(ext_ref, i // CY, i % CY))
        places = dims(high, hot, 0, 0) + dims(low, hot, 0, 0)
        yield
        mask = row_slots == code_ref[3, pl.ds(i, 1), :]
        for c in range(3):
            part = places[c * PER_CELL : (c + 1) * PER_CELL]
            near_ref[c, pl.ds(i, 1), :] = jnp.sum(jnp.where(mask, part, 0.0), 0, keepdims=True)

    looped(COLS, fetch, 16)

    spread = one_hot(iota((32, PAIRS), 0) == (iota((32, PAIRS), 1) >> 5))
    own_high, own_low = halves(own_ref[...])
    own = dims(own_high, spread, 1, 0) + dims(own_low, spread, 1, 0)
    count = dims(count_ref[...].astype(F32).astype(BF16), spread, 1, 0)
    live = ((lane & 31).astype(F32) < count).astype(F32)
    step_x = (dx - 2).astype(F32) * CELL_SIDE + near_ref[0] - own[0:COLS]
    step_y = (dy - 2).astype(F32) * CELL_SIDE + near_ref[1] - own[COLS : 2 * COLS]
    step_z = (
        (cell_z - 2 - (lane >> 9)).astype(F32) * CELL_SIDE + near_ref[2] - own[2 * COLS : 3 * COLS]
    )
    square = step_x * step_x + step_y * step_y + step_z * step_z
    distance = jnp.sqrt(square)
    inverse = 1.0 / distance
    nx, ny, nz = step_x * inverse, step_y * inverse, step_z * inverse

    def put(row, value):
        put_feature(feat_ref, row, value)

    three, five, fifteen = math.sqrt(3.0), math.sqrt(5.0), math.sqrt(15.0)
    put(F_Y, jnp.ones(shape, F32))
    put(F_Y + 1, three * nx)
    put(F_Y + 2, three * ny)
    put(F_Y + 3, three * nz)
    put(F_Y + 4, fifteen * nx * ny)
    put(F_Y + 5, fifteen * ny * nz)
    put(F_Y + 6, (0.5 * five) * (3.0 * nz * nz - 1.0))
    put(F_Y + 7, fifteen * nx * nz)
    put(F_Y + 8, (0.5 * fifteen) * (nx * nx - ny * ny))
    scaled = distance * (1.0 / CUTOFF)
    inside = 1.0 - scaled * scaled
    put(F_W, live * inside * inside)
    put(F_DW, live * (-4.0 / CUTOFF) * scaled * inside)
    put(F_INV, inverse)
    angle = distance * (math.pi / CUTOFF)
    sine, cosine = jnp.sin(angle), jnp.cos(angle)
    last_s, last_c = jnp.zeros(shape, F32), jnp.ones(shape, F32)
    now_s, now_c = sine, cosine
    for k in range(1, NBASIS + 1):
        basis = CELL_SIDE * now_s * inverse
        put(F_B + k - 1, basis)
        put(F_DB + k - 1, (CELL_SIDE * k * math.pi / CUTOFF * now_c - basis) * inverse)
        last_s, now_s = now_s, 2.0 * cosine * now_s - last_s
        last_c, now_c = now_c, 2.0 * cosine * now_c - last_c

    atoms = one_hot(iota((PER_CELL, CELL_PAIRS), 0) == (iota((PER_CELL, CELL_PAIRS), 1) >> 5))

    def moments(i, k):
        harmonic = feature_rows(feat_ref, F_Y, 9, i)
        weighted = feature_rows(feat_ref, F_B, NBASIS, i) * feature_rows(feat_ref, F_W, 1, i)
        products = jnp.concatenate([harmonic[m : m + 1] * weighted for m in range(9)], 0)
        high, low = halves(products)
        yield
        for z in range(CZ):
            part = slice(z * CELL_PAIRS, (z + 1) * CELL_PAIRS)
            start = pl.multiple_of((i * CZ + z) * PER_CELL, PER_CELL)
            moment_ref[pl.ds(start, PER_CELL), :] = dims(atoms, high[:, part], 1, 1) + dims(
                atoms, low[:, part], 1, 1
            )

    looped(COLS, moments, 16)

    kind = one_hot(iota((SPECIES, ATOMS), 0) == species_ref[...])
    embed_high, embed_low = halves(embed_ref[...] * (1.0 / math.sqrt(SLOTS)))
    scale = dims(kind, embed_high, 0, 0) + dims(kind, embed_low, 0, 0)
    scale_ref[...] = scale
    sums = dims_three(moment_ref[...], radial_blocks(radial_ref[...]), 1, 0)
    invariants = [None] * 3
    for m in range(9):
        value = sums[:, m * CH : (m + 1) * CH] * scale
        env_ref[m] = value
        degree = DEGREE[m]
        squared = value * value
        invariants[degree] = (
            squared if invariants[degree] is None else invariants[degree] + squared
        )
    normed, _ = normalised(invariants)
    mixed = dims(jnp.concatenate(normed, 1).astype(BF16), mix_ref[...], 1, 0)
    hidden = (mixed * sigmoid_of(mixed)).astype(BF16)
    for y in range(CY):
        for x in range(CX):
            hidden_ref[y, x] = hidden[(x * CY + y) * 32 : (x * CY + y + 1) * 32]


def normalised(invariants):
    total = sum(jnp.sum(q * q, 1, keepdims=True) for q in invariants)
    inverse = lax.rsqrt(total * (1.0 / (3 * CH)) + NORM_EPS)
    return [q * inverse for q in invariants], inverse


def spans(z):
    return slice(z * CELL_PAIRS, (z + 1) * CELL_PAIRS)


def rows_of(column, z):
    return pl.ds(pl.multiple_of((column * CZ + z) * PER_CELL, PER_CELL), PER_CELL)


def slab_rows(block, x):
    return pl.ds(pl.multiple_of((block * 8 + x) * RUN, RUN), SLAB)


def fill_table(table_ref, start, around, weights, runs):
    for h in range(2):
        rows = around[:, h].reshape(runs * RUN, CH)
        table_ref[start : start + runs * RUN, h * CH : (h + 1) * CH] = dims(
            rows, weights, 1, 0
        ).astype(BF16) * jnp.asarray(0.5, BF16)


def atom_blocks():
    mask = iota((PER_CELL, CELL_PAIRS), 0) == (iota((PER_CELL, CELL_PAIRS), 1) >> 5)
    return mask, one_hot(mask)


def pair_features(harmonic, part, mask):
    return [jnp.where(mask, harmonic[m : m + 1, part], 0.0).astype(BF16) for m in range(9)]


def scaled_env(env_ref, couple, column, z):
    rows = rows_of(column, z)
    return [
        (env_ref[m, rows, :] * couple[DEGREE[m] : DEGREE[m] + 1]).astype(BF16)
        for m in range(9)
    ]


def early_kernel(
    around_ref,
    hidden_ref,
    env_ref,
    feat_ref,
    code_ref,
    center_ref,
    neigh_ref,
    radial_ref,
    couple_ref,
    early_ref,
    table_ref,
    own_ref,
):
    y = pl.program_id(0)

    @pl.when(y == 0)
    def _():
        fill_table(table_ref, 0, around_ref, neigh_ref[...], OWN_RUNS)
        for yy in range(CY):
            for x in range(CX):
                start = (x * CY + yy) * 32
                own_ref[start : start + 32, :] = dims(
                    hidden_ref[yy, x], center_ref[...], 1, 0
                ) * 0.5

    radial_high, radial_low = halves(radial_ref[...] * 0.5)
    couple = couple_ref[...] * 0.5
    mask, atoms = atom_blocks()

    def column(x, place, first, count, block):
        i = x * CY + y
        harmonic = feature_rows(feat_ref, F_Y, 9, i)
        basis_high, basis_low = halves(feature_rows(feat_ref, F_B, NBASIS, i))
        code = code_ref[0, pl.ds(i, 1), :]
        upper = code_ref[1, pl.ds(i, 1), :] > 0
        parts = []
        for z in range(CZ):
            part = spans(z)
            feature = jnp.concatenate(
                pair_features(harmonic, part, mask)
                + [
                    atoms,
                    atoms,
                    basis_high[:, part],
                    basis_low[:, part],
                    basis_high[:, part],
                    jnp.zeros((8, CELL_PAIRS), BF16),
                ],
                0,
            )
            own_high, own_low = halves(own_ref[rows_of(i, z), :])
            table = jnp.concatenate(
                scaled_env(env_ref, couple, i, z)
                + [
                    own_high,
                    own_low,
                    radial_high,
                    radial_high,
                    radial_low,
                    jnp.zeros((8, CH), BF16),
                ],
                0,
            )
            parts.append(dims(table, feature, 0, 0))
        yield
        fetched = None
        for k in range(count):
            hot = hot_rows(SLAB, code - (first + k) * SLAB)
            found = dims(table_ref[slab_rows(block + k, x), :], hot, 0, 0)
            fetched = found if fetched is None else fetched + found
        yield
        early_ref[x] = jnp.concatenate(parts, 1) + jnp.where(upper, fetched[CH:], fetched[:CH])

    @pl.when((y == 0) | (y == 3))
    def _():
        far = (y == 3).astype(jnp.int32)
        looped(CX, lambda x, k: column(x, k, 2 - 2 * far, 3, far), 4)

    @pl.when((y == 1) | (y == 2))
    def _():
        looped(CX, lambda x, k: column(x, k, 2 - y, 4, 0), 4)


def pair_kernel(
    early_ref,
    low_ref,
    up_ref,
    feat_ref,
    code_ref,
    neigh_ref,
    two_ref,
    three_ref,
    readout_ref,
    energy_ref,
    low_out_ref,
    up_out_ref,
    grad_ref,
    raw_ref,
    table_ref,
    total_ref,
    hot_ref,
):
    y = pl.program_id(0)

    @pl.when(y == 0)
    def _():
        fill_table(table_ref, 0, low_ref, neigh_ref[...], RIM_RUNS)
        fill_table(table_ref, RIM_RUNS * RUN, up_ref, neigh_ref[...], RIM_RUNS)
        total_ref[...] = jnp.zeros_like(total_ref)

    readout = jnp.transpose(jnp.broadcast_to(0.5 * readout_ref[...], (CH, CH)))
    readout = jnp.concatenate([readout] * LANES, 1)
    two_half = two_ref[...] * jnp.asarray(0.5, BF16)
    three_half = three_ref[...] * jnp.asarray(0.5, BF16)

    def column(x, place, first, count, block):
        i = x * CY + y
        weight = feature_rows(feat_ref, F_W, 1, i)
        code = code_ref[0, pl.ds(i, 1), :]
        upper = code_ref[1, pl.ds(i, 1), :] > 0
        fetched = None
        for k in range(count):
            hot = hot_rows(SLAB, code - (first + k) * SLAB)
            hot_ref[place, k * SLAB : (k + 1) * SLAB, :] = hot
            found = dims(table_ref[slab_rows(block + k, x), :], hot, 0, 0)
            fetched = found if fetched is None else fetched + found
        yield
        value = early_ref[x] + jnp.where(upper, fetched[CH:], fetched[:CH])
        one, slope_one = gated(value)
        value = dims(two_half, one, 0, 0)
        yield
        two, slope_two = gated(value)
        value = dims(three_half, two, 0, 0)
        yield
        top, slope_top = gated(value)
        raw_ref[pl.ds(i, 1), :] = 2.0 * jnp.sum(top.astype(F32) * readout, 0, keepdims=True)
        grad = slope_top * (readout * weight).astype(BF16)
        grad = dims(three_half, grad, 1, 0)
        yield
        grad = dims(two_half, grad.astype(BF16) * slope_two, 1, 0)
        yield
        grad = grad.astype(BF16) * slope_one
        high = grad * jnp.where(upper, 1.0, 0.0).astype(BF16)
        spread = jnp.concatenate([grad - high, high], 0)
        grad_ref[x] = grad
        found = dims(hot_ref[place, : count * SLAB, :], spread, 1, 1)
        yield
        for k in range(count):
            total_ref[slab_rows(block + k, x), :] += found[k * SLAB : (k + 1) * SLAB]

    @pl.when((y == 0) | (y == 3))
    def _():
        far = (y == 3).astype(jnp.int32)
        looped(CX, lambda x, k: column(x, k, 3 * far, 2, 2 * far), 4)

    @pl.when((y == 1) | (y == 2))
    def _():
        looped(CX, lambda x, k: column(x, k, 4 * (y - 1), 1, y), 4)

    @pl.when(y == CY - 1)
    def _():
        for h in range(2):
            rim = total_ref[:, h * CH : (h + 1) * CH].astype(BF16).reshape(2 * RIM_RUNS, RUN, CH)
            low_out_ref[:, h] = rim[:RIM_RUNS]
            up_out_ref[:, h] = rim[RIM_RUNS:]
        gather = one_hot(iota((32, PAIRS), 0) == (iota((32, PAIRS), 1) >> 5))
        high, low = halves(raw_ref[...] * whole_feature(feat_ref, F_W))
        energy_ref[...] = dims(high, gather, 1, 1) + dims(low, gather, 1, 1)


def spread_kernel(grad_ref, code_ref, ghost_ref, total_ref, hot_ref):
    y = pl.program_id(0)

    @pl.when(y == 0)
    def _():
        total_ref[...] = jnp.zeros_like(total_ref)


    def column(x, place, first, count, block):
        i = x * CY + y
        code = code_ref[0, pl.ds(i, 1), :]
        upper = jnp.where(code_ref[1, pl.ds(i, 1), :] > 0, 1.0, 0.0).astype(BF16)
        for k in range(count):
            hot_ref[place, k * SLAB : (k + 1) * SLAB, :] = hot_rows(
                SLAB, code - (first + k) * SLAB
            )
        grad = grad_ref[x]
        high = grad * upper
        spread = jnp.concatenate([grad - high, high], 0)
        found = dims(hot_ref[place, : count * SLAB, :], spread, 1, 1)
        for k in range(count):
            total_ref[slab_rows(block + k, x), :] += found[k * SLAB : (k + 1) * SLAB]
        yield

    @pl.when((y == 0) | (y == 3))
    def _():
        far = (y == 3).astype(jnp.int32)
        looped(CX, lambda x, k: column(x, k, 2 - 2 * far, 3, far), 4)

    @pl.when((y == 1) | (y == 2))
    def _():
        looped(CX, lambda x, k: column(x, k, 2 - y, 4, 0), 4)

    @pl.when(y == CY - 1)
    def _():
        for h in range(2):
            ghost_ref[:, h] = (
                total_ref[:, h * CH : (h + 1) * CH].astype(BF16).reshape(OWN_RUNS, RUN, CH)
            )


def back_kernel(
    grad_ref,
    env_ref,
    scale_ref,
    feat_ref,
    mix_ref,
    center_ref,
    radial_a_ref,
    radial_ref,
    couple_ref,
    down_ref,
    base_ref,
    slope_ref,
    normed_ref,
    pull_ref,
    direct_ref,
    grad_env_ref,
    grad_center_ref,
):
    y = pl.program_id(0)
    mask, atoms = atom_blocks()
    radial = radial_ref[...].astype(BF16)

    def column(x, k):
        i = x * CY + y
        harmonic = feature_rows(feat_ref, F_Y, 9, i)
        found = []
        for z in range(CZ):
            part = spans(z)
            grad = grad_ref[x, :, part]
            feature = jnp.concatenate(pair_features(harmonic, part, mask) + [atoms], 0)
            back = dims(feature, grad, 1, 1)
            table = jnp.concatenate(
                scaled_env(env_ref, couple_ref, i, z) + [radial, jnp.zeros((8, CH), BF16)], 0
            )
            found.append((back, dims(table, grad, 1, 0)))
        yield
        for z in range(CZ):
            part = spans(z)
            back, down = found[z]
            for m in range(9):
                grad_env_ref[m, rows_of(i, z), :] = back[m * PER_CELL : (m + 1) * PER_CELL]
            grad_center_ref[rows_of(i, z), :] = back[9 * PER_CELL :]
            rows = [down[9 * PER_CELL : 9 * PER_CELL + NBASIS]]
            for m in range(9):
                kept = jnp.where(mask, down[m * PER_CELL : (m + 1) * PER_CELL], 0.0)
                rows.append(jnp.sum(kept, 0, keepdims=True))
            down_ref[i, 0 : NBASIS + 9, part] = jnp.concatenate(rows, 0)

    looped(CX, column, 4)

    @pl.when(y == CY - 1)
    def _():
        invariants = [None] * 3
        for m in range(9):
            value = env_ref[m]
            squared = value * value
            degree = DEGREE[m]
            invariants[degree] = (
                squared if invariants[degree] is None else invariants[degree] + squared
            )
        normed, inverse = normalised(invariants)
        mixed = dims(jnp.concatenate(normed, 1).astype(BF16), mix_ref[...], 1, 0)
        gate = sigmoid_of(mixed)
        act = mixed * gate
        slope_ref[...] = gate + act - act * gate
        for d in range(3):
            normed_ref[d] = normed[d]
        high, low = halves(grad_center_ref[...])
        base_ref[...] = dims(high, center_ref[...], 1, 1) + dims(low, center_ref[...], 1, 1)
        scale = scale_ref[...]
        for m in range(9):
            pull_ref[m] = 2.0 * env_ref[m] * scale * inverse
        pulled = [
            grad_env_ref[m] * couple_ref[DEGREE[m] : DEGREE[m] + 1] * scale for m in range(9)
        ]
        direct_ref[...] = dims(
            jnp.concatenate(pulled, 1).astype(BF16),
            radial_blocks(radial_a_ref[...]).astype(BF16),
            1,
            1,
        )


def force_kernel(
    neigh_ref,
    base_ref,
    slope_ref,
    normed_ref,
    pull_env_ref,
    direct_ref,
    feat_ref,
    code_ref,
    down_ref,
    raw_ref,
    mix_ref,
    proj_ref,
    radial_ref,
    low_out_ref,
    core_ref,
    up_out_ref,
    moment_ref,
    ghost_ref,
):
    neigh = jnp.concatenate([neigh_ref[y, x] for x in range(CX) for y in range(CY)], 0)
    grad = base_ref[...] + dims(neigh.astype(BF16), proj_ref[...], 1, 1)
    grad = grad * slope_ref[...]
    grad = dims(grad.astype(BF16), mix_ref[...], 1, 1)
    grads = [grad[:, d * CH : (d + 1) * CH] for d in range(3)]
    normed = [normed_ref[d] for d in range(3)]
    mean = sum(jnp.sum(g * q, 1, keepdims=True) for g, q in zip(grads, normed)) * (1.0 / (3 * CH))
    grads = [g - q * mean for g, q in zip(grads, normed)]
    pulled = [pull_env_ref[m] * grads[DEGREE[m]] for m in range(9)]
    moment_ref[...] = direct_ref[...] + dims(
        jnp.concatenate(pulled, 1).astype(BF16),
        radial_blocks(radial_ref[...]).astype(BF16),
        1,
        1,
    )

    _, atoms = atom_blocks()
    row_slots = iota((PER_CELL, PAIRS), 0)
    own_slots = row_slots == ((iota((PER_CELL, PAIRS), 1) & (CELL_PAIRS - 1)) >> 5)
    own_cells = one_hot(iota((8, PAIRS), 0) == 2 + (iota((8, PAIRS), 1) >> 9))
    ghost_ref[...] = jnp.zeros_like(ghost_ref)
    three, five, fifteen = math.sqrt(3.0), math.sqrt(5.0), math.sqrt(15.0)

    def column(i, k):
        harmonic = feature_rows(feat_ref, F_Y, 9, i)
        basis = feature_rows(feat_ref, F_B, NBASIS, i)
        slope = feature_rows(feat_ref, F_DB, NBASIS, i)
        weight = feature_rows(feat_ref, F_W, 1, i)
        weight_slope = feature_rows(feat_ref, F_DW, 1, i)
        inverse = feature_rows(feat_ref, F_INV, 1, i)
        parts = []
        for z in range(CZ):
            parts.append(dims(moment_ref[rows_of(i, z), :].astype(BF16), atoms, 0, 0))
        back = jnp.concatenate(parts, 1)
        yield
        weighted = basis * weight
        grad_weighted = jnp.zeros((NBASIS, PAIRS), F32)
        chain = []
        for m in range(9):
            block = back[m * NBASIS : (m + 1) * NBASIS]
            grad_weighted += block * harmonic[m : m + 1]
            if m:
                chain.append(
                    down_ref[i, NBASIS + m : NBASIS + m + 1, :]
                    + jnp.sum(block * weighted, 0, keepdims=True)
                )
        y1, y2, y3, y4, y5, y6, y7, y8 = chain
        grad_basis = down_ref[i, 0:NBASIS, :] + grad_weighted * weight
        grad_weight = raw_ref[pl.ds(i, 1), :] + jnp.sum(grad_weighted * basis, 0, keepdims=True)
        radial = jnp.sum(grad_basis * slope, 0, keepdims=True) + grad_weight * weight_slope
        nx, ny, nz = (harmonic[c : c + 1] * (1.0 / three) for c in range(1, 4))
        grad_x = three * y1 + fifteen * (ny * y4 + nz * y7 + nx * y8)
        grad_y = three * y2 + fifteen * (nx * y4 + nz * y5 - ny * y8)
        grad_z = three * y3 + fifteen * (ny * y5 + nx * y7) + (3.0 * five) * nz * y6
        along = radial - inverse * (nx * grad_x + ny * grad_y + nz * grad_z)
        pulls = (
            grad_x * inverse + nx * along,
            grad_y * inverse + ny * along,
            grad_z * inverse + nz * along,
        )
        yield
        x, y = i // CY, i % CY
        hot = hot_rows(5 * CELL_ROWS, code_ref[2, pl.ds(i, 1), :])
        mask = row_slots == code_ref[3, pl.ds(i, 1), :]
        owned = jnp.concatenate([jnp.where(own_slots, pull, 0.0) for pull in pulls], 0)
        own_found = dims(own_cells, owned.astype(BF16), 1, 1)
        kept = jnp.concatenate([jnp.where(mask, pull, 0.0) for pull in pulls], 0)
        found = dims(hot, kept.astype(BF16), 1, 1)
        yield
        for dx in range(5):
            start = pl.multiple_of(((x + dx) * 8 + y) * 8, 8)
            ghost_ref[pl.ds(start, CELL_ROWS), :] -= found[dx * CELL_ROWS : (dx + 1) * CELL_ROWS]
        start = pl.multiple_of(((x + 2) * 8 + y + 2) * 8, 8)
        ghost_ref[pl.ds(start, 8), :] += own_found

    looped(COLS, column, 8)

    low_out_ref[...] = ghost_ref[:128].astype(BF16)
    core_ref[...] = ghost_ref[128:384]
    up_out_ref[...] = ghost_ref[384:].astype(BF16)


def call(kernel, outs, scratch, *args, by_y=(), by_y_out=(), micros=20):
    def spec(shape, moving):
        zeros = (0,) * len(shape)
        if not moving:
            return pl.BlockSpec(shape, lambda y: zeros)
        return pl.BlockSpec((shape[0] // CY,) + shape[1:], lambda y: (y,) + zeros[1:])

    grid = {}
    if by_y or by_y_out:
        grid = dict(
            grid=(CY,),
            in_specs=[spec(a.shape, k in by_y) for k, a in enumerate(args)],
            out_specs=[spec(shape, k in by_y_out) for k, (shape, _) in enumerate(outs)],
        )
    return pl.pallas_call(
        kernel,
        out_shape=[jax.ShapeDtypeStruct(shape, dtype) for shape, dtype in outs],
        scratch_shapes=[pltpu.VMEM(shape, dtype) for shape, dtype in scratch],
        compiler_params=pltpu.CompilerParams(vmem_limit_bytes=32 * 2**20),
        cost_estimate=pl.CostEstimate(
            flops=micros * 10**9, bytes_accessed=micros * 3 * 10**6, transcendentals=0
        ),
        **grid,
    )(*args)


def shifted(block, axis, distance):
    size = lax.axis_size(axis)
    return lax.ppermute(block, axis, [(i, (i + distance) % size) for i in range(size)])


def rims(array, axis, dim):
    length = array.shape[dim]
    before = shifted(lax.slice_in_dim(array, length - 2, length, axis=dim), axis, 1)
    after = shifted(lax.slice_in_dim(array, 0, 2, axis=dim), axis, -1)
    return before, after


def padded(array, axis, dim, tail=0, beside=None):
    before, after = rims(array, axis, dim)
    if beside is not None:
        before, beside = lax.optimization_barrier((before, beside))
    parts = [before, array, after]
    if tail:
        parts.append(jnp.zeros(after.shape[:dim] + (tail,) + after.shape[dim + 1 :], array.dtype))
    whole = jnp.concatenate(parts, axis=dim)
    return whole if beside is None else (whole, beside)


def folded(array, axis, dim, length):
    lower = lax.slice_in_dim(array, 0, 2, axis=dim).astype(BF16)
    upper = lax.slice_in_dim(array, length + 2, length + 4, axis=dim).astype(BF16)
    core = lax.slice_in_dim(array, 2, length + 2, axis=dim).astype(F32)
    to_first = shifted(upper, axis, 1).astype(F32)
    to_last = shifted(lower, axis, -1).astype(F32)
    if length == 2:
        return core + to_first + to_last
    return core + jnp.concatenate([to_first, to_last], axis=dim)


def shards(
    offsets,
    species,
    neighbours,
    counts,
    embed,
    radial_a,
    mix_in,
    proj_center,
    proj_neigh,
    radial_b,
    couple,
    latent_two,
    latent_three,
    readout,
):
    numbers = neighbours.reshape(COLS, PAIRS)
    around, numbers = padded(offsets, "gx", 0, beside=numbers)
    around = around.reshape(CX + 4, CY, CZ, 48)
    rows = (counts.reshape(COLS, 32), species.reshape(1, ATOMS))
    around, rows = padded(around, "gy", 1, beside=rows)
    own = offsets.reshape(COLS, CZ, 3, PER_CELL).transpose(2, 0, 1, 3).reshape(3 * COLS, 32)
    around = padded(around, "gz", 2, tail=2)
    hidden, env, scale, feats, codes = call(
        env_kernel,
        [
            ((CY, CX, 32, CH), BF16),
            ((9, ATOMS, CH), F32),
            ((ATOMS, CH), F32),
            ((LANES * F_COUNT * COLS, 128), F32),
            ((4, COLS, PAIRS), jnp.int32),
        ],
        [((3, COLS, PAIRS), F32), ((ATOMS, 72), F32)],
        numbers,
        around.reshape(512, 48),
        own,
        *rows,
        embed,
        radial_a,
        mix_in,
    )
    grid = hidden.reshape(CY, CX, CZ, PER_CELL, CH)
    wide = padded(padded(grid, "gz", 2), "gx", 1)
    low, up = rims(wide, "gy", 0)
    (early,) = call(
        early_kernel,
        [((COLS, CH, PAIRS), F32)],
        [((OWN_RUNS * RUN, 2 * CH), BF16), ((ATOMS, CH), F32)],
        wide.reshape(OWN_RUNS, 2, RUN, CH),
        hidden,
        env,
        feats,
        codes,
        proj_center,
        proj_neigh,
        radial_b,
        couple,
        by_y_out=(0,),
    )
    energy, low_back, up_back, grads, raw = call(
        pair_kernel,
        [
            ((COLS, 32), F32),
            ((RIM_RUNS, 2, RUN, CH), BF16),
            ((RIM_RUNS, 2, RUN, CH), BF16),
            ((COLS, CH, PAIRS), BF16),
            ((COLS, PAIRS), F32),
        ],
        [
            ((2 * RIM_RUNS * RUN, 2 * CH), BF16),
            ((2 * RIM_RUNS * RUN, 2 * CH), F32),
            ((CX, 2 * SLAB, PAIRS), BF16),
        ],
        early,
        low.reshape(RIM_RUNS, 2, RUN, CH),
        up.reshape(RIM_RUNS, 2, RUN, CH),
        feats,
        codes,
        proj_neigh,
        latent_two,
        latent_three,
        readout.reshape(1, CH),
        by_y=(0,),
        by_y_out=(3,),
    )
    to_first = shifted(up_back, "gy", 1)
    to_last = shifted(low_back, "gy", -1)
    (ghost,) = call(
        spread_kernel,
        [((OWN_RUNS, 2, RUN, CH), BF16)],
        [((OWN_RUNS * RUN, 2 * CH), F32), ((CX, 4 * SLAB, PAIRS), BF16)],
        grads,
        codes,
        by_y=(0,),
    )
    arrived = jnp.concatenate([to_first, to_last], 0)
    ghost = (ghost.astype(F32) + arrived.astype(F32)).astype(BF16)
    ghost = ghost.reshape(CY, CX + 4, CZ + 4, PER_CELL, CH)
    owned = folded(folded(ghost, "gx", 1, CX), "gz", 2, CZ)
    down, base, slope, normed, pull, direct = call(
        back_kernel,
        [
            ((COLS, 24, PAIRS), F32),
            ((ATOMS, CH), F32),
            ((ATOMS, CH), F32),
            ((3, ATOMS, CH), F32),
            ((9, ATOMS, CH), F32),
            ((ATOMS, 72), F32),
        ],
        [((9, ATOMS, CH), F32), ((ATOMS, CH), F32)],
        grads,
        env,
        scale,
        feats,
        mix_in,
        proj_center,
        radial_a,
        radial_b,
        couple,
        by_y=(0,),
    )
    low, core, up = call(
        force_kernel,
        [((128, 48), BF16), ((256, 48), F32), ((128, 48), BF16)],
        [((ATOMS, 72), F32), ((512, 48), F32)],
        owned.reshape(CY, CX, 32, CH),
        base,
        slope,
        normed,
        pull,
        direct,
        feats,
        codes,
        down,
        raw,
        mix_in,
        proj_neigh,
        radial_a,
    )
    to_first = shifted(up, "gx", 1)
    to_last = shifted(low, "gx", -1)
    pulls = core + jnp.concatenate([to_first, to_last], 0).astype(F32)
    pulls = pulls.reshape(CX, CY + 4, 8, 48)
    pulls = folded(folded(pulls, "gy", 1, CY), "gz", 2, CZ)
    forces = pulls.reshape(CX, CY, CZ, 3, PER_CELL)
    return (forces, energy.reshape(CX, CY, CZ, PER_CELL))


def solution(mesh):
    placed = (
        P("gx", "gy", "gz", None, None),
        P("gx", "gy", "gz", None),
        P("gx", "gy", "gz", None, None),
        P("gx", "gy", "gz", None),
    ) + (P(),) * 10
    return jax.shard_map(
        shards,
        mesh=mesh,
        in_specs=placed,
        out_specs=(P("gx", "gy", "gz", None, None), P("gx", "gy", "gz", None)),
        check_vma=False,
    )
```
